32 devices in a mesh: dp: 8 (over z, y), stream: 4 (over x, core).
Axes of the slice: x: 2, y: 2, z: 4, core: 2. Of those that a mesh axis runs over, the one named last changes fastest.
Arguments:
- patches: bfloat16 [16384, 768], P(('dp', 'stream')), may hold values from -6 to 6
- src_kind: int32 [32768], P(('dp', 'stream')), may hold values from 0 to 1, as said below
- src_index: int32 [32768], P(('dp', 'stream')), may hold values from 0 to 4015, as said below
- layout_coords: int32 [4, 32768], P(None, ('dp', 'stream')), may hold values from 0 to 1023
- placing: int32 [32768], P(('dp', 'stream')), may hold values from 0 to 8191, as said below
- segments: int32 [32, 1024], P(('dp', 'stream')), may hold values from 0 to 7, never falling along the last dimension, each value on 1 to 512 neighbouring positions
- text_table: bfloat16 [32128, 768], P('dp'), may hold values from -6 to 6
- layout_tables: bfloat16 [4, 1024, 768], P(None, 'dp'), may hold values from -3 to 3
- patch_proj: bfloat16 [768, 768], P('dp'), may hold values from -0.21875 to 0.21875
- rel_table: float32 [32, 12], replicated, may hold values from -4 to 4
- norm_gains: bfloat16 [2, 768], P(None, 'dp'), may hold values from 0.5 to 1.5
- w_qkv: bfloat16 [3, 768, 768], P(None, 'dp'), may hold values from -0.21875 to 0.21875
- w_attn_out: bfloat16 [768, 768], P('dp'), may hold values from -1.25 to 1.25
- w_ff_in: bfloat16 [768, 3072], P('dp'), may hold values from -0.21875 to 0.21875
- w_ff_out: bfloat16 [3072, 768], P('dp'), may hold values from -0.109375 to 0.109375
- out_grad: bfloat16 [32768, 768], P(('dp', 'stream')), may hold values from -6 to 6
Outputs:
- out_rows: bfloat16 [32768, 768], P(('dp', 'stream'))
- grad_patches: float32 [16384, 768], P(('dp', 'stream'))
- grad_text: float32 [32128, 768], P('dp')
- grad_layout: float32 [4, 1024, 768], P(None, 'dp')
- grad_patch_proj: float32 [768, 768], P('dp')
- grad_rel: float32 [32, 12], replicated
- grad_gains: float32 [2, 768], P(None, 'dp')
- grad_qkv: float32 [3, 768, 768], P(None, 'dp')
- grad_attn_out: float32 [768, 768], P('dp')
- grad_ff_in: float32 [768, 3072], P('dp')
- grad_ff_out: float32 [3072, 768], P('dp')
The draws below stay inside these ranges and needn't reach their ends.
Inputs may be any that keep to these rules, and one draw needn't show every extreme that they name: `src_kind`: each device holds exactly 512 visual tokens (0); the rest of its 1024 source tokens are text tokens (1). `src_index`: A visual token names a patch of its own device, each of the device's 512 patches named by exactly one token. A text token names one of the 4016 text table rows of its data index. For each stream index, placing over the source tokens of that stream index is a permutation of the 8192 packed places; value // 1024 is the owner's data index and value % 1024 the place in the owner's rows. One device sends at most 256 tokens to one owner, and exactly 256 to some owners. `segments`: within each packed row the segment numbers never fall.
All inputs are finite; a program needn't handle non-finite values.
Results may differ from the reference program's by a relative error of at most 0.015.
Values may be sent and summed in bfloat16 or wider, within the bound.
No kernel may reach another device: no remote copies, remote signals or barrier semaphores. Data moves between devices by JAX's collectives and lax.ppermute only.
A program may use at most 256 MiB of HBM per device.

```python
import math
import jax
import jax.numpy as jnp
import numpy as np
from jax import lax

D = 768
H = 12
FF = 3072
VOCAB = 32128
BUCKETS = 32
LAYOUT = 1024
PATCH_DIM = 768
SEQ = 1024
ROW_TOK = 1024
PATCH_DEV = 512
VOCAB_DEV = 4016
ALL_ROWS = 32
SOURCES = 32768
PATCHES = 16384
N_DP = 8
N_STREAM = 4


def source_order(key):
    keys = jax.random.split(key, N_DP * N_STREAM)
    return jax.vmap(lambda single: jax.random.permutation(single, ROW_TOK))(keys)


def draw_src_kind(key, part):
    shuffled = source_order(key)
    return (shuffled >= PATCH_DEV).astype(jnp.int32).reshape(-1)


def draw_src_index(key, part):
    shuffled = source_order(key)
    key = jax.random.fold_in(key, 12)
    text_rows = jax.random.randint(key, shuffled.shape, 0, VOCAB_DEV)
    text_rows = jnp.where(shuffled == PATCH_DEV, VOCAB_DEV - 1, text_rows)
    return jnp.where(shuffled < PATCH_DEV, shuffled, text_rows).astype(jnp.int32).reshape(-1)


def column_places(key):
    count = N_DP
    tokens = ROW_TOK
    capacity = 2 * ROW_TOK // N_DP
    quarter = N_DP // 4
    shift_key, split_key, send_key, owner_key = jax.random.split(key, 4)
    order = jax.random.permutation(shift_key, count)
    splits = jax.random.randint(split_key, (quarter,), 1, capacity)
    weights = jnp.concatenate([jnp.full((quarter,), capacity, jnp.int32), splits, capacity - splits]).astype(jnp.int32)
    shift_weight = jnp.zeros((count,), jnp.int32).at[order[:3 * quarter]].set(weights)
    sources = jnp.arange(count, dtype=jnp.int32)
    counts = shift_weight[(sources[None, :] - sources[:, None]) % count]

    def source_targets(row_counts):
        targets = jnp.repeat(sources, row_counts, total_repeat_length=tokens)
        starts = jnp.cumsum(row_counts) - row_counts
        return (targets, jnp.arange(tokens, dtype=jnp.int32) - starts[targets])
    targets, within = jax.vmap(source_targets)(counts)
    before = jnp.cumsum(counts, axis=0) - counts
    slots = before[sources[:, None], targets] + within
    owner_order = jax.vmap(lambda single: jax.random.permutation(single, tokens))(jax.random.split(owner_key, count))
    placed = targets * tokens + owner_order[targets, slots]
    token_order = jax.vmap(lambda single: jax.random.permutation(single, tokens))(jax.random.split(send_key, count))
    return jnp.take_along_axis(placed, token_order, axis=1)


def draw_placing(key, part):
    key = jax.random.fold_in(key, 13)
    columns = jax.vmap(column_places)(jax.random.split(key, N_STREAM))
    return columns.transpose(1, 0, 2).reshape(-1).astype(jnp.int32)


def touch_ends(array, own_key, smallest, high):
    longest = array.shape.index(max(array.shape))
    spots = []
    for shift in (0, 1):
        where = [jax.random.randint(jax.random.fold_in(own_key, axis), (), 0, length) for axis, length in enumerate(array.shape)]
        where[longest] = (where[longest] + shift) % array.shape[longest]
        spots.append(tuple(where))
    return array.at[spots[0]].set(smallest).at[spots[1]].set(high)


def block_levels(own_key, dims, pieces, least, largest):
    def one(dim, parts):
        draws = jax.random.uniform(jax.random.fold_in(jax.random.fold_in(own_key, 6), dim), (parts,), jnp.float32, least / len(pieces), largest / len(pieces))
        return jnp.repeat(jnp.exp(draws), dims[dim] // parts).reshape((-1,) + (1,) * (len(dims) - dim - 1))

    loudness = one(*pieces[0])
    for cut in pieces[1:]:
        loudness = loudness * one(*cut)
    return loudness


def profile(amount, total, limit, lean):
    loads = [(1 << 20) // math.isqrt(standing ** lean) + 1 for standing in range(2, amount + 1)]
    rest, given = total - limit - (amount - 1), [1] * (amount - 1)
    while rest > 0:
        movable = [i for i in range(amount - 1) if given[i] < limit]
        mass, budget = sum([loads[i] for i in movable]), rest
        for i in movable:
            more = min(limit - given[i], max(1, budget * loads[i] // mass), rest)
            given[i] = given[i] + more
            rest = rest - more
    return np.array([limit] + given)


def ragged_sizes(own_key, amount, total, limit, lean):
    if amount == 2:
        one = jax.random.randint(own_key, (), max(1, total - limit), min(limit, total - 1) + 1)
        return jnp.stack([one, total - one])
    lengths = jnp.asarray(profile(amount, total, limit, lean), jnp.int32)
    couples = (amount - 1) // 2
    giver, taker = lengths[1:1 + 2 * couples:2], lengths[2:2 + 2 * couples:2]
    margin = jnp.minimum(giver - 1, limit - taker)
    moved = jax.random.randint(jax.random.fold_in(own_key, 1), (couples,), 0, 1 << 20) % (margin + 1)
    lengths = lengths.at[1:1 + 2 * couples:2].set(giver - moved).at[2:2 + 2 * couples:2].set(taker + moved)
    return lengths[jax.random.permutation(jax.random.fold_in(own_key, 2), amount)]


def centred(stream_key, shape, spread, bound, cuts=(), kind=jnp.bfloat16):
    drawn = jax.random.normal(stream_key, shape, jnp.float32) * spread
    if len(cuts) > 0:
        drawn = block_levels(stream_key, shape, cuts, -0.22, 0.18) * drawn
    return jnp.clip(drawn, min=-bound, max=bound).astype(kind)


def setup_inputs(seed: int = 0) -> dict:
    streams_of = jax.random.split(jax.random.key(seed), 17)
    patches = centred(streams_of[0], (PATCHES, PATCH_DIM), 1.0, 6.0, ((0, 32),))
    src_kind = draw_src_kind(jax.random.fold_in(streams_of[16], 71), 0)
    src_index = draw_src_index(jax.random.fold_in(streams_of[16], 71), 0)
    layout_coords = touch_ends(jax.random.randint(streams_of[3], (4, SOURCES), 0, LAYOUT), jax.random.fold_in(streams_of[3], 1), 0, LAYOUT - 1).astype(jnp.int32)
    placing = draw_placing(jax.random.fold_in(streams_of[16], 71), 0)
    segments = jax.vmap(lambda own: jnp.searchsorted(jnp.cumsum(ragged_sizes(own, 8, SEQ, SEQ // 2, 2)), jnp.arange(SEQ), side="right"))(jax.random.split(streams_of[5], ALL_ROWS)).reshape((ALL_ROWS, SEQ)).astype(jnp.int32)
    text_table = centred(streams_of[6], (VOCAB, D), 1.0, 6.0, ((0, 8),))
    layout_tables = centred(streams_of[7], (4, LAYOUT, D), 0.5, 3.0, ((1, 8),))
    patch_proj = centred(streams_of[8], (PATCH_DIM, D), PATCH_DIM ** -0.5, 0.21875, ((0, 8),))
    rel_table = centred(streams_of[9], (BUCKETS, H), 1.0, 4.0, (), jnp.float32)
    norm_gains = jnp.clip(1.0 + 0.1 * jax.random.normal(streams_of[10], (2, D), jnp.float32), 0.5, 1.5).astype(jnp.bfloat16)
    w_qkv = centred(streams_of[11], (3, D, D), D ** -0.5, 0.21875, ((1, 8),))
    w_attn_out = centred(streams_of[12], (D, D), (D // 32) ** -0.5, 1.25, ((0, 8),))
    w_ff_in = centred(streams_of[13], (D, FF), D ** -0.5, 0.21875, ((0, 8),))
    w_ff_out = centred(streams_of[14], (FF, D), FF ** -0.5, 0.109375, ((0, 8),))
    out_grad = centred(streams_of[15], (SOURCES, D), 1.0, 6.0, ((0, 32),))
    return {"patches": patches, "src_kind": src_kind, "src_index": src_index, "layout_coords": layout_coords, "placing": placing, "segments": segments, "text_table": text_table, "layout_tables": layout_tables, "patch_proj": patch_proj, "rel_table": rel_table, "norm_gains": norm_gains, "w_qkv": w_qkv, "w_attn_out": w_attn_out, "w_ff_in": w_ff_in, "w_ff_out": w_ff_out, "out_grad": out_grad}


@jax.custom_vjp
def low(v):
    return lax.optimization_barrier(v.astype(jnp.bfloat16)).astype(jnp.float32)

@jax.custom_vjp
def low_back(v):
    return v

def low_keep(v):
    return (low(v), None)

def low_pass(kept, grad):
    return (grad,)

def back_keep(v):
    return (v, None)

def back_low(kept, grad):
    return (low(grad),)
low.defvjp(low_keep, low_pass)
low_back.defvjp(back_keep, back_low)
EPSILON = 1e-06
THRESHOLDS = (12, 16, 23, 32, 46, 64, 91)
HIGHEST = lax.Precision.HIGHEST

def bucket_of(relative):
    magnitude = jnp.abs(relative)
    beyond = 8 + sum(((magnitude >= threshold).astype(jnp.int32) for threshold in THRESHOLDS))
    return jnp.where(relative > 0, 16, 0).astype(jnp.int32) + jnp.where(magnitude < 8, magnitude, beyond).astype(jnp.int32)

def rms_norm(values, gain):
    return values * lax.rsqrt(lax.optimization_barrier(jnp.mean(values * values, axis=-1, keepdims=True)) + EPSILON) * gain

def reference(patches, src_kind, src_index, layout_coords, placing, segments, text_table, layout_tables, patch_proj, rel_table, norm_gains, w_qkv, w_attn_out, w_ff_in, w_ff_out, out_grad):
    token_ids = jnp.arange(SOURCES, dtype=jnp.int32)
    device_of = token_ids // ROW_TOK
    data_of = device_of // N_STREAM
    stream_of = device_of % N_STREAM
    is_text = src_kind == 1
    text_pick = (data_of * VOCAB_DEV + jnp.where(is_text, src_index, 0)).astype(jnp.int32)
    patch_pick = (device_of * PATCH_DEV + jnp.where(is_text, 0, src_index)).astype(jnp.int32)
    target = ((placing // ROW_TOK * N_STREAM + stream_of) * ROW_TOK + placing % ROW_TOK).astype(jnp.int32)
    inverse = jnp.zeros((SOURCES,), jnp.int32).at[target].set(token_ids)
    positions = jnp.arange(SEQ, dtype=jnp.int32)
    buckets = bucket_of(positions[None, :] - positions[:, None])
    head_size = D // H

    def forward(patch_rows, text_rows, layout_rows, projection, bias_table, gains, weights_qkv, weight_mix, weight_in, weight_down):
        projected = low_back(jnp.dot(patch_rows, projection, precision=HIGHEST))
        embedded = jnp.where(is_text[:, None], text_rows[text_pick], projected[patch_pick])
        for table in range(4):
            embedded = embedded + layout_rows[table][layout_coords[table]]
        sent = low(low_back(embedded))
        packed = sent[inverse].reshape(ALL_ROWS, SEQ, D)
        bias_full = jnp.transpose(bias_table[buckets], (2, 0, 1))

        @jax.checkpoint
        def one_row(row_input, row_segments):
            normed_one = low(rms_norm(row_input, gains[0]))
            projections = low(low_back(jnp.einsum('td,kde->kte', normed_one, weights_qkv, precision=HIGHEST)))
            split = projections.reshape(3, SEQ, H, head_size).transpose(0, 2, 1, 3)
            scores = jnp.einsum('hqd,hkd->hqk', split[0], split[1], precision=HIGHEST) / math.sqrt(head_size) + bias_full
            scores = low_back(scores)
            same = row_segments[:, None] == row_segments[None, :]
            attention = jax.nn.softmax(jnp.where(same[None], scores, -1e+30), axis=-1)
            mixed = jnp.einsum('hqk,hkd->qhd', low(attention), split[2], precision=HIGHEST).reshape(SEQ, D)
            mixed = low(low_back(mixed))
            attended = row_input + low_back(jnp.dot(mixed, weight_mix, precision=HIGHEST))
            normed_two = low(rms_norm(attended, gains[1]))
            hidden = low_back(jnp.dot(normed_two, weight_in, precision=HIGHEST))
            active = low(jax.nn.gelu(hidden, approximate=True))
            return attended + jnp.dot(active, weight_down, precision=HIGHEST)

        def scan_step(carry, items):
            return (carry, one_row(items[0], items[1]))
        _, result = lax.scan(scan_step, jnp.zeros((), jnp.float32), (packed, segments))
        return result.reshape(SOURCES, D)
    floats = [argument.astype(jnp.float32) for argument in (patches, text_table, layout_tables, patch_proj, rel_table, norm_gains, w_qkv, w_attn_out, w_ff_in, w_ff_out)]
    result, pullback = jax.vjp(forward, *floats)
    grads = pullback(out_grad.astype(jnp.float32))
    return (result.astype(jnp.bfloat16), grads[0], grads[1], grads[2], grads[3], grads[4], grads[5], grads[6], grads[7], grads[8], grads[9])
```

```python
from functools import partial
import math

import jax
import jax.numpy as jnp
from jax import lax
from jax.experimental import pallas as pl
from jax.experimental.pallas import tpu as pltpu
from jax.sharding import PartitionSpec as P

EPSILON = 1e-06
THRESHOLDS = (12, 16, 23, 32, 46, 64, 91)
BLK = 256
NEG = -1e30


def bucket_of(relative):
    magnitude = jnp.abs(relative)
    beyond = 8 + sum(((magnitude >= threshold).astype(jnp.int32) for threshold in THRESHOLDS))
    return jnp.where(relative > 0, 16, 0).astype(jnp.int32) + jnp.where(
        magnitude < 8, magnitude, beyond
    )


def dot_nt(a, b):
    return lax.dot_general(a, b, (((1,), (1,)), ((), ())), preferred_element_type=jnp.float32)

def dot_nn(a, b):
    return lax.dot_general(a, b, (((1,), (0,)), ((), ())), preferred_element_type=jnp.float32)

def dot_tn(a, b):
    return lax.dot_general(a, b, (((0,), (0,)), ((), ())), preferred_element_type=jnp.float32)

def fill_bias(bias, table, slot, flip):
    for step in (-1, 0, 1):
        shift = -step if flip else step
        window = table[slot : slot + 1, BLK * shift + BLK : BLK * shift + 3 * BLK]
        spread = jnp.broadcast_to(window, (BLK, 2 * BLK))
        bias[slot, step + 2] = pltpu.roll(spread, 0, 1, stride=1, stride_axis=0)[:, BLK:]
    low = table[slot : slot + 1, 0:1]
    high = table[slot : slot + 1, 4 * BLK - 1 : 4 * BLK]
    if flip:
        low, high = high, low
    bias[slot, 0] = jnp.broadcast_to(low, (BLK, BLK))
    bias[slot, 4] = jnp.broadcast_to(high, (BLK, BLK))

def span(segs, block, count):
    first = segs[0, block * BLK]
    last = segs[0, block * BLK + BLK - 1]
    low = jnp.int32(0)
    high = jnp.int32(count)
    for other in range(count):
        low = low + (segs[0, other * BLK + BLK - 1] < first).astype(jnp.int32)
        high = high - (segs[0, other * BLK] > last).astype(jnp.int32)
    return low, high

def forward_kernel(segs, q_ref, k_ref, v_ref, aug_q, aug_k, table, out_ref, lse_ref, bias, ka, va):
    length = q_ref.shape[0]
    count = length // BLK
    lane = lax.broadcasted_iota(jnp.int32, (1, 128), 1)
    left = lane < 64
    for h in range(2):
        fill_bias(bias, table, h, False)
        mine = left if h == 0 else jnp.logical_not(left)
        ka[h] = jnp.where(mine, k_ref[...], aug_k[...])
        va[h] = jnp.where(mine, v_ref[...], aug_k[...])
    for qb in range(count):
        rows = pl.ds(qb * BLK, BLK)
        low, high = span(segs, qb, count)
        query = q_ref[rows, :] * jnp.bfloat16(0.125)
        qa = [jnp.where(left, query, aug_q[rows, :]), jnp.where(left, aug_q[rows, :], query)]

        def step(kb, carry):
            keys = pl.ds(pl.multiple_of(kb * BLK, BLK), BLK)
            new = []
            for h in range(2):
                peak, acc = carry[h]
                s = dot_nt(qa[h], ka[h, keys, :]) + bias[h, jnp.clip(kb - qb, -2, 2) + 2]
                top = jnp.maximum(peak, jnp.max(s, axis=1, keepdims=True))
                p = jnp.exp(s - top).astype(jnp.bfloat16)
                acc = acc * jnp.exp(peak - top) + dot_nn(p, va[h, keys, :])
                new.append((top, acc))
            return tuple(new)

        init = tuple(
            (jnp.full((BLK, 1), NEG, jnp.float32), jnp.zeros((BLK, 128), jnp.float32))
            for _ in range(2)
        )
        done = lax.fori_loop(low, high, step, init)
        outs = []
        lses = []
        for h in range(2):
            peak, acc = done[h]
            mark = 72 if h == 0 else 8
            total = acc[:, mark : mark + 1]
            outs.append(acc / total)
            lses.append(jnp.broadcast_to(peak + jnp.log(total), (BLK, 128)))
        out_ref[rows, :] = jnp.where(left, outs[0], outs[1]).astype(jnp.bfloat16)
        lse_ref[rows, :] = jnp.where(left, lses[0], lses[1])

def pieces(value):
    one = value.astype(jnp.bfloat16)
    rest = value - one.astype(jnp.float32)
    two = rest.astype(jnp.bfloat16)
    three = (rest - two.astype(jnp.float32)).astype(jnp.bfloat16)
    return one, two, three

def put_pieces(base, value, lane):
    one, two, three = pieces(value)
    base = jnp.where(jnp.logical_or(lane == 8, lane == 72), one, base)
    base = jnp.where(jnp.logical_or(lane == 9, lane == 73), two, base)
    return jnp.where(jnp.logical_or(lane == 10, lane == 74), three, base)

def diagonal_sums(block):
    wide = jnp.concatenate([block, jnp.zeros_like(block)], axis=1)
    total = wide[:128]
    for start in range(128, BLK, 128):
        total = total + pltpu.roll(wide[start : start + 128], 2 * BLK - start, 1)
    eight = total[:8]
    for start in range(8, 128, 8):
        eight = eight + pltpu.roll(total[start : start + 8], 2 * BLK - start, 1)
    one = eight[:1]
    for row in range(1, 8):
        one = one + pltpu.roll(eight[row : row + 1], 2 * BLK - row, 1)
    return one

def backward_kernel(
    segs, q_ref, k_ref, v_ref, mixed_ref, grad_ref, lse_ref, aug_q, aug_k, table,
    dq_ref, dk_ref, dv_ref, rel_ref,
    bias, rel, ka, va, qa, ga, dq_acc,
):
    length = q_ref.shape[0]
    count = length // BLK
    lane = lax.broadcasted_iota(jnp.int32, (1, 128), 1)
    left = lane < 64
    rel[...] = jnp.zeros_like(rel)
    dq_acc[...] = jnp.zeros_like(dq_acc)
    inner = mixed_ref[...].astype(jnp.float32) * grad_ref[...].astype(jnp.float32)
    query = q_ref[...] * jnp.bfloat16(0.125)
    for h in range(2):
        fill_bias(bias, table, h, True)
        mine = left if h == 0 else jnp.logical_not(left)
        ka[h] = jnp.where(mine, k_ref[...], aug_k[...])
        va[h] = jnp.where(mine, v_ref[...], aug_k[...])
        at = 0 if h == 0 else 64
        qa[h] = jnp.where(mine, query, put_pieces(aug_q[...], -lse_ref[:, at : at + 1], lane))
        delta = jnp.sum(jnp.where(mine, inner, 0.0), axis=1, keepdims=True)
        spare = put_pieces(jnp.zeros((length, 128), jnp.bfloat16), -delta, lane)
        ga[h] = jnp.where(mine, grad_ref[...], spare)
    for kb in range(count):
        keys = pl.ds(kb * BLK, BLK)
        low, high = span(segs, kb, count)

        def step(qb, carry):
            rows = pl.ds(pl.multiple_of(qb * BLK, BLK), BLK)
            new = []
            for h in range(2):
                dk, dv = carry[h]
                place = jnp.clip(kb - qb, -2, 2) + 2
                s = dot_nt(ka[h, keys, :], qa[h, rows, :]) + bias[h, place]
                p = jnp.exp(s)
                ds = p * dot_nt(va[h, keys, :], ga[h, rows, :])
                rel[h, place] += ds
                p = p.astype(jnp.bfloat16)
                ds = ds.astype(jnp.bfloat16)
                dv = dv + dot_nn(p, ga[h, rows, :])
                dk = dk + dot_nn(ds, qa[h, rows, :])
                dq_acc[h, rows, :] += dot_tn(ds, ka[h, keys, :])
                new.append((dk, dv))
            return tuple(new)

        zero = jnp.zeros((BLK, 128), jnp.float32)
        done = lax.fori_loop(low, high, step, ((zero, zero), (zero, zero)))
        dk_ref[keys, :] = jnp.where(left, done[0][0], done[1][0]).astype(jnp.bfloat16)
        dv_ref[keys, :] = jnp.where(left, done[0][1], done[1][1]).astype(jnp.bfloat16)
    dq_ref[...] = (jnp.where(left, dq_acc[0], dq_acc[1]) * 0.125).astype(jnp.bfloat16)
    for h in range(2):
        pieces_out = []
        for place in range(5):
            if place in (0, 4):
                summed = jnp.sum(rel[h, place], axis=0, keepdims=True)
                pieces_out.append(jnp.concatenate([summed, jnp.zeros((1, BLK), jnp.float32)], axis=1))
            else:
                pieces_out.append(diagonal_sums(rel[h, place]))
        rel_ref[h] = jnp.concatenate(pieces_out + [jnp.zeros((3, 2 * BLK), jnp.float32)], axis=0)

def attention_forward(segments, qkv, aug_q, aug_k, table):
    _, length, width = qkv.shape
    pairs = width // 128
    def part(which):
        return pl.BlockSpec((None, length, 128), lambda p, s: (which, 0, p))
    whole = pl.BlockSpec((length, 128), lambda p, s: (0, 0))
    col = pl.BlockSpec((length, 128), lambda p, s: (0, p))
    return pl.pallas_call(
        forward_kernel,
        out_shape=(jax.ShapeDtypeStruct((length, width), jnp.bfloat16), jax.ShapeDtypeStruct((length, width), jnp.float32)),
        grid_spec=pltpu.PrefetchScalarGridSpec(
            num_scalar_prefetch=1, grid=(pairs,),
            in_specs=[part(0), part(1), part(2), whole, whole, pl.BlockSpec((None, 2, table.shape[2]), lambda p, s: (p, 0, 0))],
            out_specs=[col, col],
            scratch_shapes=[pltpu.VMEM((2, 5, BLK, BLK), jnp.float32), pltpu.VMEM((2, length, 128), jnp.bfloat16), pltpu.VMEM((2, length, 128), jnp.bfloat16)],
        ),
        compiler_params=pltpu.CompilerParams(vmem_limit_bytes=48 * 2**20),
        name="attention_forward",
    )(segments, qkv, qkv, qkv, aug_q, aug_k, table)

def attention_backward(segments, qkv, mixed, grad_mixed, lse, aug_q, aug_k, table):
    _, length, width = qkv.shape
    pairs = width // 128
    def part(which):
        return pl.BlockSpec((None, length, 128), lambda p, s: (which, 0, p))
    whole = pl.BlockSpec((length, 128), lambda p, s: (0, 0))
    col = pl.BlockSpec((length, 128), lambda p, s: (0, p))
    out = jax.ShapeDtypeStruct((length, width), jnp.bfloat16)
    buf = pltpu.VMEM((2, length, 128), jnp.bfloat16)
    return pl.pallas_call(
        backward_kernel,
        out_shape=(out, out, out, jax.ShapeDtypeStruct((pairs * 2, 8, 2 * BLK), jnp.float32)),
        grid_spec=pltpu.PrefetchScalarGridSpec(
            num_scalar_prefetch=1, grid=(pairs,),
            in_specs=[part(0), part(1), part(2), col, col, col, whole, whole, pl.BlockSpec((None, 2, table.shape[2]), lambda p, s: (p, 0, 0))],
            out_specs=[col, col, col, pl.BlockSpec((2, 8, 2 * BLK), lambda p, s: (p, 0, 0))],
            scratch_shapes=[pltpu.VMEM((2, 5, BLK, BLK), jnp.float32), pltpu.VMEM((2, 5, BLK, BLK), jnp.float32),
                buf, buf, buf, buf, pltpu.VMEM((2, length, 128), jnp.float32)],
        ),
        compiler_params=pltpu.CompilerParams(vmem_limit_bytes=48 * 2**20),
        name="attention_backward",
    )(segments, qkv, qkv, qkv, mixed, grad_mixed, lse, aug_q, aug_k, table)

def bucket_choice(offsets, count):
    return (bucket_of(offsets)[:, None] == jnp.arange(count, dtype=jnp.int32)[None, :]).astype(jnp.float32)

def prepare(segments, rel_table):
    heads = rel_table.shape[1]
    offsets = jnp.arange(4 * BLK, dtype=jnp.int32) - 2 * BLK
    tables = []
    for sign in (1, -1):
        choose = bucket_choice(sign * offsets, rel_table.shape[0])
        table = lax.dot_general(rel_table, choose, (((0,), (1,)), ((), ())), precision=lax.Precision.HIGHEST)
        tables.append(table.reshape(heads // 2, 2, 4 * BLK))
    lane = (jnp.arange(128, dtype=jnp.int32) % 64)[None, :]
    row = segments.reshape(-1)[:, None]
    same = lane == row
    aug_q = jnp.where(jnp.logical_or(same, lane >= 8), 0.0, NEG).astype(jnp.bfloat16)
    aug_k = jnp.where(jnp.logical_or(same, jnp.logical_and(lane >= 8, lane < 11)), 1.0, 0.0).astype(jnp.bfloat16)
    return aug_q, aug_k, tables[0], tables[1]

def rel_gradient(rel, count):
    lane = jnp.arange(2 * BLK, dtype=jnp.int32)
    parts = []
    for place in range(5):
        if place == 0:
            offset = jnp.full((2 * BLK,), -600, jnp.int32)
        elif place == 4:
            offset = jnp.full((2 * BLK,), 600, jnp.int32)
        else:
            offset = BLK * (place - 2) - jnp.where(lane < BLK, lane, lane - 2 * BLK)
        parts.append(bucket_choice(offset, count))
    choose = jnp.concatenate(parts + [jnp.zeros((3 * 2 * BLK, count), jnp.float32)], axis=0)
    flat = rel.reshape(rel.shape[0], -1)
    return lax.dot_general(choose, flat, (((0,), (1,)), ((), ())), precision=lax.Precision.HIGHEST)


def contract_rows(left, right):
    return lax.dot_general(
        left, right, (((0,), (0,)), ((), ())), preferred_element_type=jnp.float32
    )


def times_transpose(left, right):
    return lax.dot_general(
        left, right, (((1,), (1,)), ((), ())), preferred_element_type=jnp.float32
    )


def norm_backward(grad_normed, unit, scale, gain):
    grad_unit = grad_normed * gain
    grad_input = scale * (grad_unit - unit * jnp.mean(grad_unit * unit, axis=-1, keepdims=True))
    return (grad_input, jnp.sum(grad_normed * unit, axis=0))


def shards(
    patches,
    src_kind,
    src_index,
    layout_coords,
    placing,
    segments,
    text_table,
    layout_tables,
    patch_proj,
    rel_table,
    norm_gains,
    w_qkv,
    w_attn_out,
    w_ff_in,
    w_ff_out,
    out_grad,
):
    data_count = lax.axis_size("dp")
    row_tokens = placing.shape[0]
    capacity = 2 * row_tokens // data_count
    width = text_table.shape[1]
    row_count, seq_len = segments.shape
    heads = rel_table.shape[1]
    head_size = width // heads
    full_qkv, full_mix, full_in, full_down, full_gains, full_proj, full_layout = (
        lax.all_gather(w_qkv, "dp", axis=1, tiled=True),
        lax.all_gather(w_attn_out, "dp", axis=0, tiled=True),
        lax.all_gather(w_ff_in, "dp", axis=0, tiled=True),
        lax.all_gather(w_ff_out, "dp", axis=0, tiled=True),
        lax.all_gather(norm_gains, "dp", axis=1, tiled=True),
        lax.all_gather(patch_proj, "dp", axis=0, tiled=True),
        lax.all_gather(layout_tables, "dp", axis=1, tiled=True),
    )
    is_text = src_kind == 1
    text_pick = jnp.where(is_text, src_index, 0)
    patch_pick = jnp.where(is_text, 0, src_index)
    projected = jnp.dot(patches, full_proj, preferred_element_type=jnp.float32)
    from_text = jnp.take(text_table, text_pick, axis=0).astype(jnp.float32)
    from_patch = jnp.take(projected, patch_pick, axis=0)
    embedded = jnp.where(is_text[:, None], from_text, from_patch)
    for table in range(full_layout.shape[0]):
        embedded = embedded + jnp.take(full_layout[table], layout_coords[table], axis=0).astype(
            jnp.float32
        )
    sent = embedded.astype(jnp.bfloat16)
    owner = placing // row_tokens
    position = placing % row_tokens
    member = (owner[:, None] == jnp.arange(data_count, dtype=jnp.int32)[None, :]).astype(jnp.int32)
    ranks = jnp.sum(jnp.cumsum(member, axis=0) * member, axis=1) - 1
    slots = owner * capacity + ranks
    send_rows = (
        jnp.zeros((data_count * capacity, width), jnp.bfloat16)
        .at[slots]
        .set(sent)
        .reshape(data_count, capacity, width)
    )
    send_places = (
        jnp.full((data_count * capacity,), -1, jnp.int32)
        .at[slots]
        .set(position)
        .reshape(data_count, capacity)
    )
    arrived, arrived_places = (
        lax.all_to_all(send_rows, "dp", split_axis=0, concat_axis=0, tiled=True),
        lax.all_to_all(send_places, "dp", split_axis=0, concat_axis=0, tiled=True),
    )
    flat_places = arrived_places.reshape(-1)
    landing = jnp.where(flat_places >= 0, flat_places, row_tokens)
    packed = (
        jnp.zeros((row_tokens, width), jnp.bfloat16)
        .at[landing]
        .set(arrived.reshape(-1, width), mode="drop")
        .astype(jnp.float32)
    )
    gain_one = full_gains[0].astype(jnp.float32)
    gain_two = full_gains[1].astype(jnp.float32)
    scale_one = lax.rsqrt(jnp.mean(packed * packed, axis=-1, keepdims=True) + EPSILON)
    unit_one = packed * scale_one
    normed_one = (unit_one * gain_one).astype(jnp.bfloat16)
    projections = jnp.einsum(
        "td,kde->kte", normed_one, full_qkv, preferred_element_type=jnp.float32
    ).astype(jnp.bfloat16)

    aug_q, aug_k, table, mirrored = prepare(segments, rel_table)
    mixed, lse = attention_forward(segments, projections, aug_q, aug_k, table)
    attended = packed + jnp.dot(mixed, full_mix, preferred_element_type=jnp.float32)
    scale_two = lax.rsqrt(jnp.mean(attended * attended, axis=-1, keepdims=True) + EPSILON)
    unit_two = attended * scale_two
    normed_two = (unit_two * gain_two).astype(jnp.bfloat16)
    hidden = jnp.dot(normed_two, full_in, preferred_element_type=jnp.float32)
    active = jax.nn.gelu(hidden, approximate=True).astype(jnp.bfloat16)
    result = (attended + jnp.dot(active, full_down, preferred_element_type=jnp.float32)).astype(
        jnp.bfloat16
    )
    back_qkv, back_mix, back_in, back_down, back_gains, back_proj = (
        lax.all_gather(w_qkv, "dp", axis=1, tiled=True),
        lax.all_gather(w_attn_out, "dp", axis=0, tiled=True),
        lax.all_gather(w_ff_in, "dp", axis=0, tiled=True),
        lax.all_gather(w_ff_out, "dp", axis=0, tiled=True),
        lax.all_gather(norm_gains, "dp", axis=1, tiled=True),
        lax.all_gather(patch_proj, "dp", axis=0, tiled=True),
    )
    back_one = back_gains[0].astype(jnp.float32)
    back_two = back_gains[1].astype(jnp.float32)
    grad_down = contract_rows(active, out_grad)
    grad_active = times_transpose(out_grad, back_down)
    _, gelu_pull = jax.vjp(partial(jax.nn.gelu, approximate=True), hidden)
    grad_hidden = gelu_pull(grad_active)[0].astype(jnp.bfloat16)
    grad_in = contract_rows(normed_two, grad_hidden)
    grad_normed_two = times_transpose(grad_hidden, back_in)
    grad_attended, grad_gain_two = norm_backward(grad_normed_two, unit_two, scale_two, back_two)
    grad_attended = grad_attended + out_grad.astype(jnp.float32)
    grad_branch = grad_attended.astype(jnp.bfloat16)
    grad_mix = contract_rows(mixed, grad_branch)
    grad_mixed = times_transpose(grad_branch, back_mix).astype(jnp.bfloat16)
    grad_query, grad_keys, grad_values, grad_rel = attention_backward(
        segments, projections, mixed, grad_mixed, lse, aug_q, aug_k, mirrored
    )
    grad_projections = jnp.stack([grad_query, grad_keys, grad_values])
    grad_qkv = jnp.einsum(
        "td,kte->kde", normed_one, grad_projections, preferred_element_type=jnp.float32
    )
    grad_normed_one = jnp.einsum(
        "kte,kde->td", grad_projections, back_qkv, preferred_element_type=jnp.float32
    )
    grad_packed, grad_gain_one = norm_backward(grad_normed_one, unit_one, scale_one, back_one)
    grad_packed = (grad_packed + grad_attended).astype(jnp.bfloat16)
    grad_bias = rel_gradient(grad_rel, rel_table.shape[0])
    back_places = jnp.where(flat_places >= 0, flat_places, 0)
    returned = jnp.where(
        (flat_places >= 0)[:, None],
        jnp.take(grad_packed, back_places, axis=0),
        jnp.zeros((), jnp.bfloat16),
    )
    came_back = lax.all_to_all(
        returned.reshape(data_count, capacity, width), "dp", split_axis=0, concat_axis=0, tiled=True
    ).reshape(-1, width)
    grad_embedded = jnp.take(came_back, slots, axis=0)
    grad_wide = grad_embedded.astype(jnp.float32)
    text_part = jnp.where(is_text[:, None], grad_wide, 0.0)
    grad_text = jnp.zeros((text_table.shape[0], width), jnp.float32).at[text_pick].add(text_part)
    patch_part = jnp.where(is_text[:, None], jnp.zeros((), jnp.bfloat16), grad_embedded)
    grad_projected = (
        jnp.zeros((patches.shape[0], width), jnp.bfloat16).at[patch_pick].add(patch_part)
    )
    grad_proj = contract_rows(patches, grad_projected)
    grad_patches = times_transpose(grad_projected, back_proj)
    layout_rows = full_layout.shape[1]
    grad_layout = jnp.stack(
        [
            jnp.zeros((layout_rows, width), jnp.float32).at[layout_coords[table]].add(grad_wide)
            for table in range(full_layout.shape[0])
        ]
    )
    (
        shard_qkv,
        shard_mix,
        shard_in,
        shard_down,
        shard_gain_one,
        shard_gain_two,
        shard_proj,
        shard_layout,
    ) = (
        lax.psum_scatter(grad_qkv, "dp", scatter_dimension=1, tiled=True),
        lax.psum_scatter(grad_mix, "dp", scatter_dimension=0, tiled=True),
        lax.psum_scatter(grad_in, "dp", scatter_dimension=0, tiled=True),
        lax.psum_scatter(grad_down, "dp", scatter_dimension=0, tiled=True),
        lax.psum_scatter(grad_gain_one, "dp", scatter_dimension=0, tiled=True),
        lax.psum_scatter(grad_gain_two, "dp", scatter_dimension=0, tiled=True),
        lax.psum_scatter(grad_proj, "dp", scatter_dimension=0, tiled=True),
        lax.psum_scatter(grad_layout, "dp", scatter_dimension=1, tiled=True),
    )
    shard_gains = jnp.stack([shard_gain_one, shard_gain_two])
    summed = (
        lax.psum(shard_qkv.astype(jnp.bfloat16), "stream").astype(jnp.float32),
        lax.psum(shard_mix.astype(jnp.bfloat16), "stream").astype(jnp.float32),
        lax.psum(shard_in.astype(jnp.bfloat16), "stream").astype(jnp.float32),
        lax.psum(shard_down.astype(jnp.bfloat16), "stream").astype(jnp.float32),
        lax.psum(shard_gains.astype(jnp.bfloat16), "stream").astype(jnp.float32),
        lax.psum(shard_proj.astype(jnp.bfloat16), "stream").astype(jnp.float32),
        lax.psum(shard_layout.astype(jnp.bfloat16), "stream").astype(jnp.float32),
        lax.psum(grad_text.astype(jnp.bfloat16), "stream").astype(jnp.float32),
    )
    grad_table = lax.psum(grad_bias, ("dp", "stream"))
    return (
        result,
        grad_patches,
        summed[7],
        summed[6],
        summed[5],
        grad_table,
        summed[4],
        summed[0],
        summed[1],
        summed[2],
        summed[3],
    )


def solution(mesh):
    return jax.shard_map(
        shards,
        mesh=mesh,
        in_specs=(
            P(("dp", "stream"), None),
            P(("dp", "stream")),
            P(("dp", "stream")),
            P(None, ("dp", "stream")),
            P(("dp", "stream")),
            P(("dp", "stream"), None),
            P("dp", None),
            P(None, "dp", None),
            P("dp", None),
            P(),
            P(None, "dp"),
            P(None, "dp", None),
            P("dp", None),
            P("dp", None),
            P("dp", None),
            P(("dp", "stream"), None),
        ),
        out_specs=(
            P(("dp", "stream"), None),
            P(("dp", "stream"), None),
            P("dp", None),
            P(None, "dp", None),
            P("dp", None),
            P(),
            P(None, "dp"),
            P(None, "dp", None),
            P("dp", None),
            P("dp", None),
            P("dp", None),
        ),
        check_vma=False,
    )
```

```python
from functools import partial

import jax
import jax.numpy as jnp
from jax import lax
from jax.experimental import pallas as pl
from jax.experimental.pallas import tpu as pltpu
from jax.sharding import PartitionSpec as P

EPSILON = 1e-06
THRESHOLDS = (12, 16, 23, 32, 46, 64, 91)
BLK = 256
NEG = -1e30
VMEM_LIMIT = 48 * 2**20


def bucket_of(relative):
    magnitude = jnp.abs(relative)
    beyond = 8 + sum(((magnitude >= threshold).astype(jnp.int32) for threshold in THRESHOLDS))
    return jnp.where(relative > 0, 16, 0).astype(jnp.int32) + jnp.where(
        magnitude < 8, magnitude, beyond
    )


def dot_nt(a, b):
    return lax.dot_general(a, b, (((1,), (1,)), ((), ())), preferred_element_type=jnp.float32)

def dot_nn(a, b):
    return lax.dot_general(a, b, (((1,), (0,)), ((), ())), preferred_element_type=jnp.float32)

def dot_tn(a, b):
    return lax.dot_general(a, b, (((0,), (0,)), ((), ())), preferred_element_type=jnp.float32)

def fill_bias(bias, table, slot, flip):
    for step in (-1, 0, 1):
        shift = -step if flip else step
        window = table[slot : slot + 1, BLK * shift + BLK : BLK * shift + 3 * BLK]
        spread = jnp.broadcast_to(window, (BLK, 2 * BLK))
        bias[slot, step + 2] = pltpu.roll(spread, 0, 1, stride=1, stride_axis=0)[:, BLK:]
    low = table[slot : slot + 1, 0:1]
    high = table[slot : slot + 1, 4 * BLK - 1 : 4 * BLK]
    if flip:
        low, high = high, low
    bias[slot, 0] = jnp.broadcast_to(low, (BLK, BLK))
    bias[slot, 4] = jnp.broadcast_to(high, (BLK, BLK))

def span(segs, block, count):
    first = segs[0, block * BLK]
    last = segs[0, block * BLK + BLK - 1]
    low = jnp.int32(0)
    high = jnp.int32(count)
    for other in range(count):
        low = low + (segs[0, other * BLK + BLK - 1] < first).astype(jnp.int32)
        high = high - (segs[0, other * BLK] > last).astype(jnp.int32)
    return low, high

def forward_kernel(segs, q_ref, k_ref, v_ref, aug_q, aug_k, table, out_ref, lse_ref, bias, ka, va):
    length = q_ref.shape[0]
    count = length // BLK
    lane = lax.broadcasted_iota(jnp.int32, (1, 128), 1)
    left = lane < 64
    for h in range(2):
        fill_bias(bias, table, h, False)
        mine = left if h == 0 else jnp.logical_not(left)
        ka[h] = jnp.where(mine, k_ref[...], aug_k[...])
        va[h] = jnp.where(mine, v_ref[...], aug_k[...])
    for qb in range(count):
        rows = pl.ds(qb * BLK, BLK)
        low, high = span(segs, qb, count)
        query = q_ref[rows, :] * jnp.bfloat16(0.125)
        qa = [jnp.where(left, query, aug_q[rows, :]), jnp.where(left, aug_q[rows, :], query)]

        def step(kb, carry):
            keys = pl.ds(pl.multiple_of(kb * BLK, BLK), BLK)
            new = []
            for h in range(2):
                peak, acc = carry[h]
                s = dot_nt(qa[h], ka[h, keys, :]) + bias[h, jnp.clip(kb - qb, -2, 2) + 2]
                top = jnp.maximum(peak, jnp.max(s, axis=1, keepdims=True))
                p = jnp.exp(s - top).astype(jnp.bfloat16)
                acc = acc * jnp.exp(peak - top) + dot_nn(p, va[h, keys, :])
                new.append((top, acc))
            return tuple(new)

        init = tuple(
            (jnp.full((BLK, 1), NEG, jnp.float32), jnp.zeros((BLK, 128), jnp.float32))
            for _ in range(2)
        )
        done = lax.fori_loop(low, high, step, init)
        outs = []
        lses = []
        for h in range(2):
            peak, acc = done[h]
            mark = 72 if h == 0 else 8
            total = acc[:, mark : mark + 1]
            outs.append(acc / total)
            lses.append(jnp.broadcast_to(peak + jnp.log(total), (BLK, 128)))
        out_ref[rows, :] = jnp.where(left, outs[0], outs[1]).astype(jnp.bfloat16)
        lse_ref[rows, :] = jnp.where(left, lses[0], lses[1])

def pieces(value):
    one = value.astype(jnp.bfloat16)
    rest = value - one.astype(jnp.float32)
    two = rest.astype(jnp.bfloat16)
    three = (rest - two.astype(jnp.float32)).astype(jnp.bfloat16)
    return one, two, three

def put_pieces(base, value, lane):
    one, two, three = pieces(value)
    base = jnp.where(jnp.logical_or(lane == 8, lane == 72), one, base)
    base = jnp.where(jnp.logical_or(lane == 9, lane == 73), two, base)
    return jnp.where(jnp.logical_or(lane == 10, lane == 74), three, base)

def diagonal_sums(block):
    wide = jnp.concatenate([block, jnp.zeros_like(block)], axis=1)
    total = wide[:128]
    for start in range(128, BLK, 128):
        total = total + pltpu.roll(wide[start : start + 128], 2 * BLK - start, 1)
    eight = total[:8]
    for start in range(8, 128, 8):
        eight = eight + pltpu.roll(total[start : start + 8], 2 * BLK - start, 1)
    one = eight[:1]
    for row in range(1, 8):
        one = one + pltpu.roll(eight[row : row + 1], 2 * BLK - row, 1)
    return one

def backward_kernel(
    segs, q_ref, k_ref, v_ref, mixed_ref, grad_ref, lse_ref, aug_q, aug_k, table,
    dq_ref, dk_ref, dv_ref, rel_ref,
    bias, rel, ka, va, qa, ga, dq_acc,
):
    length = q_ref.shape[0]
    count = length // BLK
    lane = lax.broadcasted_iota(jnp.int32, (1, 128), 1)
    left = lane < 64
    rel[...] = jnp.zeros_like(rel)
    dq_acc[...] = jnp.zeros_like(dq_acc)
    inner = mixed_ref[...].astype(jnp.float32) * grad_ref[...].astype(jnp.float32)
    query = q_ref[...] * jnp.bfloat16(0.125)
    for h in range(2):
        fill_bias(bias, table, h, True)
        mine = left if h == 0 else jnp.logical_not(left)
        ka[h] = jnp.where(mine, k_ref[...], aug_k[...])
        va[h] = jnp.where(mine, v_ref[...], aug_k[...])
        at = 0 if h == 0 else 64
        qa[h] = jnp.where(mine, query, put_pieces(aug_q[...], -lse_ref[:, at : at + 1], lane))
        delta = jnp.sum(jnp.where(mine, inner, 0.0), axis=1, keepdims=True)
        spare = put_pieces(jnp.zeros((length, 128), jnp.bfloat16), -delta, lane)
        ga[h] = jnp.where(mine, grad_ref[...], spare)
    for kb in range(count):
        keys = pl.ds(kb * BLK, BLK)
        low, high = span(segs, kb, count)

        def step(qb, carry):
            rows = pl.ds(pl.multiple_of(qb * BLK, BLK), BLK)
            new = []
            for h in range(2):
                dk, dv = carry[h]
                place = jnp.clip(kb - qb, -2, 2) + 2
                s = dot_nt(ka[h, keys, :], qa[h, rows, :]) + bias[h, place]
                p = jnp.exp(s)
                ds = p * dot_nt(va[h, keys, :], ga[h, rows, :])
                rel[h, place] += ds
                p = p.astype(jnp.bfloat16)
                ds = ds.astype(jnp.bfloat16)
                dv = dv + dot_nn(p, ga[h, rows, :])
                dk = dk + dot_nn(ds, qa[h, rows, :])
                dq_acc[h, rows, :] += dot_tn(ds, ka[h, keys, :])
                new.append((dk, dv))
            return tuple(new)

        zero = jnp.zeros((BLK, 128), jnp.float32)
        done = lax.fori_loop(low, high, step, ((zero, zero), (zero, zero)))
        dk_ref[keys, :] = jnp.where(left, done[0][0], done[1][0]).astype(jnp.bfloat16)
        dv_ref[keys, :] = jnp.where(left, done[0][1], done[1][1]).astype(jnp.bfloat16)
    dq_ref[...] = (jnp.where(left, dq_acc[0], dq_acc[1]) * 0.125).astype(jnp.bfloat16)
    for h in range(2):
        pieces_out = []
        for place in range(5):
            if place in (0, 4):
                summed = jnp.sum(rel[h, place], axis=0, keepdims=True)
                pieces_out.append(jnp.concatenate([summed, jnp.zeros((1, BLK), jnp.float32)], axis=1))
            else:
                pieces_out.append(diagonal_sums(rel[h, place]))
        rel_ref[h] = jnp.concatenate(pieces_out + [jnp.zeros((3, 2 * BLK), jnp.float32)], axis=0)

def attention_forward(segments, qkv, aug_q, aug_k, table):
    _, length, width = qkv.shape
    pairs = width // 128
    def part(which):
        return pl.BlockSpec((None, length, 128), lambda p, s: (which, 0, p))
    whole = pl.BlockSpec((length, 128), lambda p, s: (0, 0))
    col = pl.BlockSpec((length, 128), lambda p, s: (0, p))
    return pl.pallas_call(
        forward_kernel,
        out_shape=(jax.ShapeDtypeStruct((length, width), jnp.bfloat16), jax.ShapeDtypeStruct((length, width), jnp.float32)),
        grid_spec=pltpu.PrefetchScalarGridSpec(
            num_scalar_prefetch=1, grid=(pairs,),
            in_specs=[part(0), part(1), part(2), whole, whole, pl.BlockSpec((None, 2, table.shape[2]), lambda p, s: (p, 0, 0))],
            out_specs=[col, col],
            scratch_shapes=[pltpu.VMEM((2, 5, BLK, BLK), jnp.float32), pltpu.VMEM((2, length, 128), jnp.bfloat16), pltpu.VMEM((2, length, 128), jnp.bfloat16)],
        ),
        compiler_params=pltpu.CompilerParams(vmem_limit_bytes=VMEM_LIMIT),
        name="attention_forward",
    )(segments, qkv, qkv, qkv, aug_q, aug_k, table)

def attention_backward(segments, qkv, mixed, grad_mixed, lse, aug_q, aug_k, table):
    _, length, width = qkv.shape
    pairs = width // 128
    def part(which):
        return pl.BlockSpec((None, length, 128), lambda p, s: (which, 0, p))
    whole = pl.BlockSpec((length, 128), lambda p, s: (0, 0))
    col = pl.BlockSpec((length, 128), lambda p, s: (0, p))
    out = jax.ShapeDtypeStruct((length, width), jnp.bfloat16)
    buf = pltpu.VMEM((2, length, 128), jnp.bfloat16)
    return pl.pallas_call(
        backward_kernel,
        out_shape=(out, out, out, jax.ShapeDtypeStruct((pairs * 2, 8, 2 * BLK), jnp.float32)),
        grid_spec=pltpu.PrefetchScalarGridSpec(
            num_scalar_prefetch=1, grid=(pairs,),
            in_specs=[part(0), part(1), part(2), col, col, col, whole, whole, pl.BlockSpec((None, 2, table.shape[2]), lambda p, s: (p, 0, 0))],
            out_specs=[col, col, col, pl.BlockSpec((2, 8, 2 * BLK), lambda p, s: (p, 0, 0))],
            scratch_shapes=[pltpu.VMEM((2, 5, BLK, BLK), jnp.float32), pltpu.VMEM((2, 5, BLK, BLK), jnp.float32),
                buf, buf, buf, buf, pltpu.VMEM((2, length, 128), jnp.float32)],
        ),
        compiler_params=pltpu.CompilerParams(vmem_limit_bytes=VMEM_LIMIT),
        name="attention_backward",
    )(segments, qkv, qkv, qkv, mixed, grad_mixed, lse, aug_q, aug_k, table)

def bucket_choice(offsets, count):
    return (bucket_of(offsets)[:, None] == jnp.arange(count, dtype=jnp.int32)[None, :]).astype(jnp.float32)

def prepare(segments, rel_table):
    heads = rel_table.shape[1]
    offsets = jnp.arange(4 * BLK, dtype=jnp.int32) - 2 * BLK
    tables = []
    for sign in (1, -1):
        choose = bucket_choice(sign * offsets, rel_table.shape[0])
        table = lax.dot_general(rel_table, choose, (((0,), (1,)), ((), ())), precision=lax.Precision.HIGHEST)
        tables.append(table.reshape(heads // 2, 2, 4 * BLK))
    lane = (jnp.arange(128, dtype=jnp.int32) % 64)[None, :]
    row = segments.reshape(-1)[:, None]
    same = lane == row
    aug_q = jnp.where(jnp.logical_or(same, lane >= 8), 0.0, NEG).astype(jnp.bfloat16)
    aug_k = jnp.where(jnp.logical_or(same, jnp.logical_and(lane >= 8, lane < 11)), 1.0, 0.0).astype(jnp.bfloat16)
    return aug_q, aug_k, tables[0], tables[1]

def rel_gradient(rel, count):
    lane = jnp.arange(2 * BLK, dtype=jnp.int32)
    parts = []
    for place in range(5):
        if place == 0:
            offset = jnp.full((2 * BLK,), -600, jnp.int32)
        elif place == 4:
            offset = jnp.full((2 * BLK,), 600, jnp.int32)
        else:
            offset = BLK * (place - 2) - jnp.where(lane < BLK, lane, lane - 2 * BLK)
        parts.append(bucket_choice(offset, count))
    choose = jnp.concatenate(parts + [jnp.zeros((3 * 2 * BLK, count), jnp.float32)], axis=0)
    flat = rel.reshape(rel.shape[0], -1)
    return lax.dot_general(choose, flat, (((0,), (1,)), ((), ())), precision=lax.Precision.HIGHEST)


def iota(shape, axis):
    return lax.broadcasted_iota(jnp.int32, shape, axis)


def as_bf16(flag):
    return jnp.where(flag, 1.0, 0.0).astype(jnp.bfloat16)


def slots_kernel(owners, capacity, shift, place_ref, kind_ref, index_ref, coords_ref,
                 slot_ref, meta_ref, text_ref):
    tokens = place_ref.shape[1]
    place = place_ref[...]
    text = kind_ref[...] == 1
    owner = jnp.right_shift(place, shift)
    position = jnp.bitwise_and(place, (1 << shift) - 1)
    rows = owners + 16
    row = iota((rows, tokens), 0)
    member = jnp.logical_or(row == owner, jnp.logical_and(row == owners, text))
    upto = as_bf16(iota((tokens, tokens), 0) <= iota((tokens, tokens), 1))
    counts = dot_nn(as_bf16(member), upto)
    rank = jnp.sum(jnp.where(row == owner, counts, 0.0), axis=0, keepdims=True)
    rank = rank.astype(jnp.int32) - 1
    text_rank = jnp.where(text, counts[owners : owners + 1].astype(jnp.int32) - 1, 0)
    slot = owner * capacity + rank
    slot_ref[...] = slot
    index = index_ref[...]
    coords = coords_ref[...]
    low = jnp.bitwise_and(coords, 3)
    high = jnp.right_shift(coords, 2)
    meta = jnp.concatenate(
        [
            kind_ref[...] + 1,
            jnp.right_shift(position, 2), jnp.bitwise_and(position, 3),
            high, low,
            jnp.right_shift(index, 4), jnp.bitwise_and(index, 15),
            jnp.right_shift(text_rank, 2), jnp.bitwise_and(text_rank, 3),
            jnp.zeros_like(index),
        ],
        axis=0,
    ).astype(jnp.float32).astype(jnp.bfloat16)
    slots = meta_ref.shape[1]
    for start in range(0, slots, 512):
        pick = as_bf16(iota((512, tokens), 0) + start == slot)
        meta_ref[:, start : start + 512] = dot_nt(meta, pick).astype(jnp.bfloat16)
    texts = text_ref.shape[1]
    chosen = as_bf16(jnp.logical_and(iota((texts, tokens), 0) == text_rank, text))
    found = dot_nt(meta, chosen)
    text_ref[...] = jnp.broadcast_to(
        (found[11:12] * 16.0 + found[12:13]).astype(jnp.int32), text_ref.shape
    )


def find_slots(owners, capacity, shift, placing, src_kind, src_index, coords, texts):
    tokens = placing.shape[0]
    slots = owners * capacity
    return pl.pallas_call(
        partial(slots_kernel, owners, capacity, shift),
        out_shape=(
            jax.ShapeDtypeStruct((1, tokens), jnp.int32),
            jax.ShapeDtypeStruct((16, slots), jnp.bfloat16),
            jax.ShapeDtypeStruct((8, texts), jnp.int32),
        ),
        compiler_params=pltpu.CompilerParams(vmem_limit_bytes=VMEM_LIMIT),
        name="find_slots",
    )(placing.reshape(1, -1), src_kind.reshape(1, -1), src_index.reshape(1, -1), coords)


def pick_kernel(key_ref, rows_ref, out_ref):
    size, tokens = out_ref.shape[0], rows_ref.shape[0]
    pick = as_bf16(iota((size, tokens), 0) + pl.program_id(0) * size == key_ref[...])
    out_ref[...] = dot_nn(pick, rows_ref[...]).astype(jnp.bfloat16)


def pick_rows(keys, rows, count, name):
    tokens, width = rows.shape
    size = min(512, count)
    return pl.pallas_call(
        pick_kernel,
        out_shape=jax.ShapeDtypeStruct((count, width), jnp.bfloat16),
        grid=(count // size,),
        in_specs=[
            pl.BlockSpec((1, tokens), lambda i: (0, 0)),
            pl.BlockSpec((tokens, width), lambda i: (0, 0)),
        ],
        out_specs=pl.BlockSpec((size, width), lambda i: (i, 0)),
        compiler_params=pltpu.CompilerParams(vmem_limit_bytes=VMEM_LIMIT),
        name=name,
    )(keys, rows)


def place_kernel(meta_ref, column_ref, row_ref, place_ref):
    slots, tokens = meta_ref.shape[1], row_ref.shape[1]
    meta = meta_ref[...]
    wide = meta.astype(jnp.float32)
    place = (wide[1:2] * 4.0 + wide[2:3]).astype(jnp.int32)
    place = jnp.where(wide[0:1] > 0.5, place, -1)
    place_ref[...] = jnp.broadcast_to(place, place_ref.shape)
    for start in range(0, tokens, 256):
        pick = as_bf16(iota((256, slots), 0) + start == place)
        down = dot_nt(pick, meta)
        values = [down[:, 0:1]] + [down[:, 3 + c : 4 + c] * 4.0 + down[:, 7 + c : 8 + c] for c in range(4)]
        lane = iota((256, 8), 1)
        block = jnp.zeros((256, 8), jnp.float32)
        for c in range(5):
            block = jnp.where(lane == c, values[c], block)
        column_ref[start : start + 256, :] = block.astype(jnp.int32)
        across = dot_nt(meta, pick)
        row_ref[:, start : start + 256] = jnp.concatenate(
            [across[0:1], across[3:7] * 4.0 + across[7:11], jnp.zeros((3, 256), jnp.float32)], axis=0
        ).astype(jnp.int32)


def place_meta(meta, tokens):
    return pl.pallas_call(
        place_kernel,
        out_shape=(
            jax.ShapeDtypeStruct((tokens, 8), jnp.int32),
            jax.ShapeDtypeStruct((8, tokens), jnp.int32),
            jax.ShapeDtypeStruct((8, meta.shape[1]), jnp.int32),
        ),
        compiler_params=pltpu.CompilerParams(vmem_limit_bytes=VMEM_LIMIT),
        name="place_meta",
    )(meta)


def lookup_kernel(mine_ref, other_ref, table_ref, mine_out, other_out):
    entries = table_ref.shape[1]
    for coords, out in ((mine_ref, mine_out), (other_ref, other_out)):
        total = jnp.zeros(out.shape, jnp.float32)
        for table in range(4):
            pick = as_bf16(iota((out.shape[0], entries), 1) == coords[:, table + 1 : table + 2])
            total = total + dot_nn(pick, table_ref[table])
        out[...] = total


def layout_lookup(mine, other, tables):
    tokens = mine.shape[0]
    width = tables.shape[2]
    column = pl.BlockSpec((256, 8), lambda i: (i, 0))
    out = pl.BlockSpec((256, width), lambda i: (i, 0))
    shape = jax.ShapeDtypeStruct((tokens, width), jnp.float32)
    return pl.pallas_call(
        lookup_kernel,
        out_shape=(shape, shape),
        grid=(tokens // 256,),
        in_specs=[column, column, pl.BlockSpec(tables.shape, lambda i: (0, 0, 0))],
        out_specs=(out, out),
        compiler_params=pltpu.CompilerParams(vmem_limit_bytes=VMEM_LIMIT),
        name="layout_lookup",
    )(mine, other, tables)


def embed_kernel(place_ref, column_ref, arrived_ref, own_ref, got_ref, half_ref, project_ref,
                 gain_ref, weight_ref, raw_ref, packed_ref, normed_ref, out_ref):
    rows, slots = raw_ref.shape[0], arrived_ref.shape[0]
    pick = as_bf16(iota((rows, slots), 0) + pl.program_id(0) * rows == place_ref[0:1, :])
    raw = dot_nn(pick, arrived_ref[...])
    narrow = raw.astype(jnp.bfloat16)
    raw_ref[...] = narrow
    projected = dot_nn(narrow, project_ref[...])
    first = half_ref[0:1, 0:1] == 0
    own, got = own_ref[...], got_ref[...]
    layout = jnp.concatenate([jnp.where(first, own, got), jnp.where(first, got, own)], axis=1)
    embedded = jnp.where(column_ref[:, 0:1] == 2, raw, projected) + layout
    packed_ref[...] = embedded.astype(jnp.bfloat16)
    packed = packed_ref[...].astype(jnp.float32)
    scale = lax.rsqrt(jnp.mean(packed * packed, axis=-1, keepdims=True) + EPSILON)
    normed = (packed * scale * gain_ref[0:1, :].astype(jnp.float32)).astype(jnp.bfloat16)
    normed_ref[...] = normed
    for part in range(3):
        out_ref[part] = dot_nn(normed, weight_ref[part]).astype(jnp.bfloat16)


def embed(places, column, arrived, own, got, half, matrices, gains, tokens):
    width = arrived.shape[1]
    rows = 256
    half_width = own.shape[1]
    wide = pl.BlockSpec((rows, width), lambda i: (i, 0))
    out = jax.ShapeDtypeStruct((tokens, width), jnp.bfloat16)
    return pl.pallas_call(
        embed_kernel,
        out_shape=(out, out, out, jax.ShapeDtypeStruct((3, tokens, width), jnp.bfloat16)),
        grid=(tokens // rows,),
        in_specs=[
            pl.BlockSpec(places.shape, lambda i: (0, 0)),
            pl.BlockSpec((rows, 8), lambda i: (i, 0)),
            pl.BlockSpec(arrived.shape, lambda i: (0, 0)),
            pl.BlockSpec((rows, half_width), lambda i: (i, 0)),
            pl.BlockSpec((rows, half_width), lambda i: (i, 0)),
            pl.BlockSpec((8, 128), lambda i: (0, 0)),
            pl.BlockSpec((None, width, width), lambda i: (3, 0, 0)),
            pl.BlockSpec((1, width), lambda i: (0, 0)),
            pl.BlockSpec((3, width, width), lambda i: (0, 0, 0)),
        ],
        out_specs=(wide, wide, wide, pl.BlockSpec((3, rows, width), lambda i: (0, i, 0))),
        compiler_params=pltpu.CompilerParams(vmem_limit_bytes=VMEM_LIMIT),
        name="embed",
    )(places, column, arrived, own, got, half, matrices, gains, matrices)


def input_grad_kernel(packed_ref, upper_ref, q_ref, k_ref, v_ref, weight_ref, gain_ref,
                      out_ref, sum_ref):
    total = dot_nt(q_ref[...], weight_ref[0])
    total = total + dot_nt(k_ref[...], weight_ref[1])
    total = total + dot_nt(v_ref[...], weight_ref[2])
    packed = packed_ref[...].astype(jnp.float32)
    scale = lax.rsqrt(jnp.mean(packed * packed, axis=-1, keepdims=True) + EPSILON)
    unit = packed * scale
    back = total * gain_ref[0:1, :].astype(jnp.float32)
    back = scale * (back - unit * jnp.mean(back * unit, axis=-1, keepdims=True))
    out_ref[...] = (back + upper_ref[...]).astype(jnp.bfloat16)

    @pl.when(pl.program_id(0) == 0)
    def _():
        sum_ref[...] = jnp.zeros_like(sum_ref)

    sum_ref[0:1, :] += jnp.sum(total * unit, axis=0, keepdims=True)


def input_grad(packed, upper, query, keys, values, matrices, gains):
    tokens, width = packed.shape
    rows = 256
    wide = pl.BlockSpec((rows, width), lambda i: (i, 0))
    return pl.pallas_call(
        input_grad_kernel,
        out_shape=(
            jax.ShapeDtypeStruct((tokens, width), jnp.bfloat16),
            jax.ShapeDtypeStruct((8, width), jnp.float32),
        ),
        grid=(tokens // rows,),
        in_specs=[
            wide, wide, wide, wide, wide,
            pl.BlockSpec((3, width, width), lambda i: (0, 0, 0)),
            pl.BlockSpec((1, width), lambda i: (0, 0)),
        ],
        out_specs=(wide, pl.BlockSpec((8, width), lambda i: (0, 0))),
        compiler_params=pltpu.CompilerParams(vmem_limit_bytes=VMEM_LIMIT),
        name="input_grad",
    )(packed, upper, query, keys, values, matrices, gains)


def return_kernel(place_ref, rows_ref, out_ref):
    pick = as_bf16(iota((out_ref.shape[0], rows_ref.shape[0]), 1) == place_ref[...])
    out_ref[...] = dot_nn(pick, rows_ref[...]).astype(jnp.bfloat16)


def return_rows(places, rows):
    slots = places.shape[0]
    tokens, width = rows.shape
    return pl.pallas_call(
        return_kernel,
        out_shape=jax.ShapeDtypeStruct((slots, width), jnp.bfloat16),
        grid=(slots // 512,),
        in_specs=[
            pl.BlockSpec((512, 1), lambda i: (i, 0)),
            pl.BlockSpec((tokens, width), lambda i: (0, 0)),
        ],
        out_specs=pl.BlockSpec((512, width), lambda i: (i, 0)),
        compiler_params=pltpu.CompilerParams(vmem_limit_bytes=VMEM_LIMIT),
        name="return_rows",
    )(places, rows)


def layout_grad_kernel(mine_ref, other_ref, first_ref, second_ref, out_ref):
    table = pl.program_id(0)
    shards, rows, width = out_ref.shape
    entries = shards * rows
    total = jnp.zeros((entries, width), jnp.float32)
    for coords, grads in ((mine_ref, first_ref), (other_ref, second_ref)):
        tokens = grads.shape[0]
        key = coords[pl.ds(table + 1, 1), :]
        pick = as_bf16(iota((entries, tokens), 0) + pl.program_id(1) * entries == key)
        total = total + dot_nn(pick, grads[...])
    out_ref[...] = total.astype(jnp.bfloat16).reshape(shards, rows, width)


def layout_grad(mine, other, first, second, shards, rows):
    tokens, width = first.shape
    step = max(1, min(shards, 512 // rows))
    across = pl.BlockSpec((8, tokens), lambda t, i: (0, 0))
    whole = pl.BlockSpec((tokens, width), lambda t, i: (0, 0))
    return pl.pallas_call(
        layout_grad_kernel,
        out_shape=jax.ShapeDtypeStruct((shards, 4, rows, width), jnp.bfloat16),
        grid=(4, shards // step),
        in_specs=[across, across, whole, whole],
        out_specs=pl.BlockSpec((step, None, rows, width), lambda t, i: (i, t, 0, 0)),
        compiler_params=pltpu.CompilerParams(vmem_limit_bytes=VMEM_LIMIT),
        name="layout_grad",
    )(mine, other, first, second)


def patch_kernel(key_ref, rows_ref, weight_ref, grad_ref):
    patches, slots = grad_ref.shape[0], rows_ref.shape[0]
    pick = as_bf16(iota((patches, slots), 0) == key_ref[...])
    projected = dot_nn(pick, rows_ref[...]).astype(jnp.bfloat16)
    grad_ref[...] = dot_nt(projected, weight_ref[...])


def patch_grads(keys, rows, matrices, patches):
    width = rows.shape[1]
    return pl.pallas_call(
        patch_kernel,
        out_shape=jax.ShapeDtypeStruct((patches, width), jnp.float32),
        grid=(1,),
        in_specs=[
            pl.BlockSpec(keys.shape, lambda i: (0, 0)),
            pl.BlockSpec(rows.shape, lambda i: (0, 0)),
            pl.BlockSpec((None, width, width), lambda i: (3, 0, 0)),
        ],
        out_specs=pl.BlockSpec((patches, width), lambda i: (0, 0)),
        compiler_params=pltpu.CompilerParams(vmem_limit_bytes=VMEM_LIMIT),
        name="patch_grads",
    )(keys, rows, matrices)


def text_kernel(key_ref, rows_ref, out_ref):
    size = out_ref.shape[0]
    tokens = rows_ref.shape[0]
    pick = as_bf16(iota((size, tokens), 0) + pl.program_id(0) * size == key_ref[...])
    out_ref[...] = dot_nn(pick, rows_ref[...])


def text_grads(keys, rows, entries):
    tokens, width = rows.shape
    size = 512
    return pl.pallas_call(
        text_kernel,
        out_shape=jax.ShapeDtypeStruct((entries, width), jnp.float32),
        grid=(pl.cdiv(entries, size),),
        in_specs=[
            pl.BlockSpec((1, tokens), lambda i: (0, 0)),
            pl.BlockSpec((tokens, width), lambda i: (0, 0)),
        ],
        out_specs=pl.BlockSpec((size, width), lambda i: (i, 0)),
        compiler_params=pltpu.CompilerParams(vmem_limit_bytes=VMEM_LIMIT),
        name="text_grads",
    )(keys, rows)


def swap(value, axis, bit):
    count = lax.axis_size(axis)
    return lax.ppermute(value, axis, [(i, i ^ bit) for i in range(count)])


def bit_of(axis, bit):
    return jnp.bitwise_and(lax.axis_index(axis), bit) != 0


def both(value, place, axis, bit):
    got = swap(value, axis, bit)
    second = bit_of(axis, bit)
    return jnp.stack(
        [jnp.where(second, got, value), jnp.where(second, value, got)], axis=place
    )


def gather_dp(value):
    count = lax.axis_size("dp")
    shape = value.shape
    bit = count // 2
    step = 0
    while bit >= 1:
        value = both(value, step, "dp", bit)
        step += 1
        bit //= 2
    return value.reshape((count,) + shape)


def gather_stream(value):
    value = both(value, 0, "stream", 2)
    return both(value, 1, "stream", 1).reshape((4,) + value.shape[1:])


def halve(value, place, axis, bit):
    mine = bit_of(axis, bit).astype(jnp.int32)
    keep = lax.dynamic_index_in_dim(value, mine, place, keepdims=False)
    give = lax.dynamic_index_in_dim(value, 1 - mine, place, keepdims=False)
    got = swap(give, axis, bit)
    return (keep.astype(jnp.float32) + got.astype(jnp.float32)).astype(jnp.bfloat16)


def scatter_dp(value):
    count = lax.axis_size("dp")
    rest = value.shape[1:]
    bit = 1
    while bit < count:
        value = value.reshape((-1, 2) + rest)
        value = halve(value, 1, "dp", bit)
        bit *= 2
    return value.reshape(rest)


def contract_rows(left, right):
    return lax.dot_general(
        left, right, (((0,), (0,)), ((), ())), preferred_element_type=jnp.float32
    )


def times_transpose(left, right):
    return lax.dot_general(
        left, right, (((1,), (1,)), ((), ())), preferred_element_type=jnp.float32
    )


def norm_backward(grad_normed, unit, scale, gain):
    grad_unit = grad_normed * gain
    grad_input = scale * (grad_unit - unit * jnp.mean(grad_unit * unit, axis=-1, keepdims=True))
    return (grad_input, jnp.sum(grad_normed * unit, axis=0))


def shards(
    patches,
    src_kind,
    src_index,
    layout_coords,
    placing,
    segments,
    text_table,
    layout_tables,
    patch_proj,
    rel_table,
    norm_gains,
    w_qkv,
    w_attn_out,
    w_ff_in,
    w_ff_out,
    out_grad,
):
    data_count = lax.axis_size("dp")
    tokens = placing.shape[0]
    capacity = 2 * tokens // data_count
    width = text_table.shape[1]
    half_width = width // 2
    texts = tokens - patches.shape[0]
    shift = tokens.bit_length() - 1
    shard_rows = w_attn_out.shape[0]
    layout_rows = layout_tables.shape[1]
    stream = lax.axis_index("stream")
    core = jnp.bitwise_and(stream, 1)
    side = jnp.right_shift(stream, 1)
    gain_count = norm_gains.shape[1]

    in_quarter = lax.dynamic_index_in_dim(
        w_ff_in.reshape(shard_rows, 4, -1), stream, 1, keepdims=False
    )
    down_quarter = lax.dynamic_index_in_dim(
        w_ff_out.reshape(4, -1, width), stream, 0, keepdims=False
    )
    quarters_in = lax.all_gather(in_quarter, ("dp", "stream"), axis=0)
    full_down = lax.all_gather(down_quarter, ("dp", "stream"), axis=0, tiled=True)
    full_in = (
        quarters_in.reshape(data_count, 4, shard_rows, -1)
        .transpose(0, 2, 1, 3)
        .reshape(width, -1)
    )

    slot, meta, text_index = find_slots(
        data_count, capacity, shift, placing, src_kind, src_index, layout_coords, texts
    )
    arrived_meta = lax.all_to_all(
        meta.reshape(16, data_count, capacity), "dp", split_axis=1, concat_axis=1, tiled=True
    ).reshape(16, -1)
    is_text = src_kind == 1
    raw_rows = jnp.where(
        is_text[:, None],
        jnp.take(text_table, jnp.where(is_text, src_index, 0), axis=0),
        jnp.take(patches, jnp.where(is_text, 0, src_index), axis=0),
    )
    send_rows = pick_rows(slot, raw_rows, data_count * capacity, "pack")
    arrived = lax.all_to_all(
        send_rows.reshape(data_count, capacity, width), "dp", split_axis=0, concat_axis=0, tiled=True
    ).reshape(-1, width)

    square = jnp.concatenate([w_qkv, patch_proj[None]], axis=0)
    one_square = gather_dp(lax.dynamic_index_in_dim(square, stream, 0, keepdims=False))
    matrices = gather_stream(one_square).reshape(4, width, width)

    def own_half(value):
        return lax.dynamic_slice_in_dim(value, core * half_width, half_width, axis=-1)

    layout_part = own_half(
        lax.dynamic_slice_in_dim(layout_tables, side * 2, 2, axis=0)
    ).reshape(-1, half_width)
    mix_part = own_half(
        lax.dynamic_slice_in_dim(w_attn_out, side * (shard_rows // 2), shard_rows // 2, axis=0)
    )
    gain_part = jnp.pad(norm_gains, ((0, 14), (0, half_width - gain_count)))
    mix_rows = mix_part.shape[0]
    columns = gather_dp(jnp.concatenate([layout_part, mix_part, gain_part], axis=0))
    columns = both(columns, 1, "stream", 2)
    table_rows = layout_part.shape[0]
    tables = (
        columns[:, :, :table_rows]
        .reshape(data_count, 2, 2, layout_rows, half_width)
        .transpose(1, 2, 0, 3, 4)
        .reshape(4, -1, half_width)
    )
    mix_half = columns[:, :, table_rows : table_rows + mix_rows].reshape(width, half_width)
    full_mix = both(mix_half, 1, "stream", 1).reshape(width, width)
    gains = columns[:, 0, table_rows + mix_rows :][:, :2, :gain_count]
    gains = gains.transpose(1, 0, 2).reshape(2, width)

    column, across, place = place_meta(arrived_meta, tokens)
    column_other, across_other = swap(column, "stream", 1), swap(across, "stream", 1)
    own_sum, other_sum = layout_lookup(column, column_other, tables)
    got_sum = swap(other_sum, "stream", 1)

    half_index = jnp.broadcast_to(core, (8, 128)).astype(jnp.int32)
    raw, packed, normed_one, projections = embed(
        place, column, arrived, own_sum, got_sum, half_index, matrices, gains[:1], tokens
    )
    aug_q, aug_k, table, mirrored = prepare(segments, rel_table)
    mixed, lse = attention_forward(segments, projections, aug_q, aug_k, table)

    gain_two = gains[1].astype(jnp.float32)
    packed_wide = packed.astype(jnp.float32)
    attended = packed_wide + jnp.dot(mixed, full_mix, preferred_element_type=jnp.float32)
    scale_two = lax.rsqrt(jnp.mean(attended * attended, axis=-1, keepdims=True) + EPSILON)
    unit_two = attended * scale_two
    normed_two = (unit_two * gain_two).astype(jnp.bfloat16)
    hidden = jnp.dot(normed_two, full_in, preferred_element_type=jnp.float32)
    active = jax.nn.gelu(hidden, approximate=True).astype(jnp.bfloat16)
    result = (attended + jnp.dot(active, full_down, preferred_element_type=jnp.float32)).astype(
        jnp.bfloat16
    )

    grad_active = times_transpose(out_grad, full_down)
    _, gelu_pull = jax.vjp(partial(jax.nn.gelu, approximate=True), hidden)
    grad_hidden = gelu_pull(grad_active)[0].astype(jnp.bfloat16)
    grad_normed_two = times_transpose(grad_hidden, full_in)
    grad_attended, grad_gain_two = norm_backward(grad_normed_two, unit_two, scale_two, gain_two)
    grad_attended = grad_attended + out_grad.astype(jnp.float32)
    grad_branch = grad_attended.astype(jnp.bfloat16)
    grad_mixed = times_transpose(grad_branch, full_mix).astype(jnp.bfloat16)

    grad_down = contract_rows(active, out_grad).astype(jnp.bfloat16)
    grad_in = contract_rows(normed_two, grad_hidden).astype(jnp.bfloat16)
    grad_mix = contract_rows(mixed, grad_branch).astype(jnp.bfloat16)
    down_parts = grad_down.reshape(data_count, 2, 2, shard_rows, width)
    in_parts = grad_in.reshape(data_count, shard_rows, 2, 2, width).transpose(0, 2, 3, 1, 4)

    def reduce_quarters(value):
        value = halve(value, 2, "stream", 1)
        value = halve(value, 1, "stream", 2)
        return gather_stream(scatter_dp(value))

    shard_down = reduce_quarters(down_parts)
    shard_in = reduce_quarters(in_parts)

    grad_query, grad_keys, grad_values, grad_rel = attention_backward(
        segments, projections, mixed, grad_mixed, lse, aug_q, aug_k, mirrored
    )
    grad_packed, gain_one_sum = input_grad(
        packed, grad_attended, grad_query, grad_keys, grad_values, matrices, gains[:1]
    )
    returned = return_rows(place[:1].reshape(-1, 1), grad_packed)
    came_back = lax.all_to_all(
        returned.reshape(data_count, capacity, width), "dp", split_axis=0, concat_axis=0, tiled=True
    ).reshape(-1, width)

    own_columns = own_half(grad_packed)
    other_columns = swap(
        lax.dynamic_slice_in_dim(grad_packed, (1 - core) * half_width, half_width, axis=1),
        "stream", 1,
    )
    table_grads = layout_grad(
        across, across_other, own_columns, other_columns, data_count, layout_rows
    ).reshape(data_count, 2, table_rows, half_width)
    mix_grads = halve(
        grad_mix.reshape(data_count, 2, shard_rows // 2, 2, half_width), 3, "stream", 1
    )
    column_grads = jnp.concatenate([table_grads, mix_grads], axis=2)
    column_grads = scatter_dp(halve(column_grads, 1, "stream", 2))
    column_grads = gather_stream(column_grads).reshape(2, 2, -1, half_width)
    shard_layout = (
        column_grads[:, :, :table_rows]
        .reshape(2, 2, 2, layout_rows, half_width)
        .transpose(0, 2, 3, 1, 4)
        .reshape(4, layout_rows, width)
    )
    shard_mix = (
        column_grads[:, :, table_rows:].transpose(0, 2, 1, 3).reshape(shard_rows, width)
    )

    visual_rows = jnp.where(column[:, :1] == 1, raw, jnp.zeros((), jnp.bfloat16))
    square_grads = jnp.stack(
        [
            contract_rows(normed_one, grad_query).astype(jnp.bfloat16),
            contract_rows(normed_one, grad_keys).astype(jnp.bfloat16),
            contract_rows(normed_one, grad_values).astype(jnp.bfloat16),
            contract_rows(visual_rows, grad_packed).astype(jnp.bfloat16),
        ]
    ).reshape(2, 2, data_count, shard_rows, width)
    square_grads = halve(square_grads, 1, "stream", 1)
    square_grads = halve(square_grads, 0, "stream", 2)
    shard_square = gather_stream(scatter_dp(square_grads))

    slot_kind = meta[:1].astype(jnp.float32)
    wide_meta = meta.astype(jnp.float32)
    slot_index = (wide_meta[11:12] * 16.0 + wide_meta[12:13]).astype(jnp.int32)
    slot_text = (wide_meta[13:14] * 4.0 + wide_meta[14:15]).astype(jnp.int32)
    text_keys = jnp.where(slot_kind == 2.0, slot_text, -1)
    patch_keys = jnp.where(slot_kind == 1.0, slot_index, -1)
    text_rows = gather_stream(pick_rows(text_keys, came_back, texts, "unpack_text"))
    all_index = gather_stream(text_index)[:, 0].reshape(1, -1)
    grad_text = text_grads(all_index, text_rows.reshape(-1, width), text_table.shape[0])
    grad_patches = patch_grads(patch_keys, came_back, matrices, patches.shape[0])

    rel = rel_gradient(grad_rel, rel_table.shape[0])
    small = jnp.concatenate(
        [gain_one_sum[0].reshape(-1), grad_gain_two.reshape(-1), rel.reshape(-1)]
    )
    small = lax.psum(small, ("dp", "stream"))
    grad_gains = lax.dynamic_slice_in_dim(
        small[: 2 * width].reshape(2, width), lax.axis_index("dp") * gain_count, gain_count, axis=1
    )
    wide = jnp.float32
    return (
        result,
        grad_patches,
        grad_text,
        shard_layout.astype(wide),
        shard_square[3].astype(wide),
        small[2 * width :].reshape(rel.shape),
        grad_gains,
        shard_square[:3].astype(wide),
        shard_mix.astype(wide),
        shard_in.transpose(1, 0, 2).reshape(shard_rows, -1).astype(wide),
        shard_down.reshape(-1, width).astype(wide),
    )


def solution(mesh):
    return jax.shard_map(
        shards,
        mesh=mesh,
        in_specs=(
            P(("dp", "stream"), None),
            P(("dp", "stream")),
            P(("dp", "stream")),
            P(None, ("dp", "stream")),
            P(("dp", "stream")),
            P(("dp", "stream"), None),
            P("dp", None),
            P(None, "dp", None),
            P("dp", None),
            P(),
            P(None, "dp"),
            P(None, "dp", None),
            P("dp", None),
            P("dp", None),
            P("dp", None),
            P(("dp", "stream"), None),
        ),
        out_specs=(
            P(("dp", "stream"), None),
            P(("dp", "stream"), None),
            P("dp", None),
            P(None, "dp", None),
            P("dp", None),
            P(),
            P(None, "dp"),
            P(None, "dp", None),
            P("dp", None),
            P("dp", None),
            P("dp", None),
        ),
        check_vma=False,
    )
```

```python
from functools import partial
import math

import jax
import jax.numpy as jnp
from jax import lax
from jax.experimental import pallas as pl
from jax.experimental.pallas import tpu as pltpu
from jax.sharding import PartitionSpec as P

EPSILON = 1e-06
THRESHOLDS = (12, 16, 23, 32, 46, 64, 91)
BLK = 256
NEG = -1e30
RATE = math.sqrt(2.0 / math.pi)
VMEM_LIMIT = 56 * 2**20
SMALL = pl.CostEstimate(flops=1, bytes_accessed=1, transcendentals=0)


class Line:
    def __init__(self):
        self.last = jnp.zeros((8, 128), jnp.float32)


def launch(line, kernel, operands, in_specs, out_shape, out_specs, grid, name, scalars=(), scratch=()):
    held, given, made = len(scalars), len(operands), len(out_shape)
    token = pl.BlockSpec((8, 128), lambda *_: (0, 0))

    def body(*refs):
        outs = held + given + 1
        refs[outs + made][...] = refs[outs - 1][...]
        kernel(*refs[: outs - 1], *refs[outs : outs + made], *refs[outs + made + 1 :])

    out_shape = [jax.ShapeDtypeStruct(value.shape, value.dtype) for value in out_shape]
    results = pl.pallas_call(
        body,
        out_shape=tuple(out_shape) + (jax.ShapeDtypeStruct((8, 128), jnp.float32),),
        grid_spec=pltpu.PrefetchScalarGridSpec(
            num_scalar_prefetch=held,
            grid=grid,
            in_specs=list(in_specs) + [token],
            out_specs=tuple(out_specs) + (token,),
            scratch_shapes=list(scratch),
        ),
        compiler_params=pltpu.CompilerParams(vmem_limit_bytes=VMEM_LIMIT),
        cost_estimate=SMALL,
        name=name,
    )(*scalars, *operands, line.last)
    line.last = results[-1]
    return results[:-1]


def fixed(value):
    return pl.BlockSpec(value.shape, lambda *_: (0,) * len(value.shape))


def bf16(*shape):
    return jax.ShapeDtypeStruct(shape, jnp.bfloat16)


def f32(*shape):
    return jax.ShapeDtypeStruct(shape, jnp.float32)


def i32(*shape):
    return jax.ShapeDtypeStruct(shape, jnp.int32)


def bucket_of(relative):
    magnitude = jnp.abs(relative)
    beyond = 8 + sum(((magnitude >= threshold).astype(jnp.int32) for threshold in THRESHOLDS))
    return jnp.where(relative > 0, 16, 0).astype(jnp.int32) + jnp.where(
        magnitude < 8, magnitude, beyond
    )


def dot_nt(a, b):
    return lax.dot_general(a, b, (((1,), (1,)), ((), ())), preferred_element_type=jnp.float32)

def dot_nn(a, b):
    return lax.dot_general(a, b, (((1,), (0,)), ((), ())), preferred_element_type=jnp.float32)

def dot_tn(a, b):
    return lax.dot_general(a, b, (((0,), (0,)), ((), ())), preferred_element_type=jnp.float32)


def pieces(value):
    one = value.astype(jnp.bfloat16)
    rest = value - one.astype(jnp.float32)
    two = rest.astype(jnp.bfloat16)
    three = (rest - two.astype(jnp.float32)).astype(jnp.bfloat16)
    return one, two, three

def put_pieces(base, value, lane):
    one, two, three = pieces(value)
    base = jnp.where(jnp.logical_or(lane == 8, lane == 72), one, base)
    base = jnp.where(jnp.logical_or(lane == 9, lane == 73), two, base)
    return jnp.where(jnp.logical_or(lane == 10, lane == 74), three, base)

def diagonal_sums(block):
    wide = jnp.concatenate([block, jnp.zeros_like(block)], axis=1)
    total = wide[:128]
    for start in range(128, BLK, 128):
        total = total + pltpu.roll(wide[start : start + 128], 2 * BLK - start, 1)
    eight = total[:8]
    for start in range(8, 128, 8):
        eight = eight + pltpu.roll(total[start : start + 8], 2 * BLK - start, 1)
    one = eight[:1]
    for row in range(1, 8):
        one = one + pltpu.roll(eight[row : row + 1], 2 * BLK - row, 1)
    return one


def window_of(block, count):
    low = max(0, block * BLK - 2 * BLK + 1) // BLK
    high = min(count - 1, (block * BLK + BLK - 1 + 2 * BLK - 1) // BLK)
    return low, high + 1

def fill_strip(strip, table, slot, count):
    middle = (count - 1) * BLK
    for step in (-1, 0, 1):
        window = table[slot : slot + 1, BLK * step + BLK : BLK * step + 3 * BLK]
        spread = jnp.broadcast_to(window, (BLK, 2 * BLK))
        start = middle + step * BLK
        strip[slot, :, start : start + BLK] = pltpu.roll(spread, 0, 1, stride=1, stride_axis=0)[:, BLK:]
    low = jnp.broadcast_to(table[slot : slot + 1, 0:1], (BLK, middle - BLK))
    high = jnp.broadcast_to(table[slot : slot + 1, 4 * BLK - 1 : 4 * BLK], (BLK, middle - BLK))
    strip[slot, :, 0 : middle - BLK] = low
    strip[slot, :, middle + 2 * BLK :] = high

def forward_kernel(q_ref, k_ref, v_ref, aug_q, aug_k, table, out_ref, lse_ref, strip, ka, va):
    length = q_ref.shape[0]
    count = length // BLK
    lane = lax.broadcasted_iota(jnp.int32, (1, 128), 1)
    left = lane < 64
    for h in range(2):
        fill_strip(strip, table, h, count)
        mine = left if h == 0 else jnp.logical_not(left)
        ka[h] = jnp.where(mine, k_ref[...], aug_k[...])
        va[h] = jnp.where(mine, v_ref[...], aug_k[...])
    for qb in range(count):
        rows = slice(qb * BLK, qb * BLK + BLK)
        low, high = window_of(qb, count)
        keys = slice(low * BLK, high * BLK)
        offset = (count - 1 - qb) * BLK
        query = q_ref[rows, :] * jnp.bfloat16(0.125)
        outs = []
        lses = []
        for h in range(2):
            qa = jnp.where(left if h == 0 else jnp.logical_not(left), query, aug_q[rows, :])
            s = dot_nt(qa, ka[h, keys, :]) + strip[h, :, offset + low * BLK : offset + high * BLK]
            peak = jnp.max(s, axis=1, keepdims=True)
            p = jnp.exp(s - peak).astype(jnp.bfloat16)
            acc = dot_nn(p, va[h, keys, :])
            mark = 72 if h == 0 else 8
            total = acc[:, mark : mark + 1]
            outs.append(acc / total)
            lses.append(jnp.broadcast_to(peak + jnp.log(total), (BLK, 128)))
        out_ref[rows, :] = jnp.where(left, outs[0], outs[1]).astype(jnp.bfloat16)
        lse_ref[rows, :] = jnp.where(left, lses[0], lses[1])

def backward_kernel(
    q_ref, k_ref, v_ref, mixed_ref, grad_ref, lse_ref, aug_q, aug_k, table,
    grads_ref, rel_ref,
    strip, rel, ka, va, qa, ga, dq_acc,
):
    length = q_ref.shape[0]
    count = length // BLK
    middle = (count - 1) * BLK
    lane = lax.broadcasted_iota(jnp.int32, (1, 128), 1)
    left = lane < 64
    rel[...] = jnp.zeros_like(rel)
    dq_acc[...] = jnp.zeros_like(dq_acc)
    inner = mixed_ref[...].astype(jnp.float32) * grad_ref[...].astype(jnp.float32)
    query = q_ref[...] * jnp.bfloat16(0.125)
    for h in range(2):
        fill_strip(strip, table, h, count)
        mine = left if h == 0 else jnp.logical_not(left)
        ka[h] = jnp.where(mine, k_ref[...], aug_k[...])
        va[h] = jnp.where(mine, v_ref[...], aug_k[...])
        at = 0 if h == 0 else 64
        qa[h] = jnp.where(mine, query, put_pieces(aug_q[...], -lse_ref[:, at : at + 1], lane))
        delta = jnp.sum(jnp.where(mine, inner, 0.0), axis=1, keepdims=True)
        spare = put_pieces(jnp.zeros((length, 128), jnp.bfloat16), -delta, lane)
        ga[h] = jnp.where(mine, grad_ref[...], spare)
    for kb in range(count):
        keys = slice(kb * BLK, kb * BLK + BLK)
        low, high = window_of(kb, count)
        rows = slice(low * BLK, high * BLK)
        offset = middle - kb * BLK
        cut = slice(offset + low * BLK, offset + high * BLK)
        dks, dvs = [], []
        for h in range(2):
            s = dot_nt(ka[h, keys, :], qa[h, rows, :]) + strip[h, :, cut]
            p = jnp.exp(s)
            ds = p * dot_nt(va[h, keys, :], ga[h, rows, :])
            rel[h, :, cut] += ds
            p = p.astype(jnp.bfloat16)
            ds = ds.astype(jnp.bfloat16)
            dvs.append(dot_nn(p, ga[h, rows, :]))
            dks.append(dot_nn(ds, qa[h, rows, :]))
            dq_acc[h, :, rows] += dot_tn(ka[h, keys, :], ds)
        grads_ref[1, keys, :] = jnp.where(left, dks[0], dks[1]).astype(jnp.bfloat16)
        grads_ref[2, keys, :] = jnp.where(left, dvs[0], dvs[1]).astype(jnp.bfloat16)
    row = lax.broadcasted_iota(jnp.int32, (128, 1), 0)
    dq = jnp.where(row < 64, dq_acc[0], dq_acc[1]).T
    grads_ref[0] = (dq * 0.125).astype(jnp.bfloat16)
    for h in range(2):
        out = []
        for place in range(5):
            start = middle + (2 - place) * BLK
            if place == 0:
                far = rel[h, :, middle + 2 * BLK :]
                summed = jnp.sum(jnp.sum(far, axis=0, keepdims=True).reshape(-1, BLK), axis=0, keepdims=True)
                out.append(jnp.concatenate([summed, jnp.zeros_like(summed)], axis=1))
            elif place == 4:
                far = rel[h, :, : middle - BLK]
                summed = jnp.sum(jnp.sum(far, axis=0, keepdims=True).reshape(-1, BLK), axis=0, keepdims=True)
                out.append(jnp.concatenate([summed, jnp.zeros_like(summed)], axis=1))
            else:
                out.append(diagonal_sums(rel[h, :, start : start + BLK]))
        rel_ref[h] = jnp.concatenate(out + [jnp.zeros((3, 2 * BLK), jnp.float32)], axis=0)


def attention_forward(line, qkv, aug_q, aug_k, table):
    _, length, width = qkv.shape
    col = pl.BlockSpec((length, 128), lambda p: (0, p))
    buf = pltpu.VMEM((2, length, 128), jnp.bfloat16)
    return launch(
        line, forward_kernel, (qkv, qkv, qkv, aug_q, aug_k, table),
        [
            pl.BlockSpec((None, length, 128), lambda p: (0, 0, p)),
            pl.BlockSpec((None, length, 128), lambda p: (1, 0, p)),
            pl.BlockSpec((None, length, 128), lambda p: (2, 0, p)),
            fixed(aug_q), fixed(aug_k),
            pl.BlockSpec((None, 2, table.shape[2]), lambda p: (p, 0, 0)),
        ],
        (bf16(length, width), f32(length, width)), (col, col), (width // 128,),
        "attention_forward",
        scratch=[pltpu.VMEM((2, BLK, 2 * length - BLK), jnp.float32), buf, buf],
    )


def attention_backward(line, qkv, mixed, grad_mixed, lse, aug_q, aug_k, table):
    _, length, width = qkv.shape
    col = pl.BlockSpec((length, 128), lambda p: (0, p))
    buf = pltpu.VMEM((2, length, 128), jnp.bfloat16)
    strip = pltpu.VMEM((2, BLK, 2 * length - BLK), jnp.float32)
    return launch(
        line, backward_kernel,
        (qkv, qkv, qkv, mixed, grad_mixed, lse, aug_q, aug_k, table),
        [
            pl.BlockSpec((None, length, 128), lambda p: (0, 0, p)),
            pl.BlockSpec((None, length, 128), lambda p: (1, 0, p)),
            pl.BlockSpec((None, length, 128), lambda p: (2, 0, p)),
            col, col, col, fixed(aug_q), fixed(aug_k),
            pl.BlockSpec((None, 2, table.shape[2]), lambda p: (p, 0, 0)),
        ],
        (bf16(3, length, width), f32(width // 64, 8, 2 * BLK)),
        (
            pl.BlockSpec((3, length, 128), lambda p: (0, 0, p)),
            pl.BlockSpec((2, 8, 2 * BLK), lambda p: (p, 0, 0)),
        ),
        (width // 128,), "attention_backward",
        scratch=[strip, strip, buf, buf, buf, buf, pltpu.VMEM((2, 128, length), jnp.float32)],
    )


def bucket_choice(offsets, count):
    return (bucket_of(offsets)[:, None] == jnp.arange(count, dtype=jnp.int32)[None, :]).astype(jnp.float32)

def prepare(segments, rel_table):
    heads = rel_table.shape[1]
    offsets = jnp.arange(4 * BLK, dtype=jnp.int32) - 2 * BLK
    tables = []
    for sign in (1, -1):
        choose = bucket_choice(sign * offsets, rel_table.shape[0])
        table = lax.dot_general(rel_table, choose, (((0,), (1,)), ((), ())), precision=lax.Precision.HIGHEST)
        tables.append(table.reshape(heads // 2, 2, 4 * BLK))
    lane = (jnp.arange(128, dtype=jnp.int32) % 64)[None, :]
    row = segments.reshape(-1)[:, None]
    same = lane == row
    aug_q = jnp.where(jnp.logical_or(same, lane >= 8), 0.0, NEG).astype(jnp.bfloat16)
    aug_k = jnp.where(jnp.logical_or(same, jnp.logical_and(lane >= 8, lane < 11)), 1.0, 0.0).astype(jnp.bfloat16)
    return aug_q, aug_k, tables[0], tables[1]

def rel_gradient(rel, count):
    lane = jnp.arange(2 * BLK, dtype=jnp.int32)
    parts = []
    for place in range(5):
        if place == 0:
            offset = jnp.full((2 * BLK,), -600, jnp.int32)
        elif place == 4:
            offset = jnp.full((2 * BLK,), 600, jnp.int32)
        else:
            offset = BLK * (place - 2) - jnp.where(lane < BLK, lane, lane - 2 * BLK)
        parts.append(bucket_choice(offset, count))
    choose = jnp.concatenate(parts + [jnp.zeros((3 * 2 * BLK, count), jnp.float32)], axis=0)
    flat = rel.reshape(rel.shape[0], -1)
    return lax.dot_general(choose, flat, (((0,), (1,)), ((), ())), precision=lax.Precision.HIGHEST)


def iota(shape, axis):
    return lax.broadcasted_iota(jnp.int32, shape, axis)


def as_bf16(flag):
    return jnp.where(flag, 1.0, 0.0).astype(jnp.bfloat16)


def slots_kernel(owners, capacity, shift, place_ref, kind_ref, index_ref, coords_ref,
                 meta_ref, keys_ref, text_ref):
    tokens = place_ref.shape[1]
    place = place_ref[...]
    text = kind_ref[...] == 1
    owner = jnp.right_shift(place, shift)
    position = jnp.bitwise_and(place, (1 << shift) - 1)
    rows = owners + 16
    row = iota((rows, tokens), 0)
    member = jnp.logical_or(row == owner, jnp.logical_and(row == owners, text))
    upto = as_bf16(iota((tokens, tokens), 0) <= iota((tokens, tokens), 1))
    counts = dot_nn(as_bf16(member), upto)
    rank = jnp.sum(jnp.where(row == owner, counts, 0.0), axis=0, keepdims=True)
    rank = rank.astype(jnp.int32) - 1
    text_rank = jnp.where(text, counts[owners : owners + 1].astype(jnp.int32) - 1, 0)
    slot = owner * capacity + rank
    index = index_ref[...]
    coords = coords_ref[...]
    low = jnp.bitwise_and(coords, 3)
    high = jnp.right_shift(coords, 2)
    meta = jnp.concatenate(
        [
            kind_ref[...] + 1,
            jnp.right_shift(position, 2), jnp.bitwise_and(position, 3),
            high, low,
            jnp.right_shift(index, 4), jnp.bitwise_and(index, 15),
            jnp.right_shift(text_rank, 2), jnp.bitwise_and(text_rank, 3),
            jnp.zeros_like(index),
        ],
        axis=0,
    ).astype(jnp.float32).astype(jnp.bfloat16)
    slots = meta_ref.shape[1]
    for start in range(0, slots, 512):
        pick = as_bf16(iota((512, tokens), 0) + start == slot)
        meta_ref[:, start : start + 512] = dot_nt(meta, pick).astype(jnp.bfloat16)
        down = dot_nt(pick, meta)
        index = down[:, 11:12] * 16.0 + down[:, 12:13]
        rank = down[:, 13:14] * 4.0 + down[:, 14:15] + float(tokens - text_ref.shape[1])
        key = jnp.where(down[:, 0:1] > 1.5, rank, jnp.where(down[:, 0:1] > 0.5, index, -1.0))
        keys_ref[start : start + 512, :] = jnp.broadcast_to(key.astype(jnp.int32), (512, 8))
    texts = text_ref.shape[1]
    chosen = as_bf16(jnp.logical_and(iota((texts, tokens), 0) == text_rank, text))
    found = dot_nt(meta, chosen)
    text_ref[...] = jnp.broadcast_to(
        (found[11:12] * 16.0 + found[12:13]).astype(jnp.int32), text_ref.shape
    )


def find_slots(line, owners, capacity, shift, placing, src_kind, src_index, coords, texts):
    slots = owners * capacity
    operands = (placing.reshape(1, -1), src_kind.reshape(1, -1), src_index.reshape(1, -1), coords)
    shapes = (bf16(16, slots), i32(slots, 8), i32(8, texts))
    return launch(
        line, partial(slots_kernel, owners, capacity, shift), operands,
        [fixed(value) for value in operands], shapes, [fixed(value) for value in shapes], (1,),
        "find_slots",
    )


def unpack_kernel(key_ref, rows_ref, index_ref, out_ref):
    texts, tokens = index_ref.shape[1], rows_ref.shape[1]
    count, width = rows_ref.shape[0], out_ref.shape[1]
    total = None
    small = None
    for d in range(count):
        pick = as_bf16(iota((texts, tokens), 0) == key_ref[d : d + 1, :])
        part = dot_nn(pick, rows_ref[d])
        total = part if total is None else total + part
        part = join_small(rows_ref[d, tokens - 16 :, :])
        small = part if small is None else small + part
    out_ref[:texts, :] = total.astype(jnp.bfloat16)
    index = index_ref[...]
    row = iota((16, texts), 0)
    high = jnp.broadcast_to(jnp.right_shift(index[0:1], 4), (16, texts))
    low = jnp.broadcast_to(jnp.bitwise_and(index[0:1], 15), (16, texts))
    index = jnp.where(row == 0, high, jnp.where(row == 1, low, 0)).astype(jnp.float32)
    index = jnp.concatenate([index, jnp.zeros((16, width - texts), jnp.float32)], axis=1)
    out_ref[texts : texts + 16, :] = index.astype(jnp.bfloat16)
    out_ref[texts + 16 :, :] = split_small(small)


def unpack_text(line, keys, rows, index):
    width = rows.shape[2]
    shape = bf16(index.shape[1] + 32, width)
    return launch(
        line, unpack_kernel, (keys, rows, index), [fixed(keys), fixed(rows), fixed(index)],
        (shape,), (fixed(shape),), (1,), "unpack_text",
    )[0]


def pack_kernel(key_ref, patch_ref, text_ref, *refs):
    out_ref = refs[len(refs) // 2]
    size, patches, texts = out_ref.shape[0], patch_ref.shape[0], text_ref.shape[0]
    key = key_ref[:, 0:1]
    out = dot_nn(as_bf16(iota((size, patches), 1) == key), patch_ref[...])
    out = out + dot_nn(as_bf16(iota((size, texts), 1) + patches == key), text_ref[...])
    out_ref[...] = out.astype(jnp.bfloat16)

    @pl.when(pl.program_id(0) == 0)
    def _():
        for n in range(len(refs) // 2):
            refs[len(refs) // 2 + 1 + n][...] = refs[n][...]


def pack(line, keys, patches, text_rows, later):
    slots = keys.shape[0]
    width = patches.shape[1]
    return launch(
        line, pack_kernel, (keys, patches, text_rows) + later,
        [pl.BlockSpec((512, 8), lambda i: (i, 0)), fixed(patches), fixed(text_rows)]
        + [fixed(value) for value in later],
        (bf16(slots, width),) + later,
        (pl.BlockSpec((512, width), lambda i: (i, 0)),) + tuple(fixed(value) for value in later),
        (slots // 512,), "pack",
    )


def place_kernel(meta_ref, column_ref, row_ref, place_ref):
    slots, tokens = meta_ref.shape[1], row_ref.shape[1]
    meta = meta_ref[...]
    wide = meta.astype(jnp.float32)
    place = (wide[1:2] * 4.0 + wide[2:3]).astype(jnp.int32)
    place = jnp.where(wide[0:1] > 0.5, place, -1)
    place_ref[...] = jnp.broadcast_to(place, place_ref.shape)
    for start in range(0, tokens, 256):
        pick = as_bf16(iota((256, slots), 0) + start == place)
        down = dot_nt(pick, meta)
        values = [down[:, 0:1]] + [down[:, 3 + c : 4 + c] * 4.0 + down[:, 7 + c : 8 + c] for c in range(4)]
        lane = iota((256, 8), 1)
        block = jnp.zeros((256, 8), jnp.float32)
        for c in range(5):
            block = jnp.where(lane == c, values[c], block)
        column_ref[start : start + 256, :] = block.astype(jnp.int32)
        across = dot_nt(meta, pick)
        row_ref[:, start : start + 256] = jnp.concatenate(
            [across[0:1], across[3:7] * 4.0 + across[7:11], jnp.zeros((3, 256), jnp.float32)], axis=0
        ).astype(jnp.int32)


def place_meta(line, meta, tokens):
    shapes = (i32(tokens, 8), i32(8, tokens), i32(8, meta.shape[1]))
    return launch(
        line, place_kernel, (meta,), [fixed(meta)], shapes, [fixed(value) for value in shapes],
        (1,), "place_meta",
    )


def lookup_kernel(rows, fresh, side, mine_ref, other_ref, table_ref, *refs):
    width = table_ref.shape[2]
    outs = refs[-2:]
    entries = table_ref.shape[0] * rows
    for n, coords in enumerate((mine_ref, other_ref)):
        total = jnp.zeros(outs[n].shape, jnp.float32) if fresh else refs[n][...]
        for k in range(2):
            key = jnp.where(side[0] == 0, coords[:, k + 1 : k + 2], coords[:, k + 3 : k + 4])
            pick = as_bf16(iota((total.shape[0], entries), 1) == key)
            table = table_ref[:, k * rows : k * rows + rows, :].reshape(entries, width)
            total = total + dot_nn(pick, table)
        outs[n][...] = total


def layout_lookup(line, side, mine, other, columns, rows, sums=()):
    tokens = mine.shape[0]
    width = columns.shape[2]
    column = pl.BlockSpec((256, 8), lambda i, s: (i, 0))
    out = pl.BlockSpec((256, width), lambda i, s: (i, 0))
    return launch(
        line, partial(lookup_kernel, rows, not sums), (mine, other, columns, *sums),
        [column, column, fixed(columns)] + [out] * len(sums),
        (f32(tokens, width), f32(tokens, width)), (out, out), (tokens // 256,), "layout_lookup",
        scalars=(side,),
    )


def embed_kernel(place_ref, column_ref, arrived_ref, own_ref, got_ref, half_ref, project_ref,
                 gain_ref, weight_ref, visual_ref, packed_ref, normed_ref, out_ref):
    rows, slots = packed_ref.shape[0], arrived_ref.shape[0]
    pick = as_bf16(iota((rows, slots), 0) + pl.program_id(0) * rows == place_ref[0:1, :])
    raw = dot_nn(pick, arrived_ref[...])
    narrow = raw.astype(jnp.bfloat16)
    kind = column_ref[:, 0:1]
    visual_ref[...] = jnp.where(kind == 1, raw, 0.0).T.astype(jnp.bfloat16)
    projected = dot_nn(narrow, project_ref[...])
    first = half_ref[0:1, 0:1] == 0
    own, got = own_ref[...], got_ref[...]
    layout = jnp.concatenate([jnp.where(first, own, got), jnp.where(first, got, own)], axis=1)
    embedded = jnp.where(kind == 2, raw, projected) + layout
    packed_ref[...] = embedded.astype(jnp.bfloat16)
    packed = packed_ref[...].astype(jnp.float32)
    scale = lax.rsqrt(jnp.mean(packed * packed, axis=-1, keepdims=True) + EPSILON)
    normed = packed * scale * gain_ref[0:1, :].astype(jnp.float32)
    normed_ref[...] = normed.T.astype(jnp.bfloat16)
    normed = normed.astype(jnp.bfloat16)
    for part in range(3):
        out_ref[part] = dot_nn(normed, weight_ref[part]).astype(jnp.bfloat16)


def embed(line, places, column, arrived, own, got, half, matrices, gains, tokens):
    width = arrived.shape[1]
    rows = 256
    wide = pl.BlockSpec((rows, width), lambda i: (i, 0))
    part = pl.BlockSpec((rows, own.shape[1]), lambda i: (i, 0))
    across = pl.BlockSpec((width, rows), lambda i: (0, i))
    return launch(
        line, embed_kernel, (places, column, arrived, own, got, half, matrices, gains, matrices),
        [
            fixed(places), pl.BlockSpec((rows, 8), lambda i: (i, 0)), fixed(arrived), part, part,
            fixed(half), pl.BlockSpec((None, width, width), lambda i: (3, 0, 0)), fixed(gains),
            pl.BlockSpec((3, width, width), lambda i: (0, 0, 0)),
        ],
        (bf16(width, tokens), bf16(tokens, width), bf16(width, tokens), bf16(3, tokens, width)),
        (across, wide, across, pl.BlockSpec((3, rows, width), lambda i: (0, i, 0))),
        (tokens // rows,), "embed",
    )


def input_grad_kernel(which, packed_ref, upper_ref, grads_ref, weight_ref, gain_ref,
                      out_ref, own_ref, other_ref, sum_ref):
    total = dot_nt(grads_ref[0], weight_ref[0])
    total = total + dot_nt(grads_ref[1], weight_ref[1])
    total = total + dot_nt(grads_ref[2], weight_ref[2])
    packed = packed_ref[...].astype(jnp.float32)
    scale = lax.rsqrt(jnp.mean(packed * packed, axis=-1, keepdims=True) + EPSILON)
    unit = packed * scale
    back = total * gain_ref[0:1, :].astype(jnp.float32)
    back = scale * (back - unit * jnp.mean(back * unit, axis=-1, keepdims=True))
    back = back + upper_ref[...]
    out_ref[...] = back.astype(jnp.bfloat16)
    put_halves(which, back, own_ref, other_ref)

    @pl.when(pl.program_id(0) == 0)
    def _():
        sum_ref[...] = jnp.zeros_like(sum_ref)

    sum_ref[0:1, :] += jnp.sum(total * unit, axis=0, keepdims=True)


def input_grad(line, which, packed, upper, grads, matrices, gains):
    tokens, width = packed.shape
    rows = 256
    half = width // 2
    wide = pl.BlockSpec((rows, width), lambda i, w: (i, 0))
    part = pl.BlockSpec((rows, half), lambda i, w: (i, 0))
    return launch(
        line, input_grad_kernel, (packed, upper, grads, matrices, gains),
        [
            wide, wide, pl.BlockSpec((3, rows, width), lambda i, w: (0, i, 0)),
            pl.BlockSpec((3, width, width), lambda i, w: (0, 0, 0)), fixed(gains),
        ],
        (bf16(tokens, width), bf16(tokens, half), bf16(tokens, half), f32(8, width)),
        (wide, part, part, pl.BlockSpec((8, width), lambda i, w: (0, 0))),
        (tokens // rows,), "input_grad", scalars=(which,),
    )


def split_small(small):
    parts = [part.astype(jnp.float32) for part in pieces(small)]
    pad = jnp.zeros((16 - 3 * small.shape[0], small.shape[1]), jnp.float32)
    return jnp.concatenate(parts + [pad], axis=0).astype(jnp.bfloat16)


def join_small(rows):
    rows = rows[:9].astype(jnp.float32)
    return rows[0:3] + rows[3:6] + rows[6:9]


def return_kernel(place_ref, rows_ref, small_ref, out_ref):
    capacity = place_ref.shape[0]
    pick = as_bf16(iota((capacity, rows_ref.shape[0]), 1) == place_ref[...])
    out_ref[:capacity, :] = dot_nn(pick, rows_ref[...]).astype(jnp.bfloat16)
    out_ref[capacity:, :] = split_small(small_ref[0:3, :])


def return_rows(line, places, rows, small, capacity):
    count = places.shape[0] // capacity
    width = rows.shape[1]
    return launch(
        line, return_kernel, (places, rows, small),
        [pl.BlockSpec((capacity, 1), lambda i: (i, 0)), fixed(rows), fixed(small)],
        (bf16(count, capacity + 16, width),),
        (pl.BlockSpec((None, capacity + 16, width), lambda i: (i, 0, 0)),), (count,), "return_rows",
    )[0]


def layout_grad_kernel(side, mine_ref, other_ref, first_ref, second_ref, keep_ref, give_ref):
    pair = pl.program_id(0)
    shards, rows, width = keep_ref.shape
    entries = shards * rows
    table = 2 * jnp.where(pair < 2, 1 - side[0], side[0]) + jnp.bitwise_and(pair, 1)
    total = jnp.zeros((entries, width), jnp.float32)
    for coords, grads in ((mine_ref, first_ref), (other_ref, second_ref)):
        tokens = grads.shape[0]
        key = coords[pl.ds(table + 1, 1), :]
        pick = as_bf16(iota((entries, tokens), 0) + pl.program_id(1) * entries == key)
        total = total + dot_nn(pick, grads[...])
    total = total.reshape(shards, rows, width).astype(jnp.bfloat16)

    @pl.when(pair < 2)
    def _():
        give_ref[...] = total

    @pl.when(pair >= 2)
    def _():
        keep_ref[...] = total


def layout_grad(line, side, mine, other, first, second, shards, rows):
    width = first.shape[1]
    step = max(1, min(shards, 512 // rows))
    last = shards // step - 1
    block = (step, None, rows, width)
    shape = bf16(shards, 2, rows, width)
    return launch(
        line, layout_grad_kernel, (mine, other, first, second),
        [fixed(mine), fixed(other), fixed(first), fixed(second)], (shape, shape),
        (
            pl.BlockSpec(
                block, lambda t, i, s: (jnp.where(t < 2, 0, i), jnp.maximum(t - 2, 0), 0, 0)
            ),
            pl.BlockSpec(
                block, lambda t, i, s: (jnp.where(t < 2, i, last), jnp.minimum(t, 1), 0, 0)
            ),
        ),
        (4, shards // step), "layout_grad", scalars=(side,),
    )


def patch_kernel(key_ref, rows_ref, weight_ref, grad_ref):
    patches, tokens = grad_ref.shape[0], rows_ref.shape[1]
    total = None
    for d in range(rows_ref.shape[0]):
        pick = as_bf16(iota((patches, tokens), 0) == key_ref[d : d + 1, :])
        part = dot_nn(pick, rows_ref[d])
        total = part if total is None else total + part
    grad_ref[...] = dot_nt(total.astype(jnp.bfloat16), weight_ref[...])


def patch_grads(line, keys, rows, matrices, patches):
    width = rows.shape[2]
    shape = f32(patches, width)
    return launch(
        line, patch_kernel, (keys, rows, matrices),
        [fixed(keys), fixed(rows), pl.BlockSpec((None, width, width), lambda i: (3, 0, 0))],
        (shape,), (fixed(shape),), (1,), "patch_grads",
    )[0]


def text_kernel(*refs):
    out_ref = refs[4]
    size = out_ref.shape[0]
    parts = []
    for rows_ref in refs[:4]:
        texts = rows_ref.shape[0] - 32
        index = rows_ref[texts : texts + 16, :texts].astype(jnp.float32)
        key = (index[0:1] * 16.0 + index[1:2]).astype(jnp.int32)
        place = iota((size, texts), 0) + pl.program_id(0) * size
        parts.append(dot_nn(as_bf16(place == key), rows_ref[:texts, :]))
    out_ref[...] = (parts[0] + parts[1]) + (parts[2] + parts[3])


def text_grads(line, rows, entries):
    width = rows[0].shape[1]
    size = 512
    return launch(
        line, text_kernel, rows, [fixed(value) for value in rows],
        (f32(entries, width),), (pl.BlockSpec((size, width), lambda i: (i, 0)),),
        (pl.cdiv(entries, size),), "text_grads",
    )[0]


def feed_forward_kernel(core, packed_ref, mixed_ref, grad_ref, own_ref, other_ref, in_ref, down_ref,
                        gain_ref, result_ref, active_ref, hidden_ref, normed_ref, turned_ref, upper_ref,
                        branch_ref, back_ref, sum_ref):
    own, other = own_ref[...], other_ref[...]
    first = core[0] == 0
    mix = jnp.concatenate([jnp.where(first, own, other), jnp.where(first, other, own)], axis=1)
    attended = packed_ref[...].astype(jnp.float32) + dot_nn(mixed_ref[...], mix)
    turned_ref[...] = mixed_ref[...].astype(jnp.float32).T.astype(jnp.bfloat16)
    scale = lax.rsqrt(jnp.mean(attended * attended, axis=-1, keepdims=True) + EPSILON)
    unit = attended * scale
    gain = gain_ref[0:1, :].astype(jnp.float32)
    normed = unit * gain
    normed_ref[...] = normed.T.astype(jnp.bfloat16)
    normed = normed.astype(jnp.bfloat16)
    out_grad = grad_ref[...]
    result = attended
    back = jnp.zeros_like(attended)
    width = attended.shape[1]
    for part in range(in_ref.shape[0]):
        cut = slice(part * width, part * width + width)
        hidden = dot_nn(normed, in_ref[part])
        square = hidden * hidden
        tanh = jnp.tanh(hidden * (RATE + RATE * 0.044715 * square))
        half = 0.5 + 0.5 * tanh
        active = hidden * half
        active_ref[cut, :] = active.T.astype(jnp.bfloat16)
        active = active.astype(jnp.bfloat16)
        slope = half + hidden * half * (1.0 - tanh) * (RATE + 3.0 * 0.044715 * RATE * square)
        result = result + dot_nn(active, down_ref[cut, :])
        grad_hidden = (dot_nt(out_grad, down_ref[cut, :]) * slope).astype(jnp.bfloat16)
        hidden_ref[:, cut] = grad_hidden
        back = back + dot_nt(grad_hidden, in_ref[part])
    result_ref[...] = result.astype(jnp.bfloat16)

    @pl.when(pl.program_id(0) == 0)
    def _():
        sum_ref[...] = jnp.zeros_like(sum_ref)

    sum_ref[0:1, :] += jnp.sum(back * unit, axis=0, keepdims=True)
    back = back * gain
    back = scale * (back - unit * jnp.mean(back * unit, axis=-1, keepdims=True))
    back = back + out_grad.astype(jnp.float32)
    upper_ref[...] = back
    branch = back.astype(jnp.bfloat16)
    branch_ref[...] = branch
    back_ref[...] = dot_nt(branch, mix).astype(jnp.bfloat16)


def feed_forward(line, core, packed, mixed, out_grad, mix_own, mix_other, full_in, full_down, gains):
    tokens, width = packed.shape
    hidden = full_down.shape[0]
    rows = 256
    wide = pl.BlockSpec((rows, width), lambda i, c: (i, 0))
    tall = pl.BlockSpec((rows, hidden), lambda i, c: (i, 0))
    across = pl.BlockSpec((width, rows), lambda i, c: (0, i))
    narrow, turned = bf16(tokens, width), bf16(width, tokens)
    operands = (packed, mixed, out_grad, mix_own, mix_other, full_in, full_down, gains)
    return launch(
        line, feed_forward_kernel, operands,
        [wide, wide, wide] + [fixed(value) for value in operands[3:]],
        (
            narrow, bf16(hidden, tokens), bf16(tokens, hidden), turned, turned,
            f32(tokens, width), narrow, narrow, f32(8, width),
        ),
        (
            wide, pl.BlockSpec((hidden, rows), lambda i, c: (0, i)), tall, across, across,
            wide, wide, wide, pl.BlockSpec((8, width), lambda i, c: (0, 0)),
        ),
        (tokens // rows,), "feed_forward", scalars=(core,),
    )


def put_halves(which, total, keep_ref, give_ref):
    half = total.shape[1] // 2
    first, second = total[:, :half], total[:, half:]
    mine = which[0] == 0
    keep_ref[...] = jnp.where(mine, first, second).astype(jnp.bfloat16)
    give_ref[...] = jnp.where(mine, second, first).astype(jnp.bfloat16)


def contract_halves_kernel(which, left_ref, right_ref, keep_ref, give_ref):
    put_halves(which, dot_nn(left_ref[...], right_ref[...]), keep_ref, give_ref)


def contract_halves(line, which, left, right):
    count, tokens = left.shape
    width = right.shape[1]
    size, half = min(count, width), width // 2
    out = pl.BlockSpec((size, half), lambda i, w: (i, 0))
    shape = bf16(count, half)
    return launch(
        line, contract_halves_kernel, (left, right),
        [pl.BlockSpec((size, tokens), lambda i, w: (i, 0)), fixed(right)],
        (shape, shape), (out, out), (count // size,), "contract_halves", scalars=(which,),
    )


def contract_quarters_kernel(which, left_ref, right_ref, keep_ref, give_ref):
    del which
    total = dot_nn(left_ref[...], right_ref[...])
    shards, _, rows, half = keep_ref.shape

    def put(out_ref):
        for d in range(shards):
            for h in range(2):
                part = total[d * rows : d * rows + rows, h * half : h * half + half]
                out_ref[d, h] = part.astype(jnp.bfloat16)

    @pl.when(pl.program_id(0) < 2)
    def _():
        put(give_ref)

    @pl.when(pl.program_id(0) >= 2)
    def _():
        put(keep_ref)


def contract_quarters(line, which, left, right, shards):
    count, tokens = left.shape
    quarter = right.shape[1] // 4
    block = (shards, 2, count // shards, quarter // 2)
    shape = bf16(2, *block)

    def column(i, w):
        return (0, jnp.where(i < 2, 2 * i + 1 - w[0], 2 * (i - 2) + w[0]))

    return launch(
        line, contract_quarters_kernel, (left, right),
        [fixed(left), pl.BlockSpec((tokens, quarter), column)], (shape, shape),
        (
            pl.BlockSpec((None,) + block, lambda i, w: (jnp.maximum(i - 2, 0), 0, 0, 0, 0)),
            pl.BlockSpec((None,) + block, lambda i, w: (jnp.minimum(i, 1), 0, 0, 0, 0)),
        ),
        (4,), "contract_quarters", scalars=(which,),
    )


def square_kernel(which, normed_ref, grads_ref, visual_ref, packed_ref, keep_ref, give_ref):
    shards, rows, half = keep_ref.shape

    def put(total):
        mine = which[0] == 0
        for d in range(shards):
            part = total[d * rows : d * rows + rows]
            first, second = part[:, :half], part[:, half:]
            keep_ref[d] = jnp.where(mine, first, second).astype(jnp.bfloat16)
            give_ref[d] = jnp.where(mine, second, first).astype(jnp.bfloat16)

    @pl.when(pl.program_id(0) < 3)
    def _():
        put(dot_nn(normed_ref[...], grads_ref[...]))

    @pl.when(pl.program_id(0) == 3)
    def _():
        put(dot_nn(visual_ref[...], packed_ref[...]))


def square_grads(line, which, normed, grads, visual, grad_packed, shards):
    width, tokens = normed.shape
    rows, half = width // shards, width // 2
    out = pl.BlockSpec((shards, None, None, rows, half), lambda m, w: (0, m // 2, m % 2, 0, 0))
    shape = bf16(shards, 2, 2, rows, half)
    return launch(
        line, square_kernel, (normed, grads, visual, grad_packed),
        [
            fixed(normed),
            pl.BlockSpec((None, tokens, width), lambda m, w: (jnp.minimum(m, 2), 0, 0)),
            fixed(visual), fixed(grad_packed),
        ],
        (shape, shape), (out, out), (4,), "square_grads", scalars=(which,),
    )


def fold_kernel(bit, value_ref, got_ref, keep_ref, give_ref):
    del bit
    total = value_ref[...].astype(jnp.float32) + got_ref[...].astype(jnp.float32)

    @pl.when(pl.program_id(0) == 0)
    def _():
        give_ref[...] = total.astype(give_ref.dtype)

    @pl.when(pl.program_id(0) == 1)
    def _():
        keep_ref[...] = total.astype(keep_ref.dtype)


def fold(line, bit, value, got):
    a, _, b, rows, width = value.shape
    step = a
    while step > 1 and step * b * rows * width * value.dtype.itemsize > 800_000:
        step //= 2
    count = a // step
    source = pl.BlockSpec(
        (step, None, b, rows, width), lambda n, i, s: (i, jnp.where(n == 0, 1 - s[0], s[0]), 0, 0, 0)
    )
    block = (step, b, rows, width)
    shape = jax.ShapeDtypeStruct((a, b, rows, width), value.dtype)
    return launch(
        line, fold_kernel, (value, got), [source, source], (shape, shape),
        (
            pl.BlockSpec(block, lambda n, i, s: (jnp.where(n == 0, 0, i), 0, 0, 0)),
            pl.BlockSpec(block, lambda n, i, s: (jnp.where(n == 0, i, count - 1), 0, 0, 0)),
        ),
        (2, count), "fold", scalars=(bit,),
    )


def add_kernel(value_ref, got_ref, out_ref):
    total = value_ref[...].astype(jnp.float32) + got_ref[...].astype(jnp.float32)
    out_ref[...] = total.astype(out_ref.dtype)


def add(line, value, got):
    shape = jax.ShapeDtypeStruct(value.shape, value.dtype)
    return launch(
        line, add_kernel, (value, got), [fixed(value), fixed(got)], (shape,), (fixed(shape),),
        (1,), "add",
    )[0]


def rows_fold_kernel(side, down_ref, down_got_ref, mix_ref, mix_got_ref, keep_ref, give_ref):
    del side
    down = down_ref[...].astype(jnp.float32) + down_got_ref[...].astype(jnp.float32)
    mix = mix_ref[...].astype(jnp.float32) + mix_got_ref[...].astype(jnp.float32)
    total = jnp.concatenate([down, mix], axis=1).astype(jnp.bfloat16)

    @pl.when(pl.program_id(0) == 0)
    def _():
        give_ref[...] = total

    @pl.when(pl.program_id(0) == 1)
    def _():
        keep_ref[...] = total


def rows_fold(line, side, down, down_got, mix, mix_got):
    parts, _, rows, width = down.shape
    extra = mix.shape[2]
    step = max(1, parts // 2)

    def source(count):
        return pl.BlockSpec(
            (step, None, count, width), lambda n, i, s: (i, jnp.where(n == 0, 1 - s[0], s[0]), 0, 0)
        )

    shape = bf16(parts, rows + extra, width)
    block = (step, rows + extra, width)
    last = parts // step - 1
    return launch(
        line, rows_fold_kernel, (down, down_got, mix, mix_got),
        [source(rows), source(rows), source(extra), source(extra)], (shape, shape),
        (
            pl.BlockSpec(block, lambda n, i, s: (jnp.where(n == 0, 0, i), 0, 0)),
            pl.BlockSpec(block, lambda n, i, s: (jnp.where(n == 0, i, last), 0, 0)),
        ),
        (2, parts // step), "rows_fold", scalars=(side,),
    )


def stack_kernel(bit, value_ref, got_ref, out_ref):
    del bit

    @pl.when(pl.program_id(0) == 0)
    def _():
        out_ref[...] = value_ref[...]

    @pl.when(pl.program_id(0) == 1)
    def _():
        out_ref[...] = got_ref[...]


def stack(line, bit, value, got):
    a, rows, width = value.shape
    return launch(
        line, stack_kernel, (value, got), [fixed(value), fixed(got)],
        (jax.ShapeDtypeStruct((a, 2, rows, width), value.dtype),),
        (
            pl.BlockSpec(
                (a, None, rows, width), lambda n, s: (0, jnp.where(n == 0, s[0], 1 - s[0]), 0, 0)
            ),
        ),
        (2,), "stack", scalars=(bit,),
    )[0]


def split_stack_kernel(parts, bit, value_ref, got_ref, *outs):
    del bit

    def put(source_ref):
        start = 0
        for rows, out_ref in zip(parts, outs):
            out_ref[...] = source_ref[:, start : start + rows, :]
            start += rows

    @pl.when(pl.program_id(0) == 0)
    def _():
        put(value_ref)

    @pl.when(pl.program_id(0) == 1)
    def _():
        put(got_ref)


def split_stack(line, bit, value, got, parts):
    a, _, width = value.shape
    return launch(
        line, partial(split_stack_kernel, parts), (value, got), [fixed(value), fixed(got)],
        [bf16(a, 2, rows, width) for rows in parts],
        [
            pl.BlockSpec(
                (a, None, rows, width), lambda n, s: (0, jnp.where(n == 0, s[0], 1 - s[0]), 0, 0)
            )
            for rows in parts
        ],
        (2,), "split_stack", scalars=(bit,),
    )


def both_sides(line, side, value, got):
    return stack(line, side, value, got)


def arrange_kernel(me, *refs):
    del me
    for n in range(4):

        @pl.when(pl.program_id(0) == n)
        def _():
            refs[4][...] = refs[n][...]


def arrange(line, me, values):
    shape = values[0].shape
    return launch(
        line, arrange_kernel, tuple(values), [fixed(value) for value in values],
        (bf16(4, *shape),),
        (pl.BlockSpec((None,) + shape, lambda n, s: (jnp.bitwise_xor(n, s[0]), 0, 0)),),
        (4,), "arrange", scalars=(me,),
    )[0]


def assemble_forward_kernel(me, *refs):
    del me
    down_ref, mix_ref, in_ref = refs[4:]
    for n in range(4):

        @pl.when(pl.program_id(0) == n)
        def _():
            start = 0
            for out_ref in (down_ref, mix_ref):
                rows = out_ref.shape[0]
                out_ref[...] = refs[n][start : start + rows, :].astype(jnp.float32)
                start += rows
            rows = in_ref.shape[0]
            first = refs[n][start : start + rows, :]
            second = refs[n][start + rows : start + 2 * rows, :]
            in_ref[...] = jnp.concatenate([first, second], axis=1).astype(jnp.float32)


def assemble_forward(line, me, values, down_rows, mix_rows, shard_rows):
    half = values[0].shape[1]

    def part(rows):
        return pl.BlockSpec(
            (None, rows, half),
            lambda n, s: (jnp.bitwise_xor(n, s[0]) // 2, 0, jnp.bitwise_xor(n, s[0]) % 2),
        )

    return launch(
        line, assemble_forward_kernel, tuple(values), [fixed(value) for value in values],
        (
            f32(2, down_rows, 2 * half), f32(2, mix_rows, 2 * half), f32(shard_rows, 8 * half),
        ),
        (
            part(down_rows), part(mix_rows),
            pl.BlockSpec((shard_rows, 2 * half), lambda n, s: (0, jnp.bitwise_xor(n, s[0]))),
        ),
        (4,), "assemble_forward", scalars=(me,),
    )


def assemble_backward_kernel(me, *refs):
    layout_ref, qkv_ref, project_ref = refs[4:]
    device, k = pl.program_id(0), pl.program_id(1)
    layout_rows, rows = layout_ref.shape[0], project_ref.shape[0]
    for n in range(4):

        @pl.when(device == jnp.bitwise_xor(me[0], n))
        def _():
            for part in range(2):

                @pl.when(k == part)
                def _():
                    start = part * layout_rows
                    layout_ref[...] = refs[n][start : start + layout_rows, :].astype(jnp.float32)
                    start = 2 * layout_rows + part * rows
                    matrix = refs[n][start : start + rows, :].astype(jnp.float32)
                    last = jnp.logical_and(device >= 2, k == 1)

                    @pl.when(jnp.logical_not(last))
                    def _():
                        qkv_ref[...] = matrix

                    @pl.when(last)
                    def _():
                        project_ref[...] = matrix


def assemble_backward(line, me, values, layout_rows, rows):
    half = values[0].shape[1]
    return launch(
        line, assemble_backward_kernel, tuple(values), [fixed(value) for value in values],
        (f32(4, layout_rows, 2 * half), f32(3, rows, 2 * half), f32(rows, 2 * half)),
        (
            pl.BlockSpec(
                (None, layout_rows, half), lambda t, k, s: (2 * (t // 2) + k, 0, t % 2)
            ),
            pl.BlockSpec(
                (None, rows, half), lambda t, k, s: (jnp.minimum(2 * (t // 2) + k, 2), 0, t % 2)
            ),
            pl.BlockSpec((rows, half), lambda t, k, s: (0, jnp.where(t == 3, 1, 0))),
        ),
        (4, 2), "assemble_backward", scalars=(me,),
    )


def swap(value, axis, bit):
    count = lax.axis_size(axis)
    return lax.ppermute(value, axis, [(i, i ^ bit) for i in range(count)])


def bit_of(axis, bit):
    return jnp.bitwise_and(lax.axis_index(axis), bit) != 0


def bit_index(axis, bit):
    return bit_of(axis, bit).astype(jnp.int32).reshape(1)


class Gather:
    def __init__(self, line, value):
        self.line = line
        self.value = value[None]
        self.bit = lax.axis_size("dp") // 2
        self.got = swap(self.value, "dp", self.bit)

    def step(self):
        rows, width = self.value.shape[1:]
        value = stack(self.line, bit_index("dp", self.bit), self.value, self.got)
        self.value = value.reshape(-1, rows, width)
        self.bit //= 2
        self.got = swap(self.value, "dp", self.bit)

    def finish(self, parts):
        while self.bit > 1:
            self.step()
        values = split_stack(self.line, bit_index("dp", 1), self.value, self.got, parts)
        return [value.reshape((-1,) + value.shape[2:]) for value in values]


def padded(value):
    return jnp.pad(value, ((0, -value.shape[0] % 16), (0, 0)))


class Sum:
    def __init__(self, line, bits, value, got):
        self.line, self.bits, self.value, self.got = line, list(bits), value, got
        self.done = False

    def step(self):
        if self.done:
            return
        rows, width = self.value.shape[-2:]
        if not self.bits:
            self.value = add(self.line, self.value.reshape(rows, width), self.got.reshape(rows, width))
            self.done = True
            return
        bit = self.bits.pop()
        shape = (-1, 2, 1, rows, width)
        value, give = fold(
            self.line, bit_index("dp", bit), self.value.reshape(shape), self.got.reshape(shape)
        )
        self.value, self.got = value, swap(give, "dp", bit)

    def finish(self):
        while not self.done:
            self.step()
        return self.value


def shards(
    patches,
    src_kind,
    src_index,
    layout_coords,
    placing,
    segments,
    text_table,
    layout_tables,
    patch_proj,
    rel_table,
    norm_gains,
    w_qkv,
    w_attn_out,
    w_ff_in,
    w_ff_out,
    out_grad,
):
    data_count = lax.axis_size("dp")
    tokens = placing.shape[0]
    capacity = 2 * tokens // data_count
    width = text_table.shape[1]
    half_width = width // 2
    texts = tokens - patches.shape[0]
    shift = tokens.bit_length() - 1
    shard_rows = w_attn_out.shape[0]
    layout_rows = layout_tables.shape[1]
    stream = lax.axis_index("stream")
    core = jnp.bitwise_and(stream, 1)
    side = jnp.right_shift(stream, 1)
    gain_count = norm_gains.shape[1]

    own_core, own_side = core.reshape(1), side.reshape(1)
    dp_bits = [1 << n for n in reversed(range(data_count.bit_length() - 1))]
    line = Line()

    def own_half(value):
        return lax.dynamic_slice_in_dim(value, core * half_width, half_width, axis=-1)

    in_quarter = lax.dynamic_index_in_dim(
        w_ff_in.reshape(shard_rows, 4, -1), stream, 1, keepdims=False
    )
    down_quarter = lax.dynamic_index_in_dim(
        w_ff_out.reshape(4, -1, width), stream, 0, keepdims=False
    )
    layout_part = own_half(
        lax.dynamic_slice_in_dim(layout_tables, side * 2, 2, axis=0)
    ).reshape(-1, half_width)
    mix_part = own_half(
        lax.dynamic_slice_in_dim(w_attn_out, side * (shard_rows // 2), shard_rows // 2, axis=0)
    )
    gain_part = jnp.pad(norm_gains, ((0, 0), (0, half_width - gain_count)))
    table_rows, mix_rows = layout_part.shape[0], mix_part.shape[0]
    square = jnp.concatenate([w_qkv, patch_proj[None]], axis=0)
    square = lax.dynamic_index_in_dim(square, stream, 0, keepdims=False)
    mix_part, gain_part = padded(mix_part), padded(gain_part)
    columns = Gather(line, jnp.concatenate([layout_part, mix_part, gain_part], axis=0))
    square = Gather(line, square)
    full_in = lax.all_gather(in_quarter, ("stream", "dp"), axis=0, tiled=True)
    full_in = full_in.reshape(4, width, -1)

    meta, slot_keys, text_index = find_slots(
        line, data_count, capacity, shift, placing, src_kind, src_index, layout_coords, texts
    )
    arrived_meta = lax.all_to_all(
        meta.reshape(16, data_count, capacity), "dp", split_axis=1, concat_axis=1, tiled=True
    ).reshape(16, -1)
    columns.step()
    square.step()
    columns.step()
    square.step()
    column, across, place = place_meta(line, arrived_meta, tokens)
    column_other = swap(column, "stream", 1)
    across_other = column_other.T
    tables, mix, gains = columns.finish((table_rows, mix_part.shape[0], gain_part.shape[0]))
    tables_got = swap(tables, "stream", 2)
    (square,) = square.finish((shard_rows,))
    square = square.reshape(width, width)
    square_got = swap(square, "stream", 2)
    mix_got = swap(mix, "stream", 2)
    gains = gains[:, :2, :gain_count].transpose(1, 0, 2).reshape(2, width)
    text_rows = jnp.take(text_table, text_index[0], axis=0)
    send_rows, down_quarter = pack(line, slot_keys, patches, text_rows, (down_quarter,))
    arrived = lax.all_to_all(
        send_rows.reshape(data_count, capacity, width), "dp", split_axis=0, concat_axis=0, tiled=True
    ).reshape(-1, width)
    full_down = lax.all_gather(down_quarter, ("dp", "stream"), axis=0, tiled=True)
    sums = layout_lookup(line, own_side, column, column_other, tables, layout_rows)
    matrices = arrange(
        line, stream.reshape(1),
        (square, swap(square, "stream", 1), square_got, swap(square_got, "stream", 1)),
    )
    own_sum, other_sum = layout_lookup(
        line, 1 - own_side, column, column_other, tables_got, layout_rows, sums
    )
    got_sum = swap(other_sum, "stream", 1)
    half_index = jnp.broadcast_to(core, (8, 128)).astype(jnp.int32)
    visual, packed, normed_one, projections = embed(
        line, place, column, arrived, own_sum, got_sum, half_index, matrices, gains[:1], tokens
    )
    mix_own = both_sides(line, own_side, mix, mix_got)
    mix_own = mix_own[:, :, :mix_rows].reshape(width, half_width)
    mix_other = swap(mix_own, "stream", 1)
    aug_q, aug_k, table, mirrored = prepare(segments, rel_table)
    mixed, lse = attention_forward(line, projections, aug_q, aug_k, table)
    (
        result, active, grad_hidden, normed_two, turned, upper, grad_branch, grad_mixed,
        gain_two_sum,
    ) = feed_forward(
        line, own_core, packed, mixed, out_grad, mix_own, mix_other, full_in, full_down, gains[1:]
    )

    down_keep, down_give = contract_halves(line, own_core, active, out_grad)
    down_got = swap(down_give, "stream", 1)
    mix_keep, mix_give = contract_halves(line, own_core, turned, grad_branch)
    mix_got = swap(mix_give, "stream", 1)
    in_keep, in_give = contract_quarters(
        line, own_core, normed_two, grad_hidden, data_count
    )
    in_got = swap(in_give, "stream", 1)
    down_shape = (data_count, 2, down_keep.shape[0] // data_count // 2, half_width)
    mix_shape = (data_count, 2, mix_rows, half_width)
    rows_keep, rows_give = rows_fold(
        line, own_side, down_keep.reshape(down_shape), down_got.reshape(down_shape),
        mix_keep.reshape(mix_shape), mix_got.reshape(mix_shape),
    )
    rows_got = swap(rows_give, "stream", 2)
    in_shape = (data_count, 2, 2 * shard_rows, half_width)
    in_keep, in_give = fold(
        line, bit_index("dp", 1), in_keep.reshape(in_shape)[:, :, None],
        in_got.reshape(in_shape)[:, :, None],
    )
    in_got = swap(in_give, "dp", 1)

    qkv_grads, grad_rel = attention_backward(
        line, projections, mixed, grad_mixed, lse, aug_q, aug_k, mirrored
    )
    rows_shape = (data_count // 2, 2, 1) + rows_keep.shape[1:]
    rows_keep, rows_give = fold(
        line, bit_index("dp", 1), rows_keep.reshape(rows_shape), rows_got.reshape(rows_shape)
    )
    rows_got = swap(rows_give, "dp", 1)
    in_shape = (1, 2, data_count // 2, 2 * shard_rows, half_width)
    in_keep, in_give = fold(line, own_side, in_keep.reshape(in_shape), in_got.reshape(in_shape))
    in_got = swap(in_give, "stream", 2)
    grad_packed, own_columns, other_columns, gain_one_sum = input_grad(
        line, own_core, packed, upper, qkv_grads, matrices, gains[:1]
    )
    other_columns = swap(other_columns, "stream", 1)
    rows_shape = (data_count // 4, 2) + rows_keep.shape[-2:]
    in_shape = (data_count // 4, 2) + in_keep.shape[-2:]
    value, give = rows_fold(
        line, bit_index("dp", 2), rows_keep.reshape(rows_shape), rows_got.reshape(rows_shape),
        in_keep.reshape(in_shape), in_got.reshape(in_shape),
    )
    forward_sum = Sum(line, dp_bits[:-2], value, swap(give, "dp", 2))
    rel = rel_gradient(grad_rel, rel_table.shape[0])
    rel_row = jnp.pad(rel.reshape(1, -1), ((0, 0), (0, width - rel.size)))
    small = jnp.concatenate([gain_one_sum[:1], gain_two_sum[:1], rel_row], axis=0)
    returned = return_rows(
        line, place[:1].reshape(-1, 1), grad_packed, jnp.pad(small, ((0, 5), (0, 0))), capacity
    )
    came_back = lax.all_to_all(returned, "dp", split_axis=0, concat_axis=0, tiled=True)

    table_keep, table_give = layout_grad(
        line, own_side, across, across_other, own_columns, other_columns, data_count, layout_rows
    )
    table_got = swap(table_give, "stream", 2)
    square_keep, square_give = square_grads(
        line, own_core, normed_one, qkv_grads, visual, grad_packed, data_count
    )
    square_got = swap(square_give, "stream", 1)
    square_shape = (data_count, 2, 1, 2 * shard_rows, half_width)
    square_keep, square_give = fold(
        line, own_side, square_keep.reshape(square_shape), square_got.reshape(square_shape)
    )
    square_got = swap(square_give, "stream", 2)
    table_shape = (data_count // 2, 2, 1, table_rows, half_width)
    table_keep, table_give = fold(
        line, bit_index("dp", 1), table_keep.reshape(table_shape), table_got.reshape(table_shape)
    )
    table_got = swap(table_give, "dp", 1)

    def stream_group(value):
        across_sides = swap(value, "stream", 2)
        return (value, swap(value, "stream", 1), across_sides, swap(across_sides, "stream", 1))

    wide_meta = meta.astype(jnp.float32)
    slot_kind = wide_meta[:1]
    slot_index = (wide_meta[11:12] * 16.0 + wide_meta[12:13]).astype(jnp.int32)
    slot_text = (wide_meta[13:14] * 4.0 + wide_meta[14:15]).astype(jnp.int32)

    def slot_keys_of(kind, value):
        keys = jnp.where(slot_kind == kind, value, -1).reshape(data_count, capacity)
        return jnp.pad(keys, ((0, 0), (0, 16)), constant_values=-1)

    text_grad_rows = unpack_text(line, slot_keys_of(2.0, slot_text), came_back, text_index)
    rows_side = swap(text_grad_rows, "stream", 2)
    rows_core = swap(text_grad_rows, "stream", 1)
    square_shape = (data_count // 2, 2, 1, 2 * shard_rows, half_width)
    square_keep, square_give = fold(
        line, bit_index("dp", 1), square_keep.reshape(square_shape),
        square_got.reshape(square_shape),
    )
    square_got = swap(square_give, "dp", 1)
    forward_sum.step()
    rows_both = swap(rows_side, "stream", 1)
    table_shape = (data_count // 4, 2, table_rows, half_width)
    square_shape = (data_count // 4, 2, 2 * shard_rows, half_width)
    value, give = rows_fold(
        line, bit_index("dp", 2), table_keep.reshape(table_shape), table_got.reshape(table_shape),
        square_keep.reshape(square_shape), square_got.reshape(square_shape),
    )
    backward_sum = Sum(line, dp_bits[:-2], value, swap(give, "dp", 2))
    grad_patches = patch_grads(
        line, slot_keys_of(1.0, slot_index), came_back, matrices, patches.shape[0]
    )
    backward_sum.step()
    forward_sum.finish()
    forward_group = stream_group(forward_sum.value)
    text_grad_rows = (text_grad_rows, rows_side, rows_core, rows_both)
    grad_text = text_grads(line, text_grad_rows, text_table.shape[0])
    backward_sum.finish()
    small = [join_small(rows[texts + 16 :]) for rows in text_grad_rows]
    small = (small[0] + small[1]) + (small[2] + small[3])

    shard_down, shard_mix, shard_in = assemble_forward(
        line, stream.reshape(1), forward_group, down_shape[2], mix_rows,
        shard_rows,
    )
    shard_layout, shard_qkv, shard_project = assemble_backward(
        line, stream.reshape(1), stream_group(backward_sum.value), layout_rows, shard_rows
    )
    grad_gains = lax.dynamic_slice_in_dim(
        small[:2], lax.axis_index("dp") * gain_count, gain_count, axis=1
    )
    return (
        result,
        grad_patches,
        grad_text,
        shard_layout,
        shard_project,
        small[2, : rel.size].reshape(rel.shape),
        grad_gains,
        shard_qkv,
        shard_mix.reshape(shard_rows, width),
        shard_in,
        shard_down.reshape(-1, width),
    )


def solution(mesh):
    return jax.shard_map(
        shards,
        mesh=mesh,
        in_specs=(
            P(("dp", "stream"), None),
            P(("dp", "stream")),
            P(("dp", "stream")),
            P(None, ("dp", "stream")),
            P(("dp", "stream")),
            P(("dp", "stream"), None),
            P("dp", None),
            P(None, "dp", None),
            P("dp", None),
            P(),
            P(None, "dp"),
            P(None, "dp", None),
            P("dp", None),
            P("dp", None),
            P("dp", None),
            P(("dp", "stream"), None),
        ),
        out_specs=(
            P(("dp", "stream"), None),
            P(("dp", "stream"), None),
            P("dp", None),
            P(None, "dp", None),
            P("dp", None),
            P(),
            P(None, "dp"),
            P(None, "dp", None),
            P("dp", None),
            P("dp", None),
            P("dp", None),
        ),
        check_vma=False,
    )
```

```python
from functools import partial
import math

import jax
import jax.numpy as jnp
from jax import lax
from jax.experimental import pallas as pl
from jax.experimental.pallas import tpu as pltpu
from jax.sharding import PartitionSpec as P

EPSILON = 1e-06
THRESHOLDS = (12, 16, 23, 32, 46, 64, 91)
BLK = 256
NEG = -1e30
RATE = math.sqrt(2.0 / math.pi)
VMEM_LIMIT = 56 * 2**20
SMALL = pl.CostEstimate(flops=1, bytes_accessed=1, transcendentals=0)


class Line:
    def __init__(self):
        self.last = jnp.zeros((8, 128), jnp.float32)


def launch(
    line, kernel, operands, in_specs, out_shape, out_specs, grid, name, scalars=(), scratch=(), waits=()
):
    held, given, made = len(scalars), len(operands), len(out_shape)
    token = pl.BlockSpec((8, 128), lambda *_: (0, 0))

    def body(*refs):
        outs = held + given + 1 + len(waits)
        refs[outs + made][...] = refs[held + given][...]
        kernel(*refs[: held + given], *refs[outs : outs + made], *refs[outs + made + 1 :])

    out_shape = [jax.ShapeDtypeStruct(value.shape, value.dtype) for value in out_shape]
    results = pl.pallas_call(
        body,
        out_shape=tuple(out_shape) + (jax.ShapeDtypeStruct((8, 128), jnp.float32),),
        grid_spec=pltpu.PrefetchScalarGridSpec(
            num_scalar_prefetch=held,
            grid=grid,
            in_specs=list(in_specs) + [token] + [pl.BlockSpec(memory_space=pl.ANY)] * len(waits),
            out_specs=tuple(out_specs) + (token,),
            scratch_shapes=list(scratch),
        ),
        compiler_params=pltpu.CompilerParams(vmem_limit_bytes=VMEM_LIMIT),
        cost_estimate=SMALL,
        name=name,
    )(*scalars, *operands, line.last, *waits)
    line.last = results[-1]
    return results[:-1]


def fixed(value):
    return pl.BlockSpec(value.shape, lambda *_: (0,) * len(value.shape))


def bf16(*shape):
    return jax.ShapeDtypeStruct(shape, jnp.bfloat16)


def f32(*shape):
    return jax.ShapeDtypeStruct(shape, jnp.float32)


def i32(*shape):
    return jax.ShapeDtypeStruct(shape, jnp.int32)


def bucket_of(relative):
    magnitude = jnp.abs(relative)
    beyond = 8 + sum(((magnitude >= threshold).astype(jnp.int32) for threshold in THRESHOLDS))
    return jnp.where(relative > 0, 16, 0).astype(jnp.int32) + jnp.where(
        magnitude < 8, magnitude, beyond
    )


def dot_nt(a, b):
    return lax.dot_general(a, b, (((1,), (1,)), ((), ())), preferred_element_type=jnp.float32)

def dot_nn(a, b):
    return lax.dot_general(a, b, (((1,), (0,)), ((), ())), preferred_element_type=jnp.float32)

def dot_tn(a, b):
    return lax.dot_general(a, b, (((0,), (0,)), ((), ())), preferred_element_type=jnp.float32)


def pieces(value):
    one = value.astype(jnp.bfloat16)
    rest = value - one.astype(jnp.float32)
    two = rest.astype(jnp.bfloat16)
    three = (rest - two.astype(jnp.float32)).astype(jnp.bfloat16)
    return one, two, three

def put_pieces(base, value, lane):
    one, two, three = pieces(value)
    base = jnp.where(jnp.logical_or(lane == 8, lane == 72), one, base)
    base = jnp.where(jnp.logical_or(lane == 9, lane == 73), two, base)
    return jnp.where(jnp.logical_or(lane == 10, lane == 74), three, base)

def diagonal_sums(block):
    wide = jnp.concatenate([block, jnp.zeros_like(block)], axis=1)
    total = wide[:128]
    for start in range(128, BLK, 128):
        total = total + pltpu.roll(wide[start : start + 128], 2 * BLK - start, 1)
    eight = total[:8]
    for start in range(8, 128, 8):
        eight = eight + pltpu.roll(total[start : start + 8], 2 * BLK - start, 1)
    one = eight[:1]
    for row in range(1, 8):
        one = one + pltpu.roll(eight[row : row + 1], 2 * BLK - row, 1)
    return one


def window_of(block, count):
    low = max(0, block * BLK - 2 * BLK + 1) // BLK
    high = min(count - 1, (block * BLK + BLK - 1 + 2 * BLK - 1) // BLK)
    return low, high + 1

def fill_strip(strip, table, slot, count):
    middle = (count - 1) * BLK
    for step in (-1, 0, 1):
        window = table[slot : slot + 1, BLK * step + BLK : BLK * step + 3 * BLK]
        spread = jnp.broadcast_to(window, (BLK, 2 * BLK))
        start = middle + step * BLK
        strip[slot, :, start : start + BLK] = pltpu.roll(spread, 0, 1, stride=1, stride_axis=0)[:, BLK:]
    low = jnp.broadcast_to(table[slot : slot + 1, 0:1], (BLK, middle - BLK))
    high = jnp.broadcast_to(table[slot : slot + 1, 4 * BLK - 1 : 4 * BLK], (BLK, middle - BLK))
    strip[slot, :, 0 : middle - BLK] = low
    strip[slot, :, middle + 2 * BLK :] = high

def forward_kernel(q_ref, k_ref, v_ref, aug_q, aug_k, table, out_ref, lse_ref, strip, ka, va):
    length = q_ref.shape[0]
    count = length // BLK
    lane = lax.broadcasted_iota(jnp.int32, (1, 128), 1)
    left = lane < 64
    for h in range(2):
        fill_strip(strip, table, h, count)
        mine = left if h == 0 else jnp.logical_not(left)
        ka[h] = jnp.where(mine, k_ref[...], aug_k[...])
        va[h] = jnp.where(mine, v_ref[...], aug_k[...])
    for qb in range(count):
        rows = slice(qb * BLK, qb * BLK + BLK)
        low, high = window_of(qb, count)
        keys = slice(low * BLK, high * BLK)
        offset = (count - 1 - qb) * BLK
        query = q_ref[rows, :] * jnp.bfloat16(0.125)
        outs = []
        lses = []
        for h in range(2):
            qa = jnp.where(left if h == 0 else jnp.logical_not(left), query, aug_q[rows, :])
            s = dot_nt(qa, ka[h, keys, :]) + strip[h, :, offset + low * BLK : offset + high * BLK]
            peak = jnp.max(s, axis=1, keepdims=True)
            p = jnp.exp(s - peak).astype(jnp.bfloat16)
            acc = dot_nn(p, va[h, keys, :])
            mark = 72 if h == 0 else 8
            total = acc[:, mark : mark + 1]
            outs.append(acc / total)
            lses.append(jnp.broadcast_to(peak + jnp.log(total), (BLK, 128)))
        out_ref[rows, :] = jnp.where(left, outs[0], outs[1]).astype(jnp.bfloat16)
        lse_ref[rows, :] = jnp.where(left, lses[0], lses[1])

def backward_kernel(
    q_ref, k_ref, v_ref, mixed_ref, grad_ref, lse_ref, aug_q, aug_k, table,
    grads_ref, rel_ref,
    strip, rel, ka, va, qa, ga, dq_acc,
):
    length = q_ref.shape[0]
    count = length // BLK
    middle = (count - 1) * BLK
    lane = lax.broadcasted_iota(jnp.int32, (1, 128), 1)
    left = lane < 64
    rel[...] = jnp.zeros_like(rel)
    dq_acc[...] = jnp.zeros_like(dq_acc)
    inner = mixed_ref[...].astype(jnp.float32) * grad_ref[...].astype(jnp.float32)
    query = q_ref[...] * jnp.bfloat16(0.125)
    for h in range(2):
        fill_strip(strip, table, h, count)
        mine = left if h == 0 else jnp.logical_not(left)
        ka[h] = jnp.where(mine, k_ref[...], aug_k[...])
        va[h] = jnp.where(mine, v_ref[...], aug_k[...])
        at = 0 if h == 0 else 64
        qa[h] = jnp.where(mine, query, put_pieces(aug_q[...], -lse_ref[:, at : at + 1], lane))
        delta = jnp.sum(jnp.where(mine, inner, 0.0), axis=1, keepdims=True)
        spare = put_pieces(jnp.zeros((length, 128), jnp.bfloat16), -delta, lane)
        ga[h] = jnp.where(mine, grad_ref[...], spare)
    for kb in range(count):
        keys = slice(kb * BLK, kb * BLK + BLK)
        low, high = window_of(kb, count)
        rows = slice(low * BLK, high * BLK)
        offset = middle - kb * BLK
        cut = slice(offset + low * BLK, offset + high * BLK)
        dks, dvs = [], []
        for h in range(2):
            s = dot_nt(ka[h, keys, :], qa[h, rows, :]) + strip[h, :, cut]
            p = jnp.exp(s)
            ds = p * dot_nt(va[h, keys, :], ga[h, rows, :])
            rel[h, :, cut] += ds
            p = p.astype(jnp.bfloat16)
            ds = ds.astype(jnp.bfloat16)
            dvs.append(dot_nn(p, ga[h, rows, :]))
            dks.append(dot_nn(ds, qa[h, rows, :]))
            dq_acc[h, :, rows] += dot_tn(ka[h, keys, :], ds)
        grads_ref[1, keys, :] = jnp.where(left, dks[0], dks[1]).astype(jnp.bfloat16)
        grads_ref[2, keys, :] = jnp.where(left, dvs[0], dvs[1]).astype(jnp.bfloat16)
    row = lax.broadcasted_iota(jnp.int32, (128, 1), 0)
    dq = jnp.where(row < 64, dq_acc[0], dq_acc[1]).T
    grads_ref[0] = (dq * 0.125).astype(jnp.bfloat16)
    for h in range(2):
        out = []
        for place in range(5):
            start = middle + (2 - place) * BLK
            if place == 0:
                far = rel[h, :, middle + 2 * BLK :]
                summed = jnp.sum(jnp.sum(far, axis=0, keepdims=True).reshape(-1, BLK), axis=0, keepdims=True)
                out.append(jnp.concatenate([summed, jnp.zeros_like(summed)], axis=1))
            elif place == 4:
                far = rel[h, :, : middle - BLK]
                summed = jnp.sum(jnp.sum(far, axis=0, keepdims=True).reshape(-1, BLK), axis=0, keepdims=True)
                out.append(jnp.concatenate([summed, jnp.zeros_like(summed)], axis=1))
            else:
                out.append(diagonal_sums(rel[h, :, start : start + BLK]))
        rel_ref[h] = jnp.concatenate(out + [jnp.zeros((3, 2 * BLK), jnp.float32)], axis=0)


def attention_forward(line, qkv, aug_q, aug_k, table):
    _, length, width = qkv.shape
    col = pl.BlockSpec((length, 128), lambda p: (0, p))
    buf = pltpu.VMEM((2, length, 128), jnp.bfloat16)
    return launch(
        line, forward_kernel, (qkv, qkv, qkv, aug_q, aug_k, table),
        [
            pl.BlockSpec((None, length, 128), lambda p: (0, 0, p)),
            pl.BlockSpec((None, length, 128), lambda p: (1, 0, p)),
            pl.BlockSpec((None, length, 128), lambda p: (2, 0, p)),
            fixed(aug_q), fixed(aug_k),
            pl.BlockSpec((None, 2, table.shape[2]), lambda p: (p, 0, 0)),
        ],
        (bf16(length, width), f32(length, width)), (col, col), (width // 128,),
        "attention_forward",
        scratch=[pltpu.VMEM((2, BLK, 2 * length - BLK), jnp.float32), buf, buf],
    )


def attention_backward(line, qkv, mixed, grad_mixed, lse, aug_q, aug_k, table):
    _, length, width = qkv.shape
    col = pl.BlockSpec((length, 128), lambda p: (0, p))
    buf = pltpu.VMEM((2, length, 128), jnp.bfloat16)
    strip = pltpu.VMEM((2, BLK, 2 * length - BLK), jnp.float32)
    return launch(
        line, backward_kernel,
        (qkv, qkv, qkv, mixed, grad_mixed, lse, aug_q, aug_k, table),
        [
            pl.BlockSpec((None, length, 128), lambda p: (0, 0, p)),
            pl.BlockSpec((None, length, 128), lambda p: (1, 0, p)),
            pl.BlockSpec((None, length, 128), lambda p: (2, 0, p)),
            col, col, col, fixed(aug_q), fixed(aug_k),
            pl.BlockSpec((None, 2, table.shape[2]), lambda p: (p, 0, 0)),
        ],
        (bf16(3, length, width), f32(width // 64, 8, 2 * BLK)),
        (
            pl.BlockSpec((3, length, 128), lambda p: (0, 0, p)),
            pl.BlockSpec((2, 8, 2 * BLK), lambda p: (p, 0, 0)),
        ),
        (width // 128,), "attention_backward",
        scratch=[strip, strip, buf, buf, buf, buf, pltpu.VMEM((2, 128, length), jnp.float32)],
    )


def bucket_choice(offsets, count):
    return (bucket_of(offsets)[:, None] == jnp.arange(count, dtype=jnp.int32)[None, :]).astype(jnp.float32)

def prepare(segments, rel_table):
    heads = rel_table.shape[1]
    offsets = jnp.arange(4 * BLK, dtype=jnp.int32) - 2 * BLK
    tables = []
    for sign in (1, -1):
        choose = bucket_choice(sign * offsets, rel_table.shape[0])
        table = lax.dot_general(rel_table, choose, (((0,), (1,)), ((), ())), precision=lax.Precision.HIGHEST)
        tables.append(table.reshape(heads // 2, 2, 4 * BLK))
    lane = (jnp.arange(128, dtype=jnp.int32) % 64)[None, :]
    row = segments.reshape(-1)[:, None]
    same = lane == row
    aug_q = jnp.where(jnp.logical_or(same, lane >= 8), 0.0, NEG).astype(jnp.bfloat16)
    aug_k = jnp.where(jnp.logical_or(same, jnp.logical_and(lane >= 8, lane < 11)), 1.0, 0.0).astype(jnp.bfloat16)
    return aug_q, aug_k, tables[0], tables[1]

def rel_gradient(rel, count):
    lane = jnp.arange(2 * BLK, dtype=jnp.int32)
    parts = []
    for place in range(5):
        if place == 0:
            offset = jnp.full((2 * BLK,), -600, jnp.int32)
        elif place == 4:
            offset = jnp.full((2 * BLK,), 600, jnp.int32)
        else:
            offset = BLK * (place - 2) - jnp.where(lane < BLK, lane, lane - 2 * BLK)
        parts.append(bucket_choice(offset, count))
    choose = jnp.concatenate(parts + [jnp.zeros((3 * 2 * BLK, count), jnp.float32)], axis=0)
    flat = rel.reshape(rel.shape[0], -1)
    return lax.dot_general(choose, flat, (((0,), (1,)), ((), ())), precision=lax.Precision.HIGHEST)


def iota(shape, axis):
    return lax.broadcasted_iota(jnp.int32, shape, axis)


def as_bf16(flag):
    return jnp.where(flag, 1.0, 0.0).astype(jnp.bfloat16)


def slots_kernel(owners, capacity, shift, place_ref, kind_ref, index_ref, coords_ref,
                 meta_ref, keys_ref, text_ref):
    tokens = place_ref.shape[1]
    place = place_ref[...]
    text = kind_ref[...] == 1
    owner = jnp.right_shift(place, shift)
    position = jnp.bitwise_and(place, (1 << shift) - 1)
    rows = owners + 16
    row = iota((rows, tokens), 0)
    member = jnp.logical_or(row == owner, jnp.logical_and(row == owners, text))
    upto = as_bf16(iota((tokens, tokens), 0) <= iota((tokens, tokens), 1))
    counts = dot_nn(as_bf16(member), upto)
    rank = jnp.sum(jnp.where(row == owner, counts, 0.0), axis=0, keepdims=True)
    rank = rank.astype(jnp.int32) - 1
    text_rank = jnp.where(text, counts[owners : owners + 1].astype(jnp.int32) - 1, 0)
    slot = owner * capacity + rank
    index = index_ref[...]
    coords = coords_ref[...]
    low = jnp.bitwise_and(coords, 3)
    high = jnp.right_shift(coords, 2)
    meta = jnp.concatenate(
        [
            kind_ref[...] + 1,
            jnp.right_shift(position, 2), jnp.bitwise_and(position, 3),
            high, low,
            jnp.right_shift(index, 4), jnp.bitwise_and(index, 15),
            jnp.right_shift(text_rank, 2), jnp.bitwise_and(text_rank, 3),
            jnp.zeros_like(index),
        ],
        axis=0,
    ).astype(jnp.float32).astype(jnp.bfloat16)
    slots = meta_ref.shape[1]
    for start in range(0, slots, 512):
        pick = as_bf16(iota((512, tokens), 0) + start == slot)
        meta_ref[:, start : start + 512] = dot_nt(meta, pick).astype(jnp.bfloat16)
        down = dot_nt(pick, meta)
        index = down[:, 11:12] * 16.0 + down[:, 12:13]
        rank = down[:, 13:14] * 4.0 + down[:, 14:15] + float(tokens - text_ref.shape[1])
        key = jnp.where(down[:, 0:1] > 1.5, rank, jnp.where(down[:, 0:1] > 0.5, index, -1.0))
        keys_ref[start : start + 512, :] = jnp.broadcast_to(key.astype(jnp.int32), (512, 8))
    texts = text_ref.shape[1]
    chosen = as_bf16(jnp.logical_and(iota((texts, tokens), 0) == text_rank, text))
    found = dot_nt(meta, chosen)
    text_ref[...] = jnp.broadcast_to(
        (found[11:12] * 16.0 + found[12:13]).astype(jnp.int32), text_ref.shape
    )


def find_slots(line, owners, capacity, shift, placing, src_kind, src_index, coords, texts):
    slots = owners * capacity
    operands = (placing.reshape(1, -1), src_kind.reshape(1, -1), src_index.reshape(1, -1), coords)
    shapes = (bf16(16, slots), i32(slots, 8), i32(8, texts))
    return launch(
        line, partial(slots_kernel, owners, capacity, shift), operands,
        [fixed(value) for value in operands], shapes, [fixed(value) for value in shapes], (1,),
        "find_slots",
    )


def unpack_kernel(key_ref, rows_ref, index_ref, out_ref):
    texts, tokens = index_ref.shape[1], rows_ref.shape[1]
    count, width = rows_ref.shape[0], out_ref.shape[1]
    total = None
    small = None
    for d in range(count):
        pick = as_bf16(iota((texts, tokens), 0) == key_ref[d : d + 1, :])
        part = dot_nn(pick, rows_ref[d])
        total = part if total is None else total + part
        part = join_small(rows_ref[d, tokens - 16 :, :])
        small = part if small is None else small + part
    out_ref[:texts, :] = total.astype(jnp.bfloat16)
    index = index_ref[...]
    row = iota((16, texts), 0)
    high = jnp.broadcast_to(jnp.right_shift(index[0:1], 4), (16, texts))
    low = jnp.broadcast_to(jnp.bitwise_and(index[0:1], 15), (16, texts))
    index = jnp.where(row == 0, high, jnp.where(row == 1, low, 0)).astype(jnp.float32)
    index = jnp.concatenate([index, jnp.zeros((16, width - texts), jnp.float32)], axis=1)
    out_ref[texts : texts + 16, :] = index.astype(jnp.bfloat16)
    out_ref[texts + 16 :, :] = split_small(small)


def unpack_text(line, keys, rows, index):
    width = rows.shape[2]
    shape = bf16(index.shape[1] + 32, width)
    return launch(
        line, unpack_kernel, (keys, rows, index), [fixed(keys), fixed(rows), fixed(index)],
        (shape,), (fixed(shape),), (1,), "unpack_text",
    )[0]


def pack_kernel(key_ref, patch_ref, text_ref, *refs):
    out_ref = refs[len(refs) // 2]
    size, patches, texts = out_ref.shape[0], patch_ref.shape[0], text_ref.shape[0]
    key = key_ref[:, 0:1]
    out = dot_nn(as_bf16(iota((size, patches), 1) == key), patch_ref[...])
    out = out + dot_nn(as_bf16(iota((size, texts), 1) + patches == key), text_ref[...])
    out_ref[...] = out.astype(jnp.bfloat16)

    @pl.when(pl.program_id(0) == 0)
    def _():
        for n in range(len(refs) // 2):
            refs[len(refs) // 2 + 1 + n][...] = refs[n][...]


def pack(line, keys, patches, text_rows, later):
    slots = keys.shape[0]
    width = patches.shape[1]
    return launch(
        line, pack_kernel, (keys, patches, text_rows) + later,
        [pl.BlockSpec((512, 8), lambda i: (i, 0)), fixed(patches), fixed(text_rows)]
        + [fixed(value) for value in later],
        (bf16(slots, width),) + later,
        (pl.BlockSpec((512, width), lambda i: (i, 0)),) + tuple(fixed(value) for value in later),
        (slots // 512,), "pack",
    )


def place_kernel(meta_ref, column_ref, row_ref, place_ref):
    slots, tokens = meta_ref.shape[1], row_ref.shape[1]
    meta = meta_ref[...]
    wide = meta.astype(jnp.float32)
    place = (wide[1:2] * 4.0 + wide[2:3]).astype(jnp.int32)
    place = jnp.where(wide[0:1] > 0.5, place, -1)
    place_ref[...] = jnp.broadcast_to(place, place_ref.shape)
    for start in range(0, tokens, 256):
        pick = as_bf16(iota((256, slots), 0) + start == place)
        down = dot_nt(pick, meta)
        values = [down[:, 0:1]] + [down[:, 3 + c : 4 + c] * 4.0 + down[:, 7 + c : 8 + c] for c in range(4)]
        lane = iota((256, 8), 1)
        block = jnp.zeros((256, 8), jnp.float32)
        for c in range(5):
            block = jnp.where(lane == c, values[c], block)
        column_ref[start : start + 256, :] = block.astype(jnp.int32)
        across = dot_nt(meta, pick)
        row_ref[:, start : start + 256] = jnp.concatenate(
            [across[0:1], across[3:7] * 4.0 + across[7:11], jnp.zeros((3, 256), jnp.float32)], axis=0
        ).astype(jnp.int32)


def place_meta(line, meta, tokens):
    shapes = (i32(tokens, 8), i32(8, tokens), i32(8, meta.shape[1]))
    return launch(
        line, place_kernel, (meta,), [fixed(meta)], shapes, [fixed(value) for value in shapes],
        (1,), "place_meta",
    )


def lookup_kernel(rows, fresh, side, mine_ref, other_ref, table_ref, *refs):
    width = table_ref.shape[2]
    outs = refs[-2:]
    entries = table_ref.shape[0] * rows
    for n, coords in enumerate((mine_ref, other_ref)):
        total = jnp.zeros(outs[n].shape, jnp.float32) if fresh else refs[n][...]
        for k in range(2):
            key = jnp.where(side[0] == 0, coords[:, k + 1 : k + 2], coords[:, k + 3 : k + 4])
            pick = as_bf16(iota((total.shape[0], entries), 1) == key)
            table = table_ref[:, k * rows : k * rows + rows, :].reshape(entries, width)
            total = total + dot_nn(pick, table)
        outs[n][...] = total


def layout_lookup(line, side, mine, other, columns, rows, sums=()):
    tokens = mine.shape[0]
    width = columns.shape[2]
    column = pl.BlockSpec((256, 8), lambda i, s: (i, 0))
    out = pl.BlockSpec((256, width), lambda i, s: (i, 0))
    return launch(
        line, partial(lookup_kernel, rows, not sums), (mine, other, columns, *sums),
        [column, column, fixed(columns)] + [out] * len(sums),
        (f32(tokens, width), f32(tokens, width)), (out, out), (tokens // 256,), "layout_lookup",
        scalars=(side,),
    )


def embed_kernel(place_ref, column_ref, arrived_ref, own_ref, got_ref, half_ref, project_ref,
                 gain_ref, weight_ref, visual_ref, packed_ref, normed_ref, out_ref):
    rows, slots = packed_ref.shape[0], arrived_ref.shape[0]
    pick = as_bf16(iota((rows, slots), 0) + pl.program_id(0) * rows == place_ref[0:1, :])
    raw = dot_nn(pick, arrived_ref[...])
    narrow = raw.astype(jnp.bfloat16)
    kind = column_ref[:, 0:1]
    visual_ref[...] = jnp.where(kind == 1, raw, 0.0).T.astype(jnp.bfloat16)
    projected = dot_nn(narrow, project_ref[...])
    first = half_ref[0:1, 0:1] == 0
    own, got = own_ref[...], got_ref[...]
    layout = jnp.concatenate([jnp.where(first, own, got), jnp.where(first, got, own)], axis=1)
    embedded = jnp.where(kind == 2, raw, projected) + layout
    packed_ref[...] = embedded.astype(jnp.bfloat16)
    packed = packed_ref[...].astype(jnp.float32)
    scale = lax.rsqrt(jnp.mean(packed * packed, axis=-1, keepdims=True) + EPSILON)
    normed = packed * scale * gain_ref[0:1, :].astype(jnp.float32)
    normed_ref[...] = normed.T.astype(jnp.bfloat16)
    normed = normed.astype(jnp.bfloat16)
    for part in range(3):
        out_ref[part] = dot_nn(normed, weight_ref[part]).astype(jnp.bfloat16)


def embed(line, places, column, arrived, own, got, half, matrices, gains, tokens):
    width = arrived.shape[1]
    rows = 256
    wide = pl.BlockSpec((rows, width), lambda i: (i, 0))
    part = pl.BlockSpec((rows, own.shape[1]), lambda i: (i, 0))
    across = pl.BlockSpec((width, rows), lambda i: (0, i))
    return launch(
        line, embed_kernel, (places, column, arrived, own, got, half, matrices, gains, matrices),
        [
            fixed(places), pl.BlockSpec((rows, 8), lambda i: (i, 0)), fixed(arrived), part, part,
            fixed(half), pl.BlockSpec((None, width, width), lambda i: (3, 0, 0)), fixed(gains),
            pl.BlockSpec((3, width, width), lambda i: (0, 0, 0)),
        ],
        (bf16(width, tokens), bf16(tokens, width), bf16(width, tokens), bf16(3, tokens, width)),
        (across, wide, across, pl.BlockSpec((3, rows, width), lambda i: (0, i, 0))),
        (tokens // rows,), "embed",
    )


def input_grad_kernel(which, packed_ref, upper_ref, grads_ref, weight_ref, gain_ref,
                      out_ref, own_ref, other_ref, sum_ref):
    total = dot_nt(grads_ref[0], weight_ref[0])
    total = total + dot_nt(grads_ref[1], weight_ref[1])
    total = total + dot_nt(grads_ref[2], weight_ref[2])
    packed = packed_ref[...].astype(jnp.float32)
    scale = lax.rsqrt(jnp.mean(packed * packed, axis=-1, keepdims=True) + EPSILON)
    unit = packed * scale
    back = total * gain_ref[0:1, :].astype(jnp.float32)
    back = scale * (back - unit * jnp.mean(back * unit, axis=-1, keepdims=True))
    back = back + upper_ref[...]
    out_ref[...] = back.astype(jnp.bfloat16)
    put_halves(which, back, own_ref, other_ref)

    @pl.when(pl.program_id(0) == 0)
    def _():
        sum_ref[...] = jnp.zeros_like(sum_ref)

    sum_ref[0:1, :] += jnp.sum(total * unit, axis=0, keepdims=True)


def input_grad(line, which, packed, upper, grads, matrices, gains):
    tokens, width = packed.shape
    rows = 256
    half = width // 2
    wide = pl.BlockSpec((rows, width), lambda i, w: (i, 0))
    part = pl.BlockSpec((rows, half), lambda i, w: (i, 0))
    return launch(
        line, input_grad_kernel, (packed, upper, grads, matrices, gains),
        [
            wide, wide, pl.BlockSpec((3, rows, width), lambda i, w: (0, i, 0)),
            pl.BlockSpec((3, width, width), lambda i, w: (0, 0, 0)), fixed(gains),
        ],
        (bf16(tokens, width), bf16(tokens, half), bf16(tokens, half), f32(8, width)),
        (wide, part, part, pl.BlockSpec((8, width), lambda i, w: (0, 0))),
        (tokens // rows,), "input_grad", scalars=(which,),
    )


def split_small(small):
    parts = [part.astype(jnp.float32) for part in pieces(small)]
    pad = jnp.zeros((16 - 3 * small.shape[0], small.shape[1]), jnp.float32)
    return jnp.concatenate(parts + [pad], axis=0).astype(jnp.bfloat16)


def join_small(rows):
    rows = rows[:9].astype(jnp.float32)
    return rows[0:3] + rows[3:6] + rows[6:9]


def return_kernel(place_ref, rows_ref, small_ref, out_ref):
    slots = place_ref.shape[0]
    devices, capacity = out_ref.shape[0], out_ref.shape[1] - 16
    pick = as_bf16(iota((slots, rows_ref.shape[0]), 1) == place_ref[...])
    rows = dot_nn(pick, rows_ref[...]).astype(jnp.bfloat16)
    small = split_small(small_ref[0:3, :])
    for d in range(devices):
        out_ref[d, :capacity, :] = rows[d * capacity : d * capacity + capacity]
        out_ref[d, capacity:, :] = small


def return_rows(line, places, rows, small, capacity):
    count = places.shape[0] // capacity
    width = rows.shape[1]
    step = max(1, min(count, 512 // capacity))
    return launch(
        line, return_kernel, (places, rows, small),
        [pl.BlockSpec((step * capacity, 1), lambda i: (i, 0)), fixed(rows), fixed(small)],
        (bf16(count, capacity + 16, width),),
        (pl.BlockSpec((step, capacity + 16, width), lambda i: (i, 0, 0)),), (count // step,),
        "return_rows",
    )[0]


def layout_grad_kernel(side, mine_ref, other_ref, first_ref, second_ref, keep_ref, give_ref):
    pair = pl.program_id(0)
    shards, rows, width = keep_ref.shape
    entries = shards * rows
    table = 2 * jnp.where(pair < 2, 1 - side[0], side[0]) + jnp.bitwise_and(pair, 1)
    total = jnp.zeros((entries, width), jnp.float32)
    for coords, grads in ((mine_ref, first_ref), (other_ref, second_ref)):
        tokens = grads.shape[0]
        key = coords[pl.ds(table + 1, 1), :]
        pick = as_bf16(iota((entries, tokens), 0) + pl.program_id(1) * entries == key)
        total = total + dot_nn(pick, grads[...])
    total = total.reshape(shards, rows, width).astype(jnp.bfloat16)

    @pl.when(pair < 2)
    def _():
        give_ref[...] = total

    @pl.when(pair >= 2)
    def _():
        keep_ref[...] = total


def layout_grad(line, side, mine, other, first, second, shards, rows):
    width = first.shape[1]
    step = max(1, min(shards, 512 // rows))
    last = shards // step - 1
    block = (step, None, rows, width)
    shape = bf16(shards, 2, rows, width)
    return launch(
        line, layout_grad_kernel, (mine, other, first, second),
        [fixed(mine), fixed(other), fixed(first), fixed(second)], (shape, shape),
        (
            pl.BlockSpec(
                block, lambda t, i, s: (jnp.where(t < 2, 0, i), jnp.maximum(t - 2, 0), 0, 0)
            ),
            pl.BlockSpec(
                block, lambda t, i, s: (jnp.where(t < 2, i, last), jnp.minimum(t, 1), 0, 0)
            ),
        ),
        (4, shards // step), "layout_grad", scalars=(side,),
    )


def patch_kernel(key_ref, rows_ref, weight_ref, grad_ref):
    patches, tokens = grad_ref.shape[0], rows_ref.shape[1]
    total = None
    for d in range(rows_ref.shape[0]):
        pick = as_bf16(iota((patches, tokens), 0) == key_ref[d : d + 1, :])
        part = dot_nn(pick, rows_ref[d])
        total = part if total is None else total + part
    grad_ref[...] = dot_nt(total.astype(jnp.bfloat16), weight_ref[...])


def patch_grads(line, keys, rows, matrices, patches):
    width = rows.shape[2]
    shape = f32(patches, width)
    return launch(
        line, patch_kernel, (keys, rows, matrices),
        [fixed(keys), fixed(rows), pl.BlockSpec((None, width, width), lambda i: (3, 0, 0))],
        (shape,), (fixed(shape),), (1,), "patch_grads",
    )[0]


def text_kernel(*refs):
    out_ref = refs[4]
    size = out_ref.shape[0]
    parts = []
    for rows_ref in refs[:4]:
        texts = rows_ref.shape[0] - 32
        index = rows_ref[texts : texts + 16, :texts].astype(jnp.float32)
        key = (index[0:1] * 16.0 + index[1:2]).astype(jnp.int32)
        place = iota((size, texts), 0) + pl.program_id(0) * size
        parts.append(dot_nn(as_bf16(place == key), rows_ref[:texts, :]))
    out_ref[...] = (parts[0] + parts[1]) + (parts[2] + parts[3])


def text_grads(line, rows, entries):
    width = rows[0].shape[1]
    size = 512
    return launch(
        line, text_kernel, rows, [fixed(value) for value in rows],
        (f32(entries, width),), (pl.BlockSpec((size, width), lambda i: (i, 0)),),
        (pl.cdiv(entries, size),), "text_grads",
    )[0]


def feed_forward_kernel(core, packed_ref, mixed_ref, grad_ref, own_ref, other_ref, in_ref, down_ref,
                        gain_ref, result_ref, active_ref, hidden_ref, normed_ref, turned_ref, upper_ref,
                        branch_ref, back_ref, sum_ref):
    own, other = own_ref[...], other_ref[...]
    first = core[0] == 0
    mix = jnp.concatenate([jnp.where(first, own, other), jnp.where(first, other, own)], axis=1)
    attended = packed_ref[...].astype(jnp.float32) + dot_nn(mixed_ref[...], mix)
    turned_ref[...] = mixed_ref[...].astype(jnp.float32).T.astype(jnp.bfloat16)
    scale = lax.rsqrt(jnp.mean(attended * attended, axis=-1, keepdims=True) + EPSILON)
    unit = attended * scale
    gain = gain_ref[0:1, :].astype(jnp.float32)
    normed = unit * gain
    normed_ref[...] = normed.T.astype(jnp.bfloat16)
    normed = normed.astype(jnp.bfloat16)
    out_grad = grad_ref[...]
    result = attended
    back = jnp.zeros_like(attended)
    width = attended.shape[1]
    for part in range(in_ref.shape[0]):
        cut = slice(part * width, part * width + width)
        hidden = dot_nn(normed, in_ref[part])
        square = hidden * hidden
        tanh = jnp.tanh(hidden * (RATE + RATE * 0.044715 * square))
        half = 0.5 + 0.5 * tanh
        active = hidden * half
        active_ref[cut, :] = active.T.astype(jnp.bfloat16)
        active = active.astype(jnp.bfloat16)
        slope = half + hidden * half * (1.0 - tanh) * (RATE + 3.0 * 0.044715 * RATE * square)
        result = result + dot_nn(active, down_ref[cut, :])
        grad_hidden = (dot_nt(out_grad, down_ref[cut, :]) * slope).astype(jnp.bfloat16)
        hidden_ref[:, cut] = grad_hidden
        back = back + dot_nt(grad_hidden, in_ref[part])
    result_ref[...] = result.astype(jnp.bfloat16)

    @pl.when(pl.program_id(0) == 0)
    def _():
        sum_ref[...] = jnp.zeros_like(sum_ref)

    sum_ref[0:1, :] += jnp.sum(back * unit, axis=0, keepdims=True)
    back = back * gain
    back = scale * (back - unit * jnp.mean(back * unit, axis=-1, keepdims=True))
    back = back + out_grad.astype(jnp.float32)
    upper_ref[...] = back
    branch = back.astype(jnp.bfloat16)
    branch_ref[...] = branch
    back_ref[...] = dot_nt(branch, mix).astype(jnp.bfloat16)


def feed_forward(line, core, packed, mixed, out_grad, mix_own, mix_other, full_in, full_down, gains):
    tokens, width = packed.shape
    hidden = full_down.shape[0]
    rows = 256
    wide = pl.BlockSpec((rows, width), lambda i, c: (i, 0))
    tall = pl.BlockSpec((rows, hidden), lambda i, c: (i, 0))
    across = pl.BlockSpec((width, rows), lambda i, c: (0, i))
    narrow, turned = bf16(tokens, width), bf16(width, tokens)
    operands = (packed, mixed, out_grad, mix_own, mix_other, full_in, full_down, gains)
    return launch(
        line, feed_forward_kernel, operands,
        [wide, wide, wide] + [fixed(value) for value in operands[3:]],
        (
            narrow, bf16(hidden, tokens), bf16(tokens, hidden), turned, turned,
            f32(tokens, width), narrow, narrow, f32(8, width),
        ),
        (
            wide, pl.BlockSpec((hidden, rows), lambda i, c: (0, i)), tall, across, across,
            wide, wide, wide, pl.BlockSpec((8, width), lambda i, c: (0, 0)),
        ),
        (tokens // rows,), "feed_forward", scalars=(core,),
    )


def put_halves(which, total, keep_ref, give_ref):
    half = total.shape[1] // 2
    first, second = total[:, :half], total[:, half:]
    mine = which[0] == 0
    keep_ref[...] = jnp.where(mine, first, second).astype(jnp.bfloat16)
    give_ref[...] = jnp.where(mine, second, first).astype(jnp.bfloat16)


def contract_halves_kernel(which, left_ref, right_ref, keep_ref, give_ref):
    put_halves(which, dot_nn(left_ref[...], right_ref[...]), keep_ref, give_ref)


def contract_halves(line, which, left, right):
    count, tokens = left.shape
    width = right.shape[1]
    size, half = min(count, width), width // 2
    out = pl.BlockSpec((size, half), lambda i, w: (i, 0))
    shape = bf16(count, half)
    return launch(
        line, contract_halves_kernel, (left, right),
        [pl.BlockSpec((size, tokens), lambda i, w: (i, 0)), fixed(right)],
        (shape, shape), (out, out), (count // size,), "contract_halves", scalars=(which,),
    )


def contract_quarters_kernel(which, left_ref, right_ref, keep_ref, give_ref):
    del which
    total = dot_nn(left_ref[...], right_ref[...])
    shards, _, rows, half = keep_ref.shape

    def put(out_ref):
        for d in range(shards):
            for h in range(2):
                part = total[d * rows : d * rows + rows, h * half : h * half + half]
                out_ref[d, h] = part.astype(jnp.bfloat16)

    @pl.when(pl.program_id(0) < 2)
    def _():
        put(give_ref)

    @pl.when(pl.program_id(0) >= 2)
    def _():
        put(keep_ref)


def contract_quarters(line, which, left, right, shards):
    count, tokens = left.shape
    quarter = right.shape[1] // 4
    block = (shards, 2, count // shards, quarter // 2)
    shape = bf16(2, *block)

    def column(i, w):
        return (0, jnp.where(i < 2, 2 * i + 1 - w[0], 2 * (i - 2) + w[0]))

    return launch(
        line, contract_quarters_kernel, (left, right),
        [fixed(left), pl.BlockSpec((tokens, quarter), column)], (shape, shape),
        (
            pl.BlockSpec((None,) + block, lambda i, w: (jnp.maximum(i - 2, 0), 0, 0, 0, 0)),
            pl.BlockSpec((None,) + block, lambda i, w: (jnp.minimum(i, 1), 0, 0, 0, 0)),
        ),
        (4,), "contract_quarters", scalars=(which,),
    )


def square_kernel(which, normed_ref, grads_ref, visual_ref, packed_ref, keep_ref, give_ref):
    shards, rows, half = keep_ref.shape

    def put(total):
        mine = which[0] == 0
        for d in range(shards):
            part = total[d * rows : d * rows + rows]
            first, second = part[:, :half], part[:, half:]
            keep_ref[d] = jnp.where(mine, first, second).astype(jnp.bfloat16)
            give_ref[d] = jnp.where(mine, second, first).astype(jnp.bfloat16)

    @pl.when(pl.program_id(0) < 3)
    def _():
        put(dot_nn(normed_ref[...], grads_ref[...]))

    @pl.when(pl.program_id(0) == 3)
    def _():
        put(dot_nn(visual_ref[...], packed_ref[...]))


def square_grads(line, which, normed, grads, visual, grad_packed, shards):
    width, tokens = normed.shape
    rows, half = width // shards, width // 2
    out = pl.BlockSpec((shards, None, None, rows, half), lambda m, w: (0, m // 2, m % 2, 0, 0))
    shape = bf16(shards, 2, 2, rows, half)
    return launch(
        line, square_kernel, (normed, grads, visual, grad_packed),
        [
            fixed(normed),
            pl.BlockSpec((None, tokens, width), lambda m, w: (jnp.minimum(m, 2), 0, 0)),
            fixed(visual), fixed(grad_packed),
        ],
        (shape, shape), (out, out), (4,), "square_grads", scalars=(which,),
    )


def fold_kernel(bit, value_ref, got_ref, keep_ref, give_ref):
    del bit
    total = value_ref[...].astype(jnp.float32) + got_ref[...].astype(jnp.float32)

    @pl.when(pl.program_id(0) == 0)
    def _():
        give_ref[...] = total.astype(give_ref.dtype)

    @pl.when(pl.program_id(0) == 1)
    def _():
        keep_ref[...] = total.astype(keep_ref.dtype)


def fold(line, bit, value, got):
    a, _, b, rows, width = value.shape
    step = a
    while step > 1 and step * b * rows * width * value.dtype.itemsize > 1_600_000:
        step //= 2
    count = a // step
    source = pl.BlockSpec(
        (step, None, b, rows, width), lambda n, i, s: (i, jnp.where(n == 0, 1 - s[0], s[0]), 0, 0, 0)
    )
    block = (step, b, rows, width)
    shape = jax.ShapeDtypeStruct((a, b, rows, width), value.dtype)
    return launch(
        line, fold_kernel, (value, got), [source, source], (shape, shape),
        (
            pl.BlockSpec(block, lambda n, i, s: (jnp.where(n == 0, 0, i), 0, 0, 0)),
            pl.BlockSpec(block, lambda n, i, s: (jnp.where(n == 0, i, count - 1), 0, 0, 0)),
        ),
        (2, count), "fold", scalars=(bit,),
    )


def add_kernel(value_ref, got_ref, out_ref):
    total = value_ref[...].astype(jnp.float32) + got_ref[...].astype(jnp.float32)
    out_ref[...] = total.astype(out_ref.dtype)


def add(line, value, got):
    shape = jax.ShapeDtypeStruct(value.shape, value.dtype)
    return launch(
        line, add_kernel, (value, got), [fixed(value), fixed(got)], (shape,), (fixed(shape),),
        (1,), "add",
    )[0]


def rows_fold_kernel(side, down_ref, down_got_ref, mix_ref, mix_got_ref, keep_ref, give_ref):
    del side
    down = down_ref[...].astype(jnp.float32) + down_got_ref[...].astype(jnp.float32)
    mix = mix_ref[...].astype(jnp.float32) + mix_got_ref[...].astype(jnp.float32)
    total = jnp.concatenate([down, mix], axis=1).astype(jnp.bfloat16)

    @pl.when(pl.program_id(0) == 0)
    def _():
        give_ref[...] = total

    @pl.when(pl.program_id(0) == 1)
    def _():
        keep_ref[...] = total


def rows_fold(line, side, down, down_got, mix, mix_got):
    parts, _, rows, width = down.shape
    extra = mix.shape[2]
    step = max(1, parts // 2)

    def source(count):
        return pl.BlockSpec(
            (step, None, count, width), lambda n, i, s: (i, jnp.where(n == 0, 1 - s[0], s[0]), 0, 0)
        )

    shape = bf16(parts, rows + extra, width)
    block = (step, rows + extra, width)
    last = parts // step - 1
    return launch(
        line, rows_fold_kernel, (down, down_got, mix, mix_got),
        [source(rows), source(rows), source(extra), source(extra)], (shape, shape),
        (
            pl.BlockSpec(block, lambda n, i, s: (jnp.where(n == 0, 0, i), 0, 0)),
            pl.BlockSpec(block, lambda n, i, s: (jnp.where(n == 0, i, last), 0, 0)),
        ),
        (2, parts // step), "rows_fold", scalars=(side,),
    )


def stack_kernel(bit, value_ref, got_ref, out_ref):
    del bit

    @pl.when(pl.program_id(0) == 0)
    def _():
        out_ref[...] = value_ref[...]

    @pl.when(pl.program_id(0) == 1)
    def _():
        out_ref[...] = got_ref[...]


def stack(line, bit, value, got, waits=()):
    a, rows, width = value.shape
    return launch(
        line, stack_kernel, (value, got), [fixed(value), fixed(got)],
        (jax.ShapeDtypeStruct((a, 2, rows, width), value.dtype),),
        (
            pl.BlockSpec(
                (a, None, rows, width), lambda n, s: (0, jnp.where(n == 0, s[0], 1 - s[0]), 0, 0)
            ),
        ),
        (2,), "stack", scalars=(bit,), waits=waits,
    )[0]


def split_stack_kernel(parts, bit, value_ref, got_ref, *outs):
    del bit

    def put(source_ref):
        start = 0
        for rows, out_ref in zip(parts, outs):
            out_ref[...] = source_ref[:, start : start + rows, :]
            start += rows

    @pl.when(pl.program_id(0) == 0)
    def _():
        put(value_ref)

    @pl.when(pl.program_id(0) == 1)
    def _():
        put(got_ref)


def split_stack(line, bit, value, got, parts):
    a, _, width = value.shape
    return launch(
        line, partial(split_stack_kernel, parts), (value, got), [fixed(value), fixed(got)],
        [bf16(a, 2, rows, width) for rows in parts],
        [
            pl.BlockSpec(
                (a, None, rows, width), lambda n, s: (0, jnp.where(n == 0, s[0], 1 - s[0]), 0, 0)
            )
            for rows in parts
        ],
        (2,), "split_stack", scalars=(bit,),
    )


def both_sides(line, side, value, got):
    return stack(line, side, value, got)


def arrange_kernel(me, *refs):
    del me
    for n in range(4):

        @pl.when(pl.program_id(0) == n)
        def _():
            refs[4][...] = refs[n][...]


def arrange(line, me, values):
    shape = values[0].shape
    return launch(
        line, arrange_kernel, tuple(values), [fixed(value) for value in values],
        (bf16(4, *shape),),
        (pl.BlockSpec((None,) + shape, lambda n, s: (jnp.bitwise_xor(n, s[0]), 0, 0)),),
        (4,), "arrange", scalars=(me,),
    )[0]


def assemble_forward_kernel(me, *refs):
    down_ref, mix_ref, in_ref = refs[4:]
    half = refs[0].shape[1]
    for n in range(4):
        device = jnp.bitwise_xor(me[0], n)
        side = jnp.right_shift(device, 1)
        column = pl.ds(pl.multiple_of(jnp.bitwise_and(device, 1) * half, 128), half)
        start = 0
        for out_ref in (down_ref, mix_ref):
            rows = out_ref.shape[1]
            out_ref[side, :, column] = refs[n][start : start + rows, :].astype(jnp.float32)
            start += rows
        rows = in_ref.shape[0]
        for h in range(2):
            part = refs[n][start + h * rows : start + h * rows + rows, :].astype(jnp.float32)
            in_ref[:, pl.ds(pl.multiple_of((2 * device + h) * half, 128), half)] = part


def assemble_forward(line, me, values, down_rows, mix_rows, shard_rows):
    half = values[0].shape[1]
    shapes = (f32(2, down_rows, 2 * half), f32(2, mix_rows, 2 * half), f32(shard_rows, 8 * half))
    return launch(
        line, assemble_forward_kernel, tuple(values), [fixed(value) for value in values],
        shapes, [fixed(value) for value in shapes], (1,), "assemble_forward", scalars=(me,),
    )


def assemble_backward_kernel(me, *refs):
    layout_ref, qkv_ref, project_ref = refs[4:]
    half = refs[0].shape[1]
    layout_rows, rows = layout_ref.shape[1], project_ref.shape[0]
    for n in range(4):
        device = jnp.bitwise_xor(me[0], n)
        side = jnp.right_shift(device, 1)
        column = pl.ds(pl.multiple_of(jnp.bitwise_and(device, 1) * half, 128), half)
        for k in range(2):
            start = k * layout_rows
            layout_ref[2 * side + k, :, column] = refs[n][start : start + layout_rows, :].astype(
                jnp.float32
            )
        start = 2 * layout_rows
        qkv_ref[2 * side, :, column] = refs[n][start : start + rows, :].astype(jnp.float32)
        matrix = refs[n][start + rows : start + 2 * rows, :].astype(jnp.float32)

        @pl.when(side == 0)
        def _():
            qkv_ref[1, :, column] = matrix

        @pl.when(side == 1)
        def _():
            project_ref[:, column] = matrix


def assemble_backward(line, me, values, layout_rows, rows):
    half = values[0].shape[1]
    shapes = (f32(4, layout_rows, 2 * half), f32(3, rows, 2 * half), f32(rows, 2 * half))
    return launch(
        line, assemble_backward_kernel, tuple(values), [fixed(value) for value in values],
        shapes, [fixed(value) for value in shapes], (1,), "assemble_backward", scalars=(me,),
    )


def swap(value, axis, bit):
    count = lax.axis_size(axis)
    return lax.ppermute(value, axis, [(i, i ^ bit) for i in range(count)])


def bit_of(axis, bit):
    return jnp.bitwise_and(lax.axis_index(axis), bit) != 0


def bit_index(axis, bit):
    return bit_of(axis, bit).astype(jnp.int32).reshape(1)


class Gather:
    def __init__(self, line, value):
        self.line = line
        self.value = value[None]
        self.bit = lax.axis_size("dp") // 2
        self.got = swap(self.value, "dp", self.bit)

    def step(self, waits=()):
        rows, width = self.value.shape[1:]
        value = stack(self.line, bit_index("dp", self.bit), self.value, self.got, waits)
        self.value = value.reshape(-1, rows, width)
        self.bit //= 2
        self.got = swap(self.value, "dp", self.bit)

    def finish(self, parts):
        while self.bit > 1:
            self.step()
        values = split_stack(self.line, bit_index("dp", 1), self.value, self.got, parts)
        return [value.reshape((-1,) + value.shape[2:]) for value in values]


def padded(value):
    return jnp.pad(value, ((0, -value.shape[0] % 16), (0, 0)))


class Sum:
    def __init__(self, line, bits, value, got):
        self.line, self.bits, self.value, self.got = line, list(bits), value, got
        self.done = False

    def step(self):
        if self.done:
            return
        rows, width = self.value.shape[-2:]
        if not self.bits:
            self.value = add(self.line, self.value.reshape(rows, width), self.got.reshape(rows, width))
            self.done = True
            return
        bit = self.bits.pop()
        shape = (-1, 2, 1, rows, width)
        value, give = fold(
            self.line, bit_index("dp", bit), self.value.reshape(shape), self.got.reshape(shape)
        )
        self.value, self.got = value, swap(give, "dp", bit)

    def finish(self):
        while not self.done:
            self.step()
        return self.value


def shards(
    patches,
    src_kind,
    src_index,
    layout_coords,
    placing,
    segments,
    text_table,
    layout_tables,
    patch_proj,
    rel_table,
    norm_gains,
    w_qkv,
    w_attn_out,
    w_ff_in,
    w_ff_out,
    out_grad,
):
    data_count = lax.axis_size("dp")
    tokens = placing.shape[0]
    capacity = 2 * tokens // data_count
    width = text_table.shape[1]
    half_width = width // 2
    texts = tokens - patches.shape[0]
    shift = tokens.bit_length() - 1
    shard_rows = w_attn_out.shape[0]
    layout_rows = layout_tables.shape[1]
    stream = lax.axis_index("stream")
    core = jnp.bitwise_and(stream, 1)
    side = jnp.right_shift(stream, 1)
    gain_count = norm_gains.shape[1]

    own_core, own_side = core.reshape(1), side.reshape(1)
    dp_bits = [1 << n for n in reversed(range(data_count.bit_length() - 1))]
    line = Line()

    def own_half(value):
        return lax.dynamic_slice_in_dim(value, core * half_width, half_width, axis=-1)

    in_quarter = lax.dynamic_index_in_dim(
        w_ff_in.reshape(shard_rows, 4, -1), stream, 1, keepdims=False
    )
    down_quarter = lax.dynamic_index_in_dim(
        w_ff_out.reshape(4, -1, width), stream, 0, keepdims=False
    )
    layout_part = own_half(
        lax.dynamic_slice_in_dim(layout_tables, side * 2, 2, axis=0)
    ).reshape(-1, half_width)
    mix_part = own_half(
        lax.dynamic_slice_in_dim(w_attn_out, side * (shard_rows // 2), shard_rows // 2, axis=0)
    )
    gain_part = jnp.pad(norm_gains, ((0, 0), (0, half_width - gain_count)))
    table_rows, mix_rows = layout_part.shape[0], mix_part.shape[0]
    square = jnp.concatenate([w_qkv, patch_proj[None]], axis=0)
    square = lax.dynamic_index_in_dim(square, stream, 0, keepdims=False)
    square = lax.all_gather(square, "dp", axis=0, tiled=True)
    square_got = swap(square, "stream", 2)
    mix_part, gain_part = padded(mix_part), padded(gain_part)
    columns = Gather(line, jnp.concatenate([layout_part, mix_part, gain_part], axis=0))
    full_in = lax.all_gather(in_quarter, ("stream", "dp"), axis=0, tiled=True)
    full_in = full_in.reshape(4, width, -1)

    meta, slot_keys, text_index = find_slots(
        line, data_count, capacity, shift, placing, src_kind, src_index, layout_coords, texts
    )
    arrived_meta = lax.all_to_all(
        meta.reshape(16, data_count, capacity), "dp", split_axis=1, concat_axis=1, tiled=True
    ).reshape(16, -1)
    column, across, place = place_meta(line, arrived_meta, tokens)
    column_other = swap(column, "stream", 1)
    across_other = column_other.T
    columns.step()
    columns.step(waits=(column_other,))
    tables, mix, gains = columns.finish((table_rows, mix_part.shape[0], gain_part.shape[0]))
    tables_got = swap(tables, "stream", 2)
    mix_got = swap(mix, "stream", 2)
    gains = gains[:, :2, :gain_count].transpose(1, 0, 2).reshape(2, width)
    text_rows = jnp.take(text_table, text_index[0], axis=0)
    send_rows, down_quarter = pack(line, slot_keys, patches, text_rows, (down_quarter,))
    arrived = lax.all_to_all(
        send_rows.reshape(data_count, capacity, width), "dp", split_axis=0, concat_axis=0, tiled=True
    ).reshape(-1, width)
    full_down = lax.all_gather(down_quarter, ("dp", "stream"), axis=0, tiled=True)
    sums = layout_lookup(line, own_side, column, column_other, tables, layout_rows)
    matrices = arrange(
        line, stream.reshape(1),
        (square, swap(square, "stream", 1), square_got, swap(square_got, "stream", 1)),
    )
    own_sum, other_sum = layout_lookup(
        line, 1 - own_side, column, column_other, tables_got, layout_rows, sums
    )
    got_sum = swap(other_sum, "stream", 1)
    half_index = jnp.broadcast_to(core, (8, 128)).astype(jnp.int32)
    visual, packed, normed_one, projections = embed(
        line, place, column, arrived, own_sum, got_sum, half_index, matrices, gains[:1], tokens
    )
    mix_own = both_sides(line, own_side, mix, mix_got)
    mix_own = mix_own[:, :, :mix_rows].reshape(width, half_width)
    mix_other = swap(mix_own, "stream", 1)
    aug_q, aug_k, table, mirrored = prepare(segments, rel_table)
    mixed, lse = attention_forward(line, projections, aug_q, aug_k, table)
    (
        result, active, grad_hidden, normed_two, turned, upper, grad_branch, grad_mixed,
        gain_two_sum,
    ) = feed_forward(
        line, own_core, packed, mixed, out_grad, mix_own, mix_other, full_in, full_down, gains[1:]
    )

    down_keep, down_give = contract_halves(line, own_core, active, out_grad)
    down_got = swap(down_give, "stream", 1)
    mix_keep, mix_give = contract_halves(line, own_core, turned, grad_branch)
    mix_got = swap(mix_give, "stream", 1)
    in_keep, in_give = contract_quarters(
        line, own_core, normed_two, grad_hidden, data_count
    )
    in_got = swap(in_give, "stream", 1)
    down_shape = (data_count, 2, down_keep.shape[0] // data_count // 2, half_width)
    mix_shape = (data_count, 2, mix_rows, half_width)
    rows_keep, rows_give = rows_fold(
        line, own_side, down_keep.reshape(down_shape), down_got.reshape(down_shape),
        mix_keep.reshape(mix_shape), mix_got.reshape(mix_shape),
    )
    rows_got = swap(rows_give, "stream", 2)
    in_shape = (data_count, 2, 2 * shard_rows, half_width)
    in_keep, in_give = fold(
        line, bit_index("dp", 1), in_keep.reshape(in_shape)[:, :, None],
        in_got.reshape(in_shape)[:, :, None],
    )
    in_got = swap(in_give, "dp", 1)

    qkv_grads, grad_rel = attention_backward(
        line, projections, mixed, grad_mixed, lse, aug_q, aug_k, mirrored
    )
    rows_shape = (data_count // 2, 2, 1) + rows_keep.shape[1:]
    rows_keep, rows_give = fold(
        line, bit_index("dp", 1), rows_keep.reshape(rows_shape), rows_got.reshape(rows_shape)
    )
    rows_got = swap(rows_give, "dp", 1)
    in_shape = (1, 2, data_count // 2, 2 * shard_rows, half_width)
    in_keep, in_give = fold(line, own_side, in_keep.reshape(in_shape), in_got.reshape(in_shape))
    in_got = swap(in_give, "stream", 2)
    grad_packed, own_columns, other_columns, gain_one_sum = input_grad(
        line, own_core, packed, upper, qkv_grads, matrices, gains[:1]
    )
    other_columns = swap(other_columns, "stream", 1)
    rows_shape = (data_count // 4, 2) + rows_keep.shape[-2:]
    in_shape = (data_count // 4, 2) + in_keep.shape[-2:]
    value, give = rows_fold(
        line, bit_index("dp", 2), rows_keep.reshape(rows_shape), rows_got.reshape(rows_shape),
        in_keep.reshape(in_shape), in_got.reshape(in_shape),
    )
    forward_sum = Sum(line, dp_bits[:-2], value, swap(give, "dp", 2))
    rel = rel_gradient(grad_rel, rel_table.shape[0])
    rel_row = jnp.pad(rel.reshape(1, -1), ((0, 0), (0, width - rel.size)))
    small = jnp.concatenate([gain_one_sum[:1], gain_two_sum[:1], rel_row], axis=0)
    returned = return_rows(
        line, place[:1].reshape(-1, 1), grad_packed, jnp.pad(small, ((0, 5), (0, 0))), capacity
    )
    came_back = lax.all_to_all(returned, "dp", split_axis=0, concat_axis=0, tiled=True)

    table_keep, table_give = layout_grad(
        line, own_side, across, across_other, own_columns, other_columns, data_count, layout_rows
    )
    table_got = swap(table_give, "stream", 2)
    square_keep, square_give = square_grads(
        line, own_core, normed_one, qkv_grads, visual, grad_packed, data_count
    )
    square_got = swap(square_give, "stream", 1)
    square_shape = (data_count, 2, 1, 2 * shard_rows, half_width)
    square_keep, square_give = fold(
        line, own_side, square_keep.reshape(square_shape), square_got.reshape(square_shape)
    )
    square_got = swap(square_give, "stream", 2)
    table_shape = (data_count // 2, 2, 1, table_rows, half_width)
    table_keep, table_give = fold(
        line, bit_index("dp", 1), table_keep.reshape(table_shape), table_got.reshape(table_shape)
    )
    table_got = swap(table_give, "dp", 1)

    def stream_group(value):
        across_sides = swap(value, "stream", 2)
        return (value, swap(value, "stream", 1), across_sides, swap(across_sides, "stream", 1))

    wide_meta = meta.astype(jnp.float32)
    slot_kind = wide_meta[:1]
    slot_index = (wide_meta[11:12] * 16.0 + wide_meta[12:13]).astype(jnp.int32)
    slot_text = (wide_meta[13:14] * 4.0 + wide_meta[14:15]).astype(jnp.int32)

    def slot_keys_of(kind, value):
        keys = jnp.where(slot_kind == kind, value, -1).reshape(data_count, capacity)
        return jnp.pad(keys, ((0, 0), (0, 16)), constant_values=-1)

    text_grad_rows = unpack_text(line, slot_keys_of(2.0, slot_text), came_back, text_index)
    rows_side = swap(text_grad_rows, "stream", 2)
    rows_core = swap(text_grad_rows, "stream", 1)
    square_shape = (data_count // 2, 2, 1, 2 * shard_rows, half_width)
    square_keep, square_give = fold(
        line, bit_index("dp", 1), square_keep.reshape(square_shape),
        square_got.reshape(square_shape),
    )
    square_got = swap(square_give, "dp", 1)
    forward_sum.step()
    rows_both = swap(rows_side, "stream", 1)
    table_shape = (data_count // 4, 2, table_rows, half_width)
    square_shape = (data_count // 4, 2, 2 * shard_rows, half_width)
    value, give = rows_fold(
        line, bit_index("dp", 2), table_keep.reshape(table_shape), table_got.reshape(table_shape),
        square_keep.reshape(square_shape), square_got.reshape(square_shape),
    )
    backward_sum = Sum(line, dp_bits[:-2], value, swap(give, "dp", 2))
    text_grad_rows = (text_grad_rows, rows_side, rows_core, rows_both)
    grad_text = text_grads(line, text_grad_rows, text_table.shape[0])
    backward_sum.step()
    forward_sum.finish()
    forward_group = stream_group(forward_sum.value)
    grad_patches = patch_grads(
        line, slot_keys_of(1.0, slot_index), came_back, matrices, patches.shape[0]
    )
    backward_sum.finish()
    small = [join_small(rows[texts + 16 :]) for rows in text_grad_rows]
    small = (small[0] + small[1]) + (small[2] + small[3])

    shard_down, shard_mix, shard_in = assemble_forward(
        line, stream.reshape(1), forward_group, down_shape[2], mix_rows,
        shard_rows,
    )
    shard_layout, shard_qkv, shard_project = assemble_backward(
        line, stream.reshape(1), stream_group(backward_sum.value), layout_rows, shard_rows
    )
    grad_gains = lax.dynamic_slice_in_dim(
        small[:2], lax.axis_index("dp") * gain_count, gain_count, axis=1
    )
    return (
        result,
        grad_patches,
        grad_text,
        shard_layout,
        shard_project,
        small[2, : rel.size].reshape(rel.shape),
        grad_gains,
        shard_qkv,
        shard_mix.reshape(shard_rows, width),
        shard_in,
        shard_down.reshape(-1, width),
    )


def solution(mesh):
    return jax.shard_map(
        shards,
        mesh=mesh,
        in_specs=(
            P(("dp", "stream"), None),
            P(("dp", "stream")),
            P(("dp", "stream")),
            P(None, ("dp", "stream")),
            P(("dp", "stream")),
            P(("dp", "stream"), None),
            P("dp", None),
            P(None, "dp", None),
            P("dp", None),
            P(),
            P(None, "dp"),
            P(None, "dp", None),
            P("dp", None),
            P("dp", None),
            P("dp", None),
            P(("dp", "stream"), None),
        ),
        out_specs=(
            P(("dp", "stream"), None),
            P(("dp", "stream"), None),
            P("dp", None),
            P(None, "dp", None),
            P("dp", None),
            P(),
            P(None, "dp"),
            P(None, "dp", None),
            P("dp", None),
            P("dp", None),
            P("dp", None),
        ),
        check_vma=False,
    )
```

```python
from functools import partial
import math

import jax
import jax.numpy as jnp
from jax import lax
from jax.experimental import pallas as pl
from jax.experimental.pallas import tpu as pltpu
from jax.sharding import PartitionSpec as P

EPSILON = 1e-06
THRESHOLDS = (12, 16, 23, 32, 46, 64, 91)
BLK = 256
NEG = -1e30
RATE = math.sqrt(2.0 / math.pi)
VMEM_LIMIT = 56 * 2**20
SMALL = pl.CostEstimate(flops=1, bytes_accessed=1, transcendentals=0)


class Line:
    def __init__(self):
        self.last = jnp.zeros((8, 128), jnp.float32)


def launch(
    line, kernel, operands, in_specs, out_shape, out_specs, grid, name, scalars=(), scratch=(), waits=()
):
    held, given, made = len(scalars), len(operands), len(out_shape)
    token = pl.BlockSpec((8, 128), lambda *_: (0, 0))

    def body(*refs):
        outs = held + given + 1 + len(waits)
        refs[outs + made][...] = refs[held + given][...]
        kernel(*refs[: held + given], *refs[outs : outs + made], *refs[outs + made + 1 :])

    out_shape = [jax.ShapeDtypeStruct(value.shape, value.dtype) for value in out_shape]
    results = pl.pallas_call(
        body,
        out_shape=tuple(out_shape) + (jax.ShapeDtypeStruct((8, 128), jnp.float32),),
        grid_spec=pltpu.PrefetchScalarGridSpec(
            num_scalar_prefetch=held,
            grid=grid,
            in_specs=list(in_specs) + [token] + [pl.BlockSpec(memory_space=pl.ANY)] * len(waits),
            out_specs=tuple(out_specs) + (token,),
            scratch_shapes=list(scratch),
        ),
        compiler_params=pltpu.CompilerParams(vmem_limit_bytes=VMEM_LIMIT),
        cost_estimate=SMALL,
        name=name,
    )(*scalars, *operands, line.last, *waits)
    line.last = results[-1]
    return results[:-1]


def fixed(value):
    return pl.BlockSpec(value.shape, lambda *_: (0,) * len(value.shape))


def bf16(*shape):
    return jax.ShapeDtypeStruct(shape, jnp.bfloat16)


def f32(*shape):
    return jax.ShapeDtypeStruct(shape, jnp.float32)


def i32(*shape):
    return jax.ShapeDtypeStruct(shape, jnp.int32)


def bucket_of(relative):
    magnitude = jnp.abs(relative)
    beyond = 8 + sum(((magnitude >= threshold).astype(jnp.int32) for threshold in THRESHOLDS))
    return jnp.where(relative > 0, 16, 0).astype(jnp.int32) + jnp.where(
        magnitude < 8, magnitude, beyond
    )


def dot_nt(a, b):
    return lax.dot_general(a, b, (((1,), (1,)), ((), ())), preferred_element_type=jnp.float32)

def dot_nn(a, b):
    return lax.dot_general(a, b, (((1,), (0,)), ((), ())), preferred_element_type=jnp.float32)

def dot_tn(a, b):
    return lax.dot_general(a, b, (((0,), (0,)), ((), ())), preferred_element_type=jnp.float32)


def pieces(value):
    one = value.astype(jnp.bfloat16)
    rest = value - one.astype(jnp.float32)
    two = rest.astype(jnp.bfloat16)
    three = (rest - two.astype(jnp.float32)).astype(jnp.bfloat16)
    return one, two, three

def put_pieces(base, value, lane):
    one, two, three = pieces(value)
    base = jnp.where(jnp.logical_or(lane == 8, lane == 72), one, base)
    base = jnp.where(jnp.logical_or(lane == 9, lane == 73), two, base)
    return jnp.where(jnp.logical_or(lane == 10, lane == 74), three, base)

def diagonal_sums(block):
    wide = jnp.concatenate([block, jnp.zeros_like(block)], axis=1)
    total = wide[:128]
    for start in range(128, BLK, 128):
        total = total + pltpu.roll(wide[start : start + 128], 2 * BLK - start, 1)
    eight = total[:8]
    for start in range(8, 128, 8):
        eight = eight + pltpu.roll(total[start : start + 8], 2 * BLK - start, 1)
    one = eight[:1]
    for row in range(1, 8):
        one = one + pltpu.roll(eight[row : row + 1], 2 * BLK - row, 1)
    return one


def window_of(block, count):
    low = max(0, block * BLK - 2 * BLK + 1) // BLK
    high = min(count - 1, (block * BLK + BLK - 1 + 2 * BLK - 1) // BLK)
    return low, high + 1

def fill_strip(strip, table, slot, count):
    middle = (count - 1) * BLK
    for step in (-1, 0, 1):
        window = table[slot : slot + 1, BLK * step + BLK : BLK * step + 3 * BLK]
        spread = jnp.broadcast_to(window, (BLK, 2 * BLK))
        start = middle + step * BLK
        strip[slot, :, start : start + BLK] = pltpu.roll(spread, 0, 1, stride=1, stride_axis=0)[:, BLK:]
    low = jnp.broadcast_to(table[slot : slot + 1, 0:1], (BLK, middle - BLK))
    high = jnp.broadcast_to(table[slot : slot + 1, 4 * BLK - 1 : 4 * BLK], (BLK, middle - BLK))
    strip[slot, :, 0 : middle - BLK] = low
    strip[slot, :, middle + 2 * BLK :] = high

def forward_kernel(q_ref, k_ref, v_ref, aug_q, aug_k, table, out_ref, lse_ref, strip, ka, va):
    length = q_ref.shape[0]
    count = length // BLK
    lane = lax.broadcasted_iota(jnp.int32, (1, 128), 1)
    left = lane < 64
    for h in range(2):
        fill_strip(strip, table, h, count)
        mine = left if h == 0 else jnp.logical_not(left)
        ka[h] = jnp.where(mine, k_ref[...], aug_k[...])
        va[h] = jnp.where(mine, v_ref[...], aug_k[...])
    for qb in range(count):
        rows = slice(qb * BLK, qb * BLK + BLK)
        low, high = window_of(qb, count)
        keys = slice(low * BLK, high * BLK)
        offset = (count - 1 - qb) * BLK
        query = q_ref[rows, :] * jnp.bfloat16(0.125)
        outs = []
        lses = []
        for h in range(2):
            qa = jnp.where(left if h == 0 else jnp.logical_not(left), query, aug_q[rows, :])
            s = dot_nt(qa, ka[h, keys, :]) + strip[h, :, offset + low * BLK : offset + high * BLK]
            peak = jnp.max(s, axis=1, keepdims=True)
            p = jnp.exp(s - peak).astype(jnp.bfloat16)
            acc = dot_nn(p, va[h, keys, :])
            mark = 72 if h == 0 else 8
            total = acc[:, mark : mark + 1]
            outs.append(acc / total)
            lses.append(jnp.broadcast_to(peak + jnp.log(total), (BLK, 128)))
        out_ref[rows, :] = jnp.where(left, outs[0], outs[1]).astype(jnp.bfloat16)
        lse_ref[rows, :] = jnp.where(left, lses[0], lses[1])

def backward_kernel(
    q_ref, k_ref, v_ref, mixed_ref, grad_ref, lse_ref, aug_q, aug_k, table,
    grads_ref, rel_ref,
    strip, rel, ka, va, qa, ga, dq_acc,
):
    length = q_ref.shape[0]
    count = length // BLK
    middle = (count - 1) * BLK
    lane = lax.broadcasted_iota(jnp.int32, (1, 128), 1)
    left = lane < 64
    rel[...] = jnp.zeros_like(rel)
    dq_acc[...] = jnp.zeros_like(dq_acc)
    inner = mixed_ref[...].astype(jnp.float32) * grad_ref[...].astype(jnp.float32)
    query = q_ref[...] * jnp.bfloat16(0.125)
    for h in range(2):
        fill_strip(strip, table, h, count)
        mine = left if h == 0 else jnp.logical_not(left)
        ka[h] = jnp.where(mine, k_ref[...], aug_k[...])
        va[h] = jnp.where(mine, v_ref[...], aug_k[...])
        at = 0 if h == 0 else 64
        qa[h] = jnp.where(mine, query, put_pieces(aug_q[...], -lse_ref[:, at : at + 1], lane))
        delta = jnp.sum(jnp.where(mine, inner, 0.0), axis=1, keepdims=True)
        spare = put_pieces(jnp.zeros((length, 128), jnp.bfloat16), -delta, lane)
        ga[h] = jnp.where(mine, grad_ref[...], spare)
    for kb in range(count):
        keys = slice(kb * BLK, kb * BLK + BLK)
        low, high = window_of(kb, count)
        rows = slice(low * BLK, high * BLK)
        offset = middle - kb * BLK
        cut = slice(offset + low * BLK, offset + high * BLK)
        dks, dvs = [], []
        for h in range(2):
            s = dot_nt(ka[h, keys, :], qa[h, rows, :]) + strip[h, :, cut]
            p = jnp.exp(s)
            ds = p * dot_nt(va[h, keys, :], ga[h, rows, :])
            rel[h, :, cut] += ds
            p = p.astype(jnp.bfloat16)
            ds = ds.astype(jnp.bfloat16)
            dvs.append(dot_nn(p, ga[h, rows, :]))
            dks.append(dot_nn(ds, qa[h, rows, :]))
            dq_acc[h, :, rows] += dot_tn(ka[h, keys, :], ds)
        grads_ref[1, keys, :] = jnp.where(left, dks[0], dks[1]).astype(jnp.bfloat16)
        grads_ref[2, keys, :] = jnp.where(left, dvs[0], dvs[1]).astype(jnp.bfloat16)
    row = lax.broadcasted_iota(jnp.int32, (128, 1), 0)
    dq = jnp.where(row < 64, dq_acc[0], dq_acc[1]).T
    grads_ref[0] = (dq * 0.125).astype(jnp.bfloat16)
    for h in range(2):
        out = []
        for place in range(5):
            start = middle + (2 - place) * BLK
            if place == 0:
                far = rel[h, :, middle + 2 * BLK :]
                summed = jnp.sum(jnp.sum(far, axis=0, keepdims=True).reshape(-1, BLK), axis=0, keepdims=True)
                out.append(jnp.concatenate([summed, jnp.zeros_like(summed)], axis=1))
            elif place == 4:
                far = rel[h, :, : middle - BLK]
                summed = jnp.sum(jnp.sum(far, axis=0, keepdims=True).reshape(-1, BLK), axis=0, keepdims=True)
                out.append(jnp.concatenate([summed, jnp.zeros_like(summed)], axis=1))
            else:
                out.append(diagonal_sums(rel[h, :, start : start + BLK]))
        rel_ref[h] = jnp.concatenate(out + [jnp.zeros((3, 2 * BLK), jnp.float32)], axis=0)


def attention_forward(line, qkv, aug_q, aug_k, table):
    _, length, width = qkv.shape
    col = pl.BlockSpec((length, 128), lambda p: (0, p))
    buf = pltpu.VMEM((2, length, 128), jnp.bfloat16)
    return launch(
        line, forward_kernel, (qkv, qkv, qkv, aug_q, aug_k, table),
        [
            pl.BlockSpec((None, length, 128), lambda p: (0, 0, p)),
            pl.BlockSpec((None, length, 128), lambda p: (1, 0, p)),
            pl.BlockSpec((None, length, 128), lambda p: (2, 0, p)),
            fixed(aug_q), fixed(aug_k),
            pl.BlockSpec((None, 2, table.shape[2]), lambda p: (p, 0, 0)),
        ],
        (bf16(length, width), f32(length, width)), (col, col), (width // 128,),
        "attention_forward",
        scratch=[pltpu.VMEM((2, BLK, 2 * length - BLK), jnp.float32), buf, buf],
    )


def attention_backward(line, qkv, mixed, grad_mixed, lse, aug_q, aug_k, table):
    _, length, width = qkv.shape
    col = pl.BlockSpec((length, 128), lambda p: (0, p))
    buf = pltpu.VMEM((2, length, 128), jnp.bfloat16)
    strip = pltpu.VMEM((2, BLK, 2 * length - BLK), jnp.float32)
    return launch(
        line, backward_kernel,
        (qkv, qkv, qkv, mixed, grad_mixed, lse, aug_q, aug_k, table),
        [
            pl.BlockSpec((None, length, 128), lambda p: (0, 0, p)),
            pl.BlockSpec((None, length, 128), lambda p: (1, 0, p)),
            pl.BlockSpec((None, length, 128), lambda p: (2, 0, p)),
            col, col, col, fixed(aug_q), fixed(aug_k),
            pl.BlockSpec((None, 2, table.shape[2]), lambda p: (p, 0, 0)),
        ],
        (bf16(3, length, width), f32(width // 64, 8, 2 * BLK)),
        (
            pl.BlockSpec((3, length, 128), lambda p: (0, 0, p)),
            pl.BlockSpec((2, 8, 2 * BLK), lambda p: (p, 0, 0)),
        ),
        (width // 128,), "attention_backward",
        scratch=[strip, strip, buf, buf, buf, buf, pltpu.VMEM((2, 128, length), jnp.float32)],
    )


def bucket_choice(offsets, count):
    return (bucket_of(offsets)[:, None] == jnp.arange(count, dtype=jnp.int32)[None, :]).astype(jnp.float32)

def prepare(segments, rel_table):
    heads = rel_table.shape[1]
    offsets = jnp.arange(4 * BLK, dtype=jnp.int32) - 2 * BLK
    tables = []
    for sign in (1, -1):
        choose = bucket_choice(sign * offsets, rel_table.shape[0])
        table = lax.dot_general(rel_table, choose, (((0,), (1,)), ((), ())), precision=lax.Precision.HIGHEST)
        tables.append(table.reshape(heads // 2, 2, 4 * BLK))
    lane = (jnp.arange(128, dtype=jnp.int32) % 64)[None, :]
    row = segments.reshape(-1)[:, None]
    same = lane == row
    aug_q = jnp.where(jnp.logical_or(same, lane >= 8), 0.0, NEG).astype(jnp.bfloat16)
    aug_k = jnp.where(jnp.logical_or(same, jnp.logical_and(lane >= 8, lane < 11)), 1.0, 0.0).astype(jnp.bfloat16)
    return aug_q, aug_k, tables[0], tables[1]

def rel_gradient(rel, count):
    lane = jnp.arange(2 * BLK, dtype=jnp.int32)
    parts = []
    for place in range(5):
        if place == 0:
            offset = jnp.full((2 * BLK,), -600, jnp.int32)
        elif place == 4:
            offset = jnp.full((2 * BLK,), 600, jnp.int32)
        else:
            offset = BLK * (place - 2) - jnp.where(lane < BLK, lane, lane - 2 * BLK)
        parts.append(bucket_choice(offset, count))
    choose = jnp.concatenate(parts + [jnp.zeros((3 * 2 * BLK, count), jnp.float32)], axis=0)
    flat = rel.reshape(rel.shape[0], -1)
    return lax.dot_general(choose, flat, (((0,), (1,)), ((), ())), precision=lax.Precision.HIGHEST)


def iota(shape, axis):
    return lax.broadcasted_iota(jnp.int32, shape, axis)


def as_bf16(flag):
    return jnp.where(flag, 1.0, 0.0).astype(jnp.bfloat16)


def slots_kernel(owners, capacity, shift, place_ref, kind_ref, index_ref, coords_ref,
                 meta_ref, keys_ref, text_ref):
    tokens = place_ref.shape[1]
    place = place_ref[...]
    text = kind_ref[...] == 1
    owner = jnp.right_shift(place, shift)
    position = jnp.bitwise_and(place, (1 << shift) - 1)
    rows = owners + 16
    row = iota((rows, tokens), 0)
    member = jnp.logical_or(row == owner, jnp.logical_and(row == owners, text))
    upto = as_bf16(iota((tokens, tokens), 0) <= iota((tokens, tokens), 1))
    counts = dot_nn(as_bf16(member), upto)
    rank = jnp.sum(jnp.where(row == owner, counts, 0.0), axis=0, keepdims=True)
    rank = rank.astype(jnp.int32) - 1
    text_rank = jnp.where(text, counts[owners : owners + 1].astype(jnp.int32) - 1, 0)
    slot = owner * capacity + rank
    index = index_ref[...]
    coords = coords_ref[...]
    low = jnp.bitwise_and(coords, 3)
    high = jnp.right_shift(coords, 2)
    meta = jnp.concatenate(
        [
            kind_ref[...] + 1,
            jnp.right_shift(position, 2), jnp.bitwise_and(position, 3),
            high, low,
            jnp.right_shift(index, 4), jnp.bitwise_and(index, 15),
            jnp.right_shift(text_rank, 2), jnp.bitwise_and(text_rank, 3),
            jnp.zeros_like(index),
        ],
        axis=0,
    ).astype(jnp.float32).astype(jnp.bfloat16)
    slots = meta_ref.shape[1]
    for start in range(0, slots, 512):
        pick = as_bf16(iota((512, tokens), 0) + start == slot)
        meta_ref[:, start : start + 512] = dot_nt(meta, pick).astype(jnp.bfloat16)
        down = dot_nt(pick, meta)
        index = down[:, 11:12] * 16.0 + down[:, 12:13]
        rank = down[:, 13:14] * 4.0 + down[:, 14:15] + float(tokens - text_ref.shape[1])
        key = jnp.where(down[:, 0:1] > 1.5, rank, jnp.where(down[:, 0:1] > 0.5, index, -1.0))
        keys_ref[start : start + 512, :] = jnp.broadcast_to(key.astype(jnp.int32), (512, 8))
    texts = text_ref.shape[1]
    chosen = as_bf16(jnp.logical_and(iota((texts, tokens), 0) == text_rank, text))
    found = dot_nt(meta, chosen)
    text_ref[...] = jnp.broadcast_to(
        (found[11:12] * 16.0 + found[12:13]).astype(jnp.int32), text_ref.shape
    )


def find_slots(line, owners, capacity, shift, placing, src_kind, src_index, coords, texts):
    slots = owners * capacity
    operands = (placing.reshape(1, -1), src_kind.reshape(1, -1), src_index.reshape(1, -1), coords)
    shapes = (bf16(16, slots), i32(slots, 8), i32(8, texts))
    return launch(
        line, partial(slots_kernel, owners, capacity, shift), operands,
        [fixed(value) for value in operands], shapes, [fixed(value) for value in shapes], (1,),
        "find_slots",
    )


def unpack_kernel(key_ref, rows_ref, index_ref, out_ref):
    texts, tokens = index_ref.shape[1], rows_ref.shape[1]
    count, width = rows_ref.shape[0], out_ref.shape[1]
    total = None
    small = None
    for d in range(count):
        pick = as_bf16(iota((texts, tokens), 0) == key_ref[d : d + 1, :])
        part = dot_nn(pick, rows_ref[d])
        total = part if total is None else total + part
        part = join_small(rows_ref[d, tokens - 16 :, :])
        small = part if small is None else small + part
    out_ref[:texts, :] = total.astype(jnp.bfloat16)
    index = index_ref[...]
    row = iota((16, texts), 0)
    high = jnp.broadcast_to(jnp.right_shift(index[0:1], 4), (16, texts))
    low = jnp.broadcast_to(jnp.bitwise_and(index[0:1], 15), (16, texts))
    index = jnp.where(row == 0, high, jnp.where(row == 1, low, 0)).astype(jnp.float32)
    index = jnp.concatenate([index, jnp.zeros((16, width - texts), jnp.float32)], axis=1)
    out_ref[texts : texts + 16, :] = index.astype(jnp.bfloat16)
    out_ref[texts + 16 :, :] = split_small(small)


def unpack_text(line, keys, rows, index):
    width = rows.shape[2]
    shape = bf16(index.shape[1] + 32, width)
    return launch(
        line, unpack_kernel, (keys, rows, index), [fixed(keys), fixed(rows), fixed(index)],
        (shape,), (fixed(shape),), (1,), "unpack_text",
    )[0]


def pack_kernel(key_ref, patch_ref, text_ref, *refs):
    out_ref = refs[len(refs) // 2]
    size, patches, texts = out_ref.shape[0], patch_ref.shape[0], text_ref.shape[0]
    key = key_ref[:, 0:1]
    out = dot_nn(as_bf16(iota((size, patches), 1) == key), patch_ref[...])
    out = out + dot_nn(as_bf16(iota((size, texts), 1) + patches == key), text_ref[...])
    out_ref[...] = out.astype(jnp.bfloat16)

    @pl.when(pl.program_id(0) == 0)
    def _():
        for n in range(len(refs) // 2):
            refs[len(refs) // 2 + 1 + n][...] = refs[n][...]


def pack(line, keys, patches, text_rows, later):
    slots = keys.shape[0]
    width = patches.shape[1]
    return launch(
        line, pack_kernel, (keys, patches, text_rows) + later,
        [pl.BlockSpec((512, 8), lambda i: (i, 0)), fixed(patches), fixed(text_rows)]
        + [fixed(value) for value in later],
        (bf16(slots, width),) + later,
        (pl.BlockSpec((512, width), lambda i: (i, 0)),) + tuple(fixed(value) for value in later),
        (slots // 512,), "pack",
    )


def place_kernel(meta_ref, column_ref, row_ref, place_ref):
    slots, tokens = meta_ref.shape[1], row_ref.shape[1]
    meta = meta_ref[...]
    wide = meta.astype(jnp.float32)
    place = (wide[1:2] * 4.0 + wide[2:3]).astype(jnp.int32)
    place = jnp.where(wide[0:1] > 0.5, place, -1)
    place_ref[...] = jnp.broadcast_to(place, place_ref.shape)
    for start in range(0, tokens, 256):
        pick = as_bf16(iota((256, slots), 0) + start == place)
        down = dot_nt(pick, meta)
        values = [down[:, 0:1]] + [down[:, 3 + c : 4 + c] * 4.0 + down[:, 7 + c : 8 + c] for c in range(4)]
        lane = iota((256, 8), 1)
        block = jnp.zeros((256, 8), jnp.float32)
        for c in range(5):
            block = jnp.where(lane == c, values[c], block)
        column_ref[start : start + 256, :] = block.astype(jnp.int32)
        across = dot_nt(meta, pick)
        row_ref[:, start : start + 256] = jnp.concatenate(
            [across[0:1], across[3:7] * 4.0 + across[7:11], jnp.zeros((3, 256), jnp.float32)], axis=0
        ).astype(jnp.int32)


def place_meta(line, meta, tokens):
    shapes = (i32(tokens, 8), i32(8, tokens), i32(8, meta.shape[1]))
    return launch(
        line, place_kernel, (meta,), [fixed(meta)], shapes, [fixed(value) for value in shapes],
        (1,), "place_meta",
    )


def lookup_kernel(rows, fresh, side, mine_ref, other_ref, table_ref, *refs):
    width = table_ref.shape[2]
    outs = refs[-2:]
    entries = table_ref.shape[0] * rows
    for n, coords in enumerate((mine_ref, other_ref)):
        total = jnp.zeros(outs[n].shape, jnp.float32) if fresh else refs[n][...]
        for k in range(2):
            key = jnp.where(side[0] == 0, coords[:, k + 1 : k + 2], coords[:, k + 3 : k + 4])
            pick = as_bf16(iota((total.shape[0], entries), 1) == key)
            table = table_ref[:, k * rows : k * rows + rows, :].reshape(entries, width)
            total = total + dot_nn(pick, table)
        outs[n][...] = total


def layout_lookup(line, side, mine, other, columns, rows, sums=()):
    tokens = mine.shape[0]
    width = columns.shape[2]
    column = pl.BlockSpec((256, 8), lambda i, s: (i, 0))
    out = pl.BlockSpec((256, width), lambda i, s: (i, 0))
    return launch(
        line, partial(lookup_kernel, rows, not sums), (mine, other, columns, *sums),
        [column, column, fixed(columns)] + [out] * len(sums),
        (f32(tokens, width), f32(tokens, width)), (out, out), (tokens // 256,), "layout_lookup",
        scalars=(side,),
    )


def embed_kernel(place_ref, column_ref, arrived_ref, own_ref, got_ref, half_ref, project_ref,
                 gain_ref, weight_ref, visual_ref, packed_ref, normed_ref, out_ref):
    rows, slots = packed_ref.shape[0], arrived_ref.shape[0]
    pick = as_bf16(iota((rows, slots), 0) + pl.program_id(0) * rows == place_ref[0:1, :])
    raw = dot_nn(pick, arrived_ref[...])
    narrow = raw.astype(jnp.bfloat16)
    kind = column_ref[:, 0:1]
    visual_ref[...] = jnp.where(kind == 1, raw, 0.0).astype(jnp.bfloat16).T
    projected = dot_nn(narrow, project_ref[...])
    first = half_ref[0:1, 0:1] == 0
    own, got = own_ref[...], got_ref[...]
    layout = jnp.concatenate([jnp.where(first, own, got), jnp.where(first, got, own)], axis=1)
    embedded = jnp.where(kind == 2, raw, projected) + layout
    packed_ref[...] = embedded.astype(jnp.bfloat16)
    packed = packed_ref[...].astype(jnp.float32)
    scale = lax.rsqrt(jnp.mean(packed * packed, axis=-1, keepdims=True) + EPSILON)
    normed = (packed * scale * gain_ref[0:1, :].astype(jnp.float32)).astype(jnp.bfloat16)
    normed_ref[...] = normed.T
    for part in range(3):
        out_ref[part] = dot_nn(normed, weight_ref[part]).astype(jnp.bfloat16)


def embed(line, places, column, arrived, own, got, half, matrices, gains, tokens):
    width = arrived.shape[1]
    rows = 256
    wide = pl.BlockSpec((rows, width), lambda i: (i, 0))
    part = pl.BlockSpec((rows, own.shape[1]), lambda i: (i, 0))
    across = pl.BlockSpec((width, rows), lambda i: (0, i))
    return launch(
        line, embed_kernel, (places, column, arrived, own, got, half, matrices, gains, matrices),
        [
            fixed(places), pl.BlockSpec((rows, 8), lambda i: (i, 0)), fixed(arrived), part, part,
            fixed(half), pl.BlockSpec((None, width, width), lambda i: (3, 0, 0)), fixed(gains),
            pl.BlockSpec((3, width, width), lambda i: (0, 0, 0)),
        ],
        (bf16(width, tokens), bf16(tokens, width), bf16(width, tokens), bf16(3, tokens, width)),
        (across, wide, across, pl.BlockSpec((3, rows, width), lambda i: (0, i, 0))),
        (tokens // rows,), "embed",
    )


def input_grad_kernel(which, packed_ref, upper_ref, grads_ref, weight_ref, gain_ref,
                      out_ref, own_ref, other_ref, sum_ref):
    total = dot_nt(grads_ref[0], weight_ref[0])
    total = total + dot_nt(grads_ref[1], weight_ref[1])
    total = total + dot_nt(grads_ref[2], weight_ref[2])
    packed = packed_ref[...].astype(jnp.float32)
    scale = lax.rsqrt(jnp.mean(packed * packed, axis=-1, keepdims=True) + EPSILON)
    unit = packed * scale
    back = total * gain_ref[0:1, :].astype(jnp.float32)
    back = scale * (back - unit * jnp.mean(back * unit, axis=-1, keepdims=True))
    back = back + upper_ref[...]
    out_ref[...] = back.astype(jnp.bfloat16)
    put_halves(which, back, own_ref, other_ref)

    @pl.when(pl.program_id(0) == 0)
    def _():
        sum_ref[...] = jnp.zeros_like(sum_ref)

    sum_ref[0:1, :] += jnp.sum(total * unit, axis=0, keepdims=True)


def input_grad(line, which, packed, upper, grads, matrices, gains):
    tokens, width = packed.shape
    rows = 256
    half = width // 2
    wide = pl.BlockSpec((rows, width), lambda i, w: (i, 0))
    part = pl.BlockSpec((rows, half), lambda i, w: (i, 0))
    return launch(
        line, input_grad_kernel, (packed, upper, grads, matrices, gains),
        [
            wide, wide, pl.BlockSpec((3, rows, width), lambda i, w: (0, i, 0)),
            pl.BlockSpec((3, width, width), lambda i, w: (0, 0, 0)), fixed(gains),
        ],
        (bf16(tokens, width), bf16(tokens, half), bf16(tokens, half), f32(8, width)),
        (wide, part, part, pl.BlockSpec((8, width), lambda i, w: (0, 0))),
        (tokens // rows,), "input_grad", scalars=(which,),
    )


def split_small(small):
    parts = [part.astype(jnp.float32) for part in pieces(small)]
    pad = jnp.zeros((16 - 3 * small.shape[0], small.shape[1]), jnp.float32)
    return jnp.concatenate(parts + [pad], axis=0).astype(jnp.bfloat16)


def join_small(rows):
    rows = rows[:9].astype(jnp.float32)
    return rows[0:3] + rows[3:6] + rows[6:9]


def return_kernel(place_ref, rows_ref, small_ref, out_ref):
    slots = place_ref.shape[0]
    devices, capacity = out_ref.shape[0], out_ref.shape[1] - 16
    pick = as_bf16(iota((slots, rows_ref.shape[0]), 1) == place_ref[...])
    rows = dot_nn(pick, rows_ref[...]).astype(jnp.bfloat16)
    small = split_small(small_ref[0:3, :])
    for d in range(devices):
        out_ref[d, :capacity, :] = rows[d * capacity : d * capacity + capacity]
        out_ref[d, capacity:, :] = small


def return_rows(line, places, rows, small, capacity):
    count = places.shape[0] // capacity
    width = rows.shape[1]
    step = max(1, min(count, 512 // capacity))
    return launch(
        line, return_kernel, (places, rows, small),
        [pl.BlockSpec((step * capacity, 1), lambda i: (i, 0)), fixed(rows), fixed(small)],
        (bf16(count, capacity + 16, width),),
        (pl.BlockSpec((step, capacity + 16, width), lambda i: (i, 0, 0)),), (count // step,),
        "return_rows",
    )[0]


def layout_grad_kernel(side, mine_ref, other_ref, first_ref, second_ref, keep_ref, give_ref):
    pair = pl.program_id(0)
    shards, rows, width = keep_ref.shape
    entries = shards * rows
    table = 2 * jnp.where(pair < 2, 1 - side[0], side[0]) + jnp.bitwise_and(pair, 1)
    total = jnp.zeros((entries, width), jnp.float32)
    for coords, grads in ((mine_ref, first_ref), (other_ref, second_ref)):
        tokens = grads.shape[0]
        key = coords[pl.ds(table + 1, 1), :]
        pick = as_bf16(iota((entries, tokens), 0) + pl.program_id(1) * entries == key)
        total = total + dot_nn(pick, grads[...])
    total = total.reshape(shards, rows, width).astype(jnp.bfloat16)

    @pl.when(pair < 2)
    def _():
        give_ref[...] = total

    @pl.when(pair >= 2)
    def _():
        keep_ref[...] = total


def layout_grad(line, side, mine, other, first, second, shards, rows):
    width = first.shape[1]
    step = max(1, min(shards, 512 // rows))
    last = shards // step - 1
    block = (step, None, rows, width)
    shape = bf16(shards, 2, rows, width)
    return launch(
        line, layout_grad_kernel, (mine, other, first, second),
        [fixed(mine), fixed(other), fixed(first), fixed(second)], (shape, shape),
        (
            pl.BlockSpec(
                block, lambda t, i, s: (jnp.where(t < 2, 0, i), jnp.maximum(t - 2, 0), 0, 0)
            ),
            pl.BlockSpec(
                block, lambda t, i, s: (jnp.where(t < 2, i, last), jnp.minimum(t, 1), 0, 0)
            ),
        ),
        (4, shards // step), "layout_grad", scalars=(side,),
    )


def patch_kernel(key_ref, rows_ref, weight_ref, grad_ref):
    patches, tokens = grad_ref.shape[0], rows_ref.shape[1]
    total = None
    for d in range(rows_ref.shape[0]):
        pick = as_bf16(iota((patches, tokens), 0) == key_ref[d : d + 1, :])
        part = dot_nn(pick, rows_ref[d])
        total = part if total is None else total + part
    grad_ref[...] = dot_nt(total.astype(jnp.bfloat16), weight_ref[...])


def patch_grads(line, keys, rows, matrices, patches):
    width = rows.shape[2]
    shape = f32(patches, width)
    return launch(
        line, patch_kernel, (keys, rows, matrices),
        [fixed(keys), fixed(rows), pl.BlockSpec((None, width, width), lambda i: (3, 0, 0))],
        (shape,), (fixed(shape),), (1,), "patch_grads",
    )[0]


def text_kernel(*refs):
    out_ref = refs[4]
    size = out_ref.shape[0]
    parts = []
    for rows_ref in refs[:4]:
        texts = rows_ref.shape[0] - 32
        index = rows_ref[texts : texts + 16, :texts].astype(jnp.float32)
        key = (index[0:1] * 16.0 + index[1:2]).astype(jnp.int32)
        place = iota((size, texts), 0) + pl.program_id(0) * size
        parts.append(dot_nn(as_bf16(place == key), rows_ref[:texts, :]))
    out_ref[...] = (parts[0] + parts[1]) + (parts[2] + parts[3])


def text_grads(line, rows, entries):
    width = rows[0].shape[1]
    size = 512
    return launch(
        line, text_kernel, rows, [fixed(value) for value in rows],
        (f32(entries, width),), (pl.BlockSpec((size, width), lambda i: (i, 0)),),
        (pl.cdiv(entries, size),), "text_grads",
    )[0]


def feed_forward_kernel(core, packed_ref, mixed_ref, grad_ref, own_ref, other_ref, in_ref, down_ref,
                        gain_ref, result_ref, active_ref, hidden_ref, normed_ref, turned_ref, upper_ref,
                        branch_ref, back_ref, sum_ref):
    own, other = own_ref[...], other_ref[...]
    first = core[0] == 0
    mix = jnp.concatenate([jnp.where(first, own, other), jnp.where(first, other, own)], axis=1)
    attended = packed_ref[...].astype(jnp.float32) + dot_nn(mixed_ref[...], mix)
    turned_ref[...] = mixed_ref[...].T
    scale = lax.rsqrt(jnp.mean(attended * attended, axis=-1, keepdims=True) + EPSILON)
    unit = attended * scale
    gain = gain_ref[0:1, :].astype(jnp.float32)
    normed = (unit * gain).astype(jnp.bfloat16)
    normed_ref[...] = normed.T
    out_grad = grad_ref[...]
    result = attended
    back = jnp.zeros_like(attended)
    width = attended.shape[1]
    for part in range(in_ref.shape[0]):
        cut = slice(part * width, part * width + width)
        hidden = dot_nn(normed, in_ref[part])
        square = hidden * hidden
        tanh = jnp.tanh(hidden * (RATE + RATE * 0.044715 * square))
        half = 0.5 + 0.5 * tanh
        active = (hidden * half).astype(jnp.bfloat16)
        active_ref[cut, :] = active.T
        slope = half + hidden * half * (1.0 - tanh) * (RATE + 3.0 * 0.044715 * RATE * square)
        result = result + dot_nn(active, down_ref[cut, :])
        grad_hidden = (dot_nt(out_grad, down_ref[cut, :]) * slope).astype(jnp.bfloat16)
        hidden_ref[:, cut] = grad_hidden
        back = back + dot_nt(grad_hidden, in_ref[part])
    result_ref[...] = result.astype(jnp.bfloat16)

    @pl.when(pl.program_id(0) == 0)
    def _():
        sum_ref[...] = jnp.zeros_like(sum_ref)

    sum_ref[0:1, :] += jnp.sum(back * unit, axis=0, keepdims=True)
    back = back * gain
    back = scale * (back - unit * jnp.mean(back * unit, axis=-1, keepdims=True))
    back = back + out_grad.astype(jnp.float32)
    upper_ref[...] = back
    branch = back.astype(jnp.bfloat16)
    branch_ref[...] = branch
    back_ref[...] = dot_nt(branch, mix).astype(jnp.bfloat16)


def feed_forward(line, core, packed, mixed, out_grad, mix_own, mix_other, full_in, full_down, gains):
    tokens, width = packed.shape
    hidden = full_down.shape[0]
    rows = 256
    wide = pl.BlockSpec((rows, width), lambda i, c: (i, 0))
    tall = pl.BlockSpec((rows, hidden), lambda i, c: (i, 0))
    across = pl.BlockSpec((width, rows), lambda i, c: (0, i))
    narrow, turned = bf16(tokens, width), bf16(width, tokens)
    operands = (packed, mixed, out_grad, mix_own, mix_other, full_in, full_down, gains)
    return launch(
        line, feed_forward_kernel, operands,
        [wide, wide, wide] + [fixed(value) for value in operands[3:]],
        (
            narrow, bf16(hidden, tokens), bf16(tokens, hidden), turned, turned,
            f32(tokens, width), narrow, narrow, f32(8, width),
        ),
        (
            wide, pl.BlockSpec((hidden, rows), lambda i, c: (0, i)), tall, across, across,
            wide, wide, wide, pl.BlockSpec((8, width), lambda i, c: (0, 0)),
        ),
        (tokens // rows,), "feed_forward", scalars=(core,),
    )


def put_halves(which, total, keep_ref, give_ref):
    half = total.shape[1] // 2
    first, second = total[:, :half], total[:, half:]
    mine = which[0] == 0
    keep_ref[...] = jnp.where(mine, first, second).astype(jnp.bfloat16)
    give_ref[...] = jnp.where(mine, second, first).astype(jnp.bfloat16)


def contract_halves_kernel(which, left_ref, right_ref, keep_ref, give_ref):
    put_halves(which, dot_nn(left_ref[...], right_ref[...]), keep_ref, give_ref)


def contract_halves(line, which, left, right):
    count, tokens = left.shape
    width = right.shape[1]
    size, half = min(count, width), width // 2
    out = pl.BlockSpec((size, half), lambda i, w: (i, 0))
    shape = bf16(count, half)
    return launch(
        line, contract_halves_kernel, (left, right),
        [pl.BlockSpec((size, tokens), lambda i, w: (i, 0)), fixed(right)],
        (shape, shape), (out, out), (count // size,), "contract_halves", scalars=(which,),
    )


def contract_quarters_kernel(which, left_ref, right_ref, keep_ref, give_ref):
    del which
    total = dot_nn(left_ref[...], right_ref[...])
    shards, _, rows, half = keep_ref.shape

    def put(out_ref):
        for d in range(shards):
            for h in range(2):
                part = total[d * rows : d * rows + rows, h * half : h * half + half]
                out_ref[d, h] = part.astype(jnp.bfloat16)

    @pl.when(pl.program_id(0) < 2)
    def _():
        put(give_ref)

    @pl.when(pl.program_id(0) >= 2)
    def _():
        put(keep_ref)


def contract_quarters(line, which, left, right, shards):
    count, tokens = left.shape
    quarter = right.shape[1] // 4
    block = (shards, 2, count // shards, quarter // 2)
    shape = bf16(2, *block)

    def column(i, w):
        return (0, jnp.where(i < 2, 2 * i + 1 - w[0], 2 * (i - 2) + w[0]))

    return launch(
        line, contract_quarters_kernel, (left, right),
        [fixed(left), pl.BlockSpec((tokens, quarter), column)], (shape, shape),
        (
            pl.BlockSpec((None,) + block, lambda i, w: (jnp.maximum(i - 2, 0), 0, 0, 0, 0)),
            pl.BlockSpec((None,) + block, lambda i, w: (jnp.minimum(i, 1), 0, 0, 0, 0)),
        ),
        (4,), "contract_quarters", scalars=(which,),
    )


def square_kernel(which, normed_ref, grads_ref, visual_ref, packed_ref, keep_ref, give_ref):
    shards, rows, half = keep_ref.shape

    def put(total):
        mine = which[0] == 0
        for d in range(shards):
            part = total[d * rows : d * rows + rows]
            first, second = part[:, :half], part[:, half:]
            keep_ref[d] = jnp.where(mine, first, second).astype(jnp.bfloat16)
            give_ref[d] = jnp.where(mine, second, first).astype(jnp.bfloat16)

    @pl.when(pl.program_id(0) < 3)
    def _():
        put(dot_nn(normed_ref[...], grads_ref[...]))

    @pl.when(pl.program_id(0) == 3)
    def _():
        put(dot_nn(visual_ref[...], packed_ref[...]))


def square_grads(line, which, normed, grads, visual, grad_packed, shards):
    width, tokens = normed.shape
    rows, half = width // shards, width // 2
    out = pl.BlockSpec((shards, None, None, rows, half), lambda m, w: (0, m // 2, m % 2, 0, 0))
    shape = bf16(shards, 2, 2, rows, half)
    return launch(
        line, square_kernel, (normed, grads, visual, grad_packed),
        [
            fixed(normed),
            pl.BlockSpec((None, tokens, width), lambda m, w: (jnp.minimum(m, 2), 0, 0)),
            fixed(visual), fixed(grad_packed),
        ],
        (shape, shape), (out, out), (4,), "square_grads", scalars=(which,),
    )


def fold_kernel(bit, value_ref, got_ref, keep_ref, give_ref):
    del bit
    total = value_ref[...].astype(jnp.float32) + got_ref[...].astype(jnp.float32)

    @pl.when(pl.program_id(0) == 0)
    def _():
        give_ref[...] = total.astype(give_ref.dtype)

    @pl.when(pl.program_id(0) == 1)
    def _():
        keep_ref[...] = total.astype(keep_ref.dtype)


def fold(line, bit, value, got):
    a, _, b, rows, width = value.shape
    step = a
    while step > 1 and step * b * rows * width * value.dtype.itemsize > 1_600_000:
        step //= 2
    count = a // step
    source = pl.BlockSpec(
        (step, None, b, rows, width), lambda n, i, s: (i, jnp.where(n == 0, 1 - s[0], s[0]), 0, 0, 0)
    )
    block = (step, b, rows, width)
    shape = jax.ShapeDtypeStruct((a, b, rows, width), value.dtype)
    return launch(
        line, fold_kernel, (value, got), [source, source], (shape, shape),
        (
            pl.BlockSpec(block, lambda n, i, s: (jnp.where(n == 0, 0, i), 0, 0, 0)),
            pl.BlockSpec(block, lambda n, i, s: (jnp.where(n == 0, i, count - 1), 0, 0, 0)),
        ),
        (2, count), "fold", scalars=(bit,),
    )


def add_kernel(value_ref, got_ref, out_ref):
    total = value_ref[...].astype(jnp.float32) + got_ref[...].astype(jnp.float32)
    out_ref[...] = total.astype(out_ref.dtype)


def add(line, value, got):
    shape = jax.ShapeDtypeStruct(value.shape, value.dtype)
    return launch(
        line, add_kernel, (value, got), [fixed(value), fixed(got)], (shape,), (fixed(shape),),
        (1,), "add",
    )[0]


def rows_fold_kernel(side, down_ref, down_got_ref, mix_ref, mix_got_ref, keep_ref, give_ref):
    del side
    down = down_ref[...].astype(jnp.float32) + down_got_ref[...].astype(jnp.float32)
    mix = mix_ref[...].astype(jnp.float32) + mix_got_ref[...].astype(jnp.float32)
    total = jnp.concatenate([down, mix], axis=1).astype(jnp.bfloat16)

    @pl.when(pl.program_id(0) == 0)
    def _():
        give_ref[...] = total

    @pl.when(pl.program_id(0) == 1)
    def _():
        keep_ref[...] = total


def rows_fold(line, side, down, down_got, mix, mix_got):
    parts, _, rows, width = down.shape
    extra = mix.shape[2]
    step = max(1, parts // 2)

    def source(count):
        return pl.BlockSpec(
            (step, None, count, width), lambda n, i, s: (i, jnp.where(n == 0, 1 - s[0], s[0]), 0, 0)
        )

    shape = bf16(parts, rows + extra, width)
    block = (step, rows + extra, width)
    last = parts // step - 1
    return launch(
        line, rows_fold_kernel, (down, down_got, mix, mix_got),
        [source(rows), source(rows), source(extra), source(extra)], (shape, shape),
        (
            pl.BlockSpec(block, lambda n, i, s: (jnp.where(n == 0, 0, i), 0, 0)),
            pl.BlockSpec(block, lambda n, i, s: (jnp.where(n == 0, i, last), 0, 0)),
        ),
        (2, parts // step), "rows_fold", scalars=(side,),
    )


def stack_kernel(bit, value_ref, got_ref, out_ref):
    del bit

    @pl.when(pl.program_id(0) == 0)
    def _():
        out_ref[...] = value_ref[...]

    @pl.when(pl.program_id(0) == 1)
    def _():
        out_ref[...] = got_ref[...]


def stack(line, bit, value, got, waits=()):
    a, rows, width = value.shape
    return launch(
        line, stack_kernel, (value, got), [fixed(value), fixed(got)],
        (jax.ShapeDtypeStruct((a, 2, rows, width), value.dtype),),
        (
            pl.BlockSpec(
                (a, None, rows, width), lambda n, s: (0, jnp.where(n == 0, s[0], 1 - s[0]), 0, 0)
            ),
        ),
        (2,), "stack", scalars=(bit,), waits=waits,
    )[0]


def split_stack_kernel(parts, bit, value_ref, got_ref, *outs):
    del bit

    def put(source_ref):
        start = 0
        for rows, out_ref in zip(parts, outs):
            out_ref[...] = source_ref[:, start : start + rows, :]
            start += rows

    @pl.when(pl.program_id(0) == 0)
    def _():
        put(value_ref)

    @pl.when(pl.program_id(0) == 1)
    def _():
        put(got_ref)


def split_stack(line, bit, value, got, parts):
    a, _, width = value.shape
    return launch(
        line, partial(split_stack_kernel, parts), (value, got), [fixed(value), fixed(got)],
        [bf16(a, 2, rows, width) for rows in parts],
        [
            pl.BlockSpec(
                (a, None, rows, width), lambda n, s: (0, jnp.where(n == 0, s[0], 1 - s[0]), 0, 0)
            )
            for rows in parts
        ],
        (2,), "split_stack", scalars=(bit,),
    )


def both_sides(line, side, value, got):
    return stack(line, side, value, got)


def arrange_kernel(me, *refs):
    del me
    for n in range(4):

        @pl.when(pl.program_id(0) == n)
        def _():
            refs[4][...] = refs[n][...]


def arrange(line, me, values):
    shape = values[0].shape
    return launch(
        line, arrange_kernel, tuple(values), [fixed(value) for value in values],
        (bf16(4, *shape),),
        (pl.BlockSpec((None,) + shape, lambda n, s: (jnp.bitwise_xor(n, s[0]), 0, 0)),),
        (4,), "arrange", scalars=(me,),
    )[0]


def assemble_forward_kernel(me, *refs):
    down_ref, mix_ref, in_ref = refs[4:]
    half = refs[0].shape[1]
    for n in range(4):
        device = jnp.bitwise_xor(me[0], n)
        side = jnp.right_shift(device, 1)
        column = pl.ds(pl.multiple_of(jnp.bitwise_and(device, 1) * half, 128), half)
        start = 0
        for out_ref in (down_ref, mix_ref):
            rows = out_ref.shape[1]
            out_ref[side, :, column] = refs[n][start : start + rows, :].astype(jnp.float32)
            start += rows
        rows = in_ref.shape[0]
        for h in range(2):
            part = refs[n][start + h * rows : start + h * rows + rows, :].astype(jnp.float32)
            in_ref[:, pl.ds(pl.multiple_of((2 * device + h) * half, 128), half)] = part


def assemble_forward(line, me, values, down_rows, mix_rows, shard_rows):
    half = values[0].shape[1]
    shapes = (f32(2, down_rows, 2 * half), f32(2, mix_rows, 2 * half), f32(shard_rows, 8 * half))
    return launch(
        line, assemble_forward_kernel, tuple(values), [fixed(value) for value in values],
        shapes, [fixed(value) for value in shapes], (1,), "assemble_forward", scalars=(me,),
    )


def assemble_backward_kernel(me, *refs):
    layout_ref, qkv_ref, project_ref = refs[4:]
    half = refs[0].shape[1]
    layout_rows, rows = layout_ref.shape[1], project_ref.shape[0]
    for n in range(4):
        device = jnp.bitwise_xor(me[0], n)
        side = jnp.right_shift(device, 1)
        column = pl.ds(pl.multiple_of(jnp.bitwise_and(device, 1) * half, 128), half)
        for k in range(2):
            start = k * layout_rows
            layout_ref[2 * side + k, :, column] = refs[n][start : start + layout_rows, :].astype(
                jnp.float32
            )
        start = 2 * layout_rows
        qkv_ref[2 * side, :, column] = refs[n][start : start + rows, :].astype(jnp.float32)
        matrix = refs[n][start + rows : start + 2 * rows, :].astype(jnp.float32)

        @pl.when(side == 0)
        def _():
            qkv_ref[1, :, column] = matrix

        @pl.when(side == 1)
        def _():
            project_ref[:, column] = matrix


def assemble_backward(line, me, values, layout_rows, rows):
    half = values[0].shape[1]
    shapes = (f32(4, layout_rows, 2 * half), f32(3, rows, 2 * half), f32(rows, 2 * half))
    return launch(
        line, assemble_backward_kernel, tuple(values), [fixed(value) for value in values],
        shapes, [fixed(value) for value in shapes], (1,), "assemble_backward", scalars=(me,),
    )


def swap(value, axis, bit):
    count = lax.axis_size(axis)
    return lax.ppermute(value, axis, [(i, i ^ bit) for i in range(count)])


def bit_of(axis, bit):
    return jnp.bitwise_and(lax.axis_index(axis), bit) != 0


def bit_index(axis, bit):
    return bit_of(axis, bit).astype(jnp.int32).reshape(1)


class Gather:
    def __init__(self, line, value):
        self.line = line
        self.value = value[None]
        self.bit = lax.axis_size("dp") // 2
        self.got = swap(self.value, "dp", self.bit)

    def step(self, waits=()):
        rows, width = self.value.shape[1:]
        value = stack(self.line, bit_index("dp", self.bit), self.value, self.got, waits)
        self.value = value.reshape(-1, rows, width)
        self.bit //= 2
        self.got = swap(self.value, "dp", self.bit)

    def finish(self, parts):
        while self.bit > 1:
            self.step()
        values = split_stack(self.line, bit_index("dp", 1), self.value, self.got, parts)
        return [value.reshape((-1,) + value.shape[2:]) for value in values]


def padded(value):
    return jnp.pad(value, ((0, -value.shape[0] % 16), (0, 0)))


class Sum:
    def __init__(self, line, bits, value, got):
        self.line, self.bits, self.value, self.got = line, list(bits), value, got
        self.done = False

    def step(self):
        if self.done:
            return
        rows, width = self.value.shape[-2:]
        if not self.bits:
            self.value = add(self.line, self.value.reshape(rows, width), self.got.reshape(rows, width))
            self.done = True
            return
        bit = self.bits.pop()
        shape = (-1, 2, 1, rows, width)
        value, give = fold(
            self.line, bit_index("dp", bit), self.value.reshape(shape), self.got.reshape(shape)
        )
        self.value, self.got = value, swap(give, "dp", bit)

    def finish(self):
        while not self.done:
            self.step()
        return self.value


def shards(
    patches,
    src_kind,
    src_index,
    layout_coords,
    placing,
    segments,
    text_table,
    layout_tables,
    patch_proj,
    rel_table,
    norm_gains,
    w_qkv,
    w_attn_out,
    w_ff_in,
    w_ff_out,
    out_grad,
):
    data_count = lax.axis_size("dp")
    tokens = placing.shape[0]
    capacity = 2 * tokens // data_count
    width = text_table.shape[1]
    half_width = width // 2
    texts = tokens - patches.shape[0]
    shift = tokens.bit_length() - 1
    shard_rows = w_attn_out.shape[0]
    layout_rows = layout_tables.shape[1]
    stream = lax.axis_index("stream")
    core = jnp.bitwise_and(stream, 1)
    side = jnp.right_shift(stream, 1)
    gain_count = norm_gains.shape[1]

    own_core, own_side = core.reshape(1), side.reshape(1)
    dp_bits = [1 << n for n in reversed(range(data_count.bit_length() - 1))]
    line = Line()

    def own_half(value):
        return lax.dynamic_slice_in_dim(value, core * half_width, half_width, axis=-1)

    in_quarter = lax.dynamic_index_in_dim(
        w_ff_in.reshape(shard_rows, 4, -1), stream, 1, keepdims=False
    )
    down_quarter = lax.dynamic_index_in_dim(
        w_ff_out.reshape(4, -1, width), stream, 0, keepdims=False
    )
    layout_part = own_half(
        lax.dynamic_slice_in_dim(layout_tables, side * 2, 2, axis=0)
    ).reshape(-1, half_width)
    mix_part = own_half(
        lax.dynamic_slice_in_dim(w_attn_out, side * (shard_rows // 2), shard_rows // 2, axis=0)
    )
    gain_part = jnp.pad(norm_gains, ((0, 0), (0, half_width - gain_count)))
    table_rows, mix_rows = layout_part.shape[0], mix_part.shape[0]
    square = jnp.concatenate([w_qkv, patch_proj[None]], axis=0)
    square = lax.dynamic_index_in_dim(square, stream, 0, keepdims=False)
    square = lax.all_gather(square, "dp", axis=0, tiled=True)
    square_got = swap(square, "stream", 2)
    mix_part, gain_part = padded(mix_part), padded(gain_part)
    columns = Gather(line, jnp.concatenate([layout_part, mix_part, gain_part], axis=0))
    full_in = lax.all_gather(in_quarter, ("stream", "dp"), axis=0, tiled=True)
    full_in = full_in.reshape(4, width, -1)

    meta, slot_keys, text_index = find_slots(
        line, data_count, capacity, shift, placing, src_kind, src_index, layout_coords, texts
    )
    arrived_meta = lax.all_to_all(
        meta.reshape(16, data_count, capacity), "dp", split_axis=1, concat_axis=1, tiled=True
    ).reshape(16, -1)
    column, across, place = place_meta(line, arrived_meta, tokens)
    column_other = swap(column, "stream", 1)
    across_other = column_other.T
    columns.step()
    columns.step(waits=(column_other,))
    tables, mix, gains = columns.finish((table_rows, mix_part.shape[0], gain_part.shape[0]))
    tables_got = swap(tables, "stream", 2)
    mix_got = swap(mix, "stream", 2)
    gains = gains[:, :2, :gain_count].transpose(1, 0, 2).reshape(2, width)
    text_rows = jnp.take(text_table, text_index[0], axis=0)
    send_rows, down_quarter = pack(line, slot_keys, patches, text_rows, (down_quarter,))
    arrived = lax.all_to_all(
        send_rows.reshape(data_count, capacity, width), "dp", split_axis=0, concat_axis=0, tiled=True
    ).reshape(-1, width)
    full_down = lax.all_gather(down_quarter, ("dp", "stream"), axis=0, tiled=True)
    sums = layout_lookup(line, own_side, column, column_other, tables, layout_rows)
    matrices = arrange(
        line, stream.reshape(1),
        (square, swap(square, "stream", 1), square_got, swap(square_got, "stream", 1)),
    )
    own_sum, other_sum = layout_lookup(
        line, 1 - own_side, column, column_other, tables_got, layout_rows, sums
    )
    got_sum = swap(other_sum, "stream", 1)
    half_index = jnp.broadcast_to(core, (8, 128)).astype(jnp.int32)
    visual, packed, normed_one, projections = embed(
        line, place, column, arrived, own_sum, got_sum, half_index, matrices, gains[:1], tokens
    )
    mix_own = both_sides(line, own_side, mix, mix_got)
    mix_own = mix_own[:, :, :mix_rows].reshape(width, half_width)
    mix_other = swap(mix_own, "stream", 1)
    aug_q, aug_k, table, mirrored = prepare(segments, rel_table)
    mixed, lse = attention_forward(line, projections, aug_q, aug_k, table)
    (
        result, active, grad_hidden, normed_two, turned, upper, grad_branch, grad_mixed,
        gain_two_sum,
    ) = feed_forward(
        line, own_core, packed, mixed, out_grad, mix_own, mix_other, full_in, full_down, gains[1:]
    )

    in_keep, in_give = contract_quarters(
        line, own_core, normed_two, grad_hidden, data_count
    )
    in_got = swap(in_give, "stream", 1)
    down_keep, down_give = contract_halves(line, own_core, active, out_grad)
    down_got = swap(down_give, "stream", 1)
    mix_keep, mix_give = contract_halves(line, own_core, turned, grad_branch)
    mix_got = swap(mix_give, "stream", 1)
    in_shape = (data_count, 2, 2 * shard_rows, half_width)
    in_keep, in_give = fold(
        line, bit_index("dp", 1), in_keep.reshape(in_shape)[:, :, None],
        in_got.reshape(in_shape)[:, :, None],
    )
    in_got = swap(in_give, "dp", 1)
    down_shape = (data_count, 2, down_keep.shape[0] // data_count // 2, half_width)
    mix_shape = (data_count, 2, mix_rows, half_width)
    rows_keep, rows_give = rows_fold(
        line, own_side, down_keep.reshape(down_shape), down_got.reshape(down_shape),
        mix_keep.reshape(mix_shape), mix_got.reshape(mix_shape),
    )
    rows_got = swap(rows_give, "stream", 2)

    qkv_grads, grad_rel = attention_backward(
        line, projections, mixed, grad_mixed, lse, aug_q, aug_k, mirrored
    )
    rows_shape = (data_count // 2, 2, 1) + rows_keep.shape[1:]
    rows_keep, rows_give = fold(
        line, bit_index("dp", 1), rows_keep.reshape(rows_shape), rows_got.reshape(rows_shape)
    )
    rows_got = swap(rows_give, "dp", 1)
    in_shape = (1, 2, data_count // 2, 2 * shard_rows, half_width)
    in_keep, in_give = fold(line, own_side, in_keep.reshape(in_shape), in_got.reshape(in_shape))
    in_got = swap(in_give, "stream", 2)
    grad_packed, own_columns, other_columns, gain_one_sum = input_grad(
        line, own_core, packed, upper, qkv_grads, matrices, gains[:1]
    )
    other_columns = swap(other_columns, "stream", 1)
    rows_shape = (data_count // 4, 2) + rows_keep.shape[-2:]
    in_shape = (data_count // 4, 2) + in_keep.shape[-2:]
    value, give = rows_fold(
        line, bit_index("dp", 2), rows_keep.reshape(rows_shape), rows_got.reshape(rows_shape),
        in_keep.reshape(in_shape), in_got.reshape(in_shape),
    )
    forward_sum = Sum(line, dp_bits[:-2], value, swap(give, "dp", 2))
    rel = rel_gradient(grad_rel, rel_table.shape[0])
    rel_row = jnp.pad(rel.reshape(1, -1), ((0, 0), (0, width - rel.size)))
    small = jnp.concatenate([gain_one_sum[:1], gain_two_sum[:1], rel_row], axis=0)
    returned = return_rows(
        line, place[:1].reshape(-1, 1), grad_packed, jnp.pad(small, ((0, 5), (0, 0))), capacity
    )
    came_back = lax.all_to_all(returned, "dp", split_axis=0, concat_axis=0, tiled=True)

    table_keep, table_give = layout_grad(
        line, own_side, across, across_other, own_columns, other_columns, data_count, layout_rows
    )
    table_got = swap(table_give, "stream", 2)
    square_keep, square_give = square_grads(
        line, own_core, normed_one, qkv_grads, visual, grad_packed, data_count
    )
    square_got = swap(square_give, "stream", 1)
    square_shape = (data_count, 2, 1, 2 * shard_rows, half_width)
    square_keep, square_give = fold(
        line, own_side, square_keep.reshape(square_shape), square_got.reshape(square_shape)
    )
    square_got = swap(square_give, "stream", 2)
    table_shape = (data_count // 2, 2, 1, table_rows, half_width)
    table_keep, table_give = fold(
        line, bit_index("dp", 1), table_keep.reshape(table_shape), table_got.reshape(table_shape)
    )
    table_got = swap(table_give, "dp", 1)

    def stream_group(value):
        across_sides = swap(value, "stream", 2)
        return (value, swap(value, "stream", 1), across_sides, swap(across_sides, "stream", 1))

    wide_meta = meta.astype(jnp.float32)
    slot_kind = wide_meta[:1]
    slot_index = (wide_meta[11:12] * 16.0 + wide_meta[12:13]).astype(jnp.int32)
    slot_text = (wide_meta[13:14] * 4.0 + wide_meta[14:15]).astype(jnp.int32)

    def slot_keys_of(kind, value):
        keys = jnp.where(slot_kind == kind, value, -1).reshape(data_count, capacity)
        return jnp.pad(keys, ((0, 0), (0, 16)), constant_values=-1)

    text_grad_rows = unpack_text(line, slot_keys_of(2.0, slot_text), came_back, text_index)
    rows_side = swap(text_grad_rows, "stream", 2)
    rows_core = swap(text_grad_rows, "stream", 1)
    square_shape = (data_count // 2, 2, 1, 2 * shard_rows, half_width)
    square_keep, square_give = fold(
        line, bit_index("dp", 1), square_keep.reshape(square_shape),
        square_got.reshape(square_shape),
    )
    square_got = swap(square_give, "dp", 1)
    forward_sum.step()
    rows_both = swap(rows_side, "stream", 1)
    table_shape = (data_count // 4, 2, table_rows, half_width)
    square_shape = (data_count // 4, 2, 2 * shard_rows, half_width)
    value, give = rows_fold(
        line, bit_index("dp", 2), table_keep.reshape(table_shape), table_got.reshape(table_shape),
        square_keep.reshape(square_shape), square_got.reshape(square_shape),
    )
    backward_sum = Sum(line, dp_bits[:-2], value, swap(give, "dp", 2))
    text_grad_rows = (text_grad_rows, rows_side, rows_core, rows_both)
    grad_text = text_grads(line, text_grad_rows, text_table.shape[0])
    backward_sum.step()
    forward_sum.finish()
    forward_group = stream_group(forward_sum.value)
    grad_patches = patch_grads(
        line, slot_keys_of(1.0, slot_index), came_back, matrices, patches.shape[0]
    )
    backward_sum.finish()
    small = [join_small(rows[texts + 16 :]) for rows in text_grad_rows]
    small = (small[0] + small[1]) + (small[2] + small[3])

    shard_down, shard_mix, shard_in = assemble_forward(
        line, stream.reshape(1), forward_group, down_shape[2], mix_rows,
        shard_rows,
    )
    shard_layout, shard_qkv, shard_project = assemble_backward(
        line, stream.reshape(1), stream_group(backward_sum.value), layout_rows, shard_rows
    )
    grad_gains = lax.dynamic_slice_in_dim(
        small[:2], lax.axis_index("dp") * gain_count, gain_count, axis=1
    )
    return (
        result,
        grad_patches,
        grad_text,
        shard_layout,
        shard_project,
        small[2, : rel.size].reshape(rel.shape),
        grad_gains,
        shard_qkv,
        shard_mix.reshape(shard_rows, width),
        shard_in,
        shard_down.reshape(-1, width),
    )


def solution(mesh):
    return jax.shard_map(
        shards,
        mesh=mesh,
        in_specs=(
            P(("dp", "stream"), None),
            P(("dp", "stream")),
            P(("dp", "stream")),
            P(None, ("dp", "stream")),
            P(("dp", "stream")),
            P(("dp", "stream"), None),
            P("dp", None),
            P(None, "dp", None),
            P("dp", None),
            P(),
            P(None, "dp"),
            P(None, "dp", None),
            P("dp", None),
            P("dp", None),
            P("dp", None),
            P(("dp", "stream"), None),
        ),
        out_specs=(
            P(("dp", "stream"), None),
            P(("dp", "stream"), None),
            P("dp", None),
            P(None, "dp", None),
            P("dp", None),
            P(),
            P(None, "dp"),
            P(None, "dp", None),
            P("dp", None),
            P("dp", None),
            P("dp", None),
        ),
        check_vma=False,
    )
```

```python
from functools import partial
import math

import jax
import jax.numpy as jnp
from jax import lax
from jax.experimental import pallas as pl
from jax.experimental.pallas import tpu as pltpu
from jax.sharding import PartitionSpec as P

EPSILON = 1e-06
THRESHOLDS = (12, 16, 23, 32, 46, 64, 91)
BLK = 256
NEG = -1e30
RATE = math.sqrt(2.0 / math.pi)
VMEM_LIMIT = 56 * 2**20
SMALL = pl.CostEstimate(flops=1, bytes_accessed=1, transcendentals=0)


class Line:
    def __init__(self):
        self.last = jnp.zeros((8, 128), jnp.float32)


def launch(
    line, kernel, operands, in_specs, out_shape, out_specs, grid, name, scalars=(), scratch=(), waits=()
):
    held, given, made = len(scalars), len(operands), len(out_shape)
    token = pl.BlockSpec((8, 128), lambda *_: (0, 0))

    def body(*refs):
        outs = held + given + 1 + len(waits)
        refs[outs + made][...] = refs[held + given][...]
        kernel(*refs[: held + given], *refs[outs : outs + made], *refs[outs + made + 1 :])

    out_shape = [jax.ShapeDtypeStruct(value.shape, value.dtype) for value in out_shape]
    results = pl.pallas_call(
        body,
        out_shape=tuple(out_shape) + (jax.ShapeDtypeStruct((8, 128), jnp.float32),),
        grid_spec=pltpu.PrefetchScalarGridSpec(
            num_scalar_prefetch=held,
            grid=grid,
            in_specs=list(in_specs) + [token] + [pl.BlockSpec(memory_space=pl.ANY)] * len(waits),
            out_specs=tuple(out_specs) + (token,),
            scratch_shapes=list(scratch),
        ),
        compiler_params=pltpu.CompilerParams(vmem_limit_bytes=VMEM_LIMIT),
        cost_estimate=SMALL,
        name=name,
    )(*scalars, *operands, line.last, *waits)
    line.last = results[-1]
    return results[:-1]


def fixed(value):
    return pl.BlockSpec(value.shape, lambda *_: (0,) * len(value.shape))


def bf16(*shape):
    return jax.ShapeDtypeStruct(shape, jnp.bfloat16)


def f32(*shape):
    return jax.ShapeDtypeStruct(shape, jnp.float32)


def i32(*shape):
    return jax.ShapeDtypeStruct(shape, jnp.int32)


def bucket_of(relative):
    magnitude = jnp.abs(relative)
    beyond = 8 + sum(((magnitude >= threshold).astype(jnp.int32) for threshold in THRESHOLDS))
    return jnp.where(relative > 0, 16, 0).astype(jnp.int32) + jnp.where(
        magnitude < 8, magnitude, beyond
    )


def dot_nt(a, b):
    return lax.dot_general(a, b, (((1,), (1,)), ((), ())), preferred_element_type=jnp.float32)

def dot_nn(a, b):
    return lax.dot_general(a, b, (((1,), (0,)), ((), ())), preferred_element_type=jnp.float32)

def dot_tn(a, b):
    return lax.dot_general(a, b, (((0,), (0,)), ((), ())), preferred_element_type=jnp.float32)


def pieces(value):
    one = value.astype(jnp.bfloat16)
    rest = value - one.astype(jnp.float32)
    two = rest.astype(jnp.bfloat16)
    three = (rest - two.astype(jnp.float32)).astype(jnp.bfloat16)
    return one, two, three

def put_pieces(base, value, lane):
    one, two, three = pieces(value)
    base = jnp.where(jnp.logical_or(lane == 8, lane == 72), one, base)
    base = jnp.where(jnp.logical_or(lane == 9, lane == 73), two, base)
    return jnp.where(jnp.logical_or(lane == 10, lane == 74), three, base)

def diagonal_sums(block):
    wide = jnp.concatenate([block, jnp.zeros_like(block)], axis=1)
    total = wide[:128]
    for start in range(128, BLK, 128):
        total = total + pltpu.roll(wide[start : start + 128], 2 * BLK - start, 1)
    eight = total[:8]
    for start in range(8, 128, 8):
        eight = eight + pltpu.roll(total[start : start + 8], 2 * BLK - start, 1)
    one = eight[:1]
    for row in range(1, 8):
        one = one + pltpu.roll(eight[row : row + 1], 2 * BLK - row, 1)
    return one


def window_of(block, count):
    low = max(0, block * BLK - 2 * BLK + 1) // BLK
    high = min(count - 1, (block * BLK + BLK - 1 + 2 * BLK - 1) // BLK)
    return low, high + 1

def fill_strip(strip, table, slot, count):
    middle = (count - 1) * BLK
    for step in (-1, 0, 1):
        window = table[slot : slot + 1, BLK * step + BLK : BLK * step + 3 * BLK]
        spread = jnp.broadcast_to(window, (BLK, 2 * BLK))
        start = middle + step * BLK
        strip[slot, :, start : start + BLK] = pltpu.roll(spread, 0, 1, stride=1, stride_axis=0)[:, BLK:]
    low = jnp.broadcast_to(table[slot : slot + 1, 0:1], (BLK, middle - BLK))
    high = jnp.broadcast_to(table[slot : slot + 1, 4 * BLK - 1 : 4 * BLK], (BLK, middle - BLK))
    strip[slot, :, 0 : middle - BLK] = low
    strip[slot, :, middle + 2 * BLK :] = high

def forward_kernel(q_ref, k_ref, v_ref, aug_q, aug_k, table, out_ref, lse_ref, strip, ka, va):
    length = q_ref.shape[0]
    count = length // BLK
    lane = lax.broadcasted_iota(jnp.int32, (1, 128), 1)
    left = lane < 64
    for h in range(2):
        fill_strip(strip, table, h, count)
        mine = left if h == 0 else jnp.logical_not(left)
        ka[h] = jnp.where(mine, k_ref[...], aug_k[...])
        va[h] = jnp.where(mine, v_ref[...], aug_k[...])
    for qb in range(count):
        rows = slice(qb * BLK, qb * BLK + BLK)
        low, high = window_of(qb, count)
        keys = slice(low * BLK, high * BLK)
        offset = (count - 1 - qb) * BLK
        query = q_ref[rows, :] * jnp.bfloat16(0.125)
        outs = []
        lses = []
        for h in range(2):
            qa = jnp.where(left if h == 0 else jnp.logical_not(left), query, aug_q[rows, :])
            s = dot_nt(qa, ka[h, keys, :]) + strip[h, :, offset + low * BLK : offset + high * BLK]
            peak = jnp.max(s, axis=1, keepdims=True)
            p = jnp.exp(s - peak).astype(jnp.bfloat16)
            acc = dot_nn(p, va[h, keys, :])
            mark = 72 if h == 0 else 8
            total = acc[:, mark : mark + 1]
            outs.append(acc / total)
            lses.append(jnp.broadcast_to(peak + jnp.log(total), (BLK, 128)))
        out_ref[rows, :] = jnp.where(left, outs[0], outs[1]).astype(jnp.bfloat16)
        lse_ref[rows, :] = jnp.where(left, lses[0], lses[1])

def put_blocks(ref, slot, first, value, held):
    for n in range(value.shape[1] // BLK):
        cut = slice((first + n) * BLK, (first + n) * BLK + BLK)
        part = value[:, n * BLK : n * BLK + BLK]
        if first + n in held:
            ref[slot, :, cut] += part
        else:
            ref[slot, :, cut] = part


def backward_kernel(
    q_ref, k_ref, v_ref, mixed_ref, grad_ref, lse_ref, aug_q, aug_k, table,
    grads_ref, rel_ref,
    strip, rel, ka, va, qa, ga, dq_acc,
):
    length = q_ref.shape[0]
    count = length // BLK
    middle = (count - 1) * BLK
    lane = lax.broadcasted_iota(jnp.int32, (1, 128), 1)
    left = lane < 64
    rel_blocks, dq_blocks = set(), set()
    inner = mixed_ref[...].astype(jnp.float32) * grad_ref[...].astype(jnp.float32)
    query = q_ref[...] * jnp.bfloat16(0.125)
    for h in range(2):
        fill_strip(strip, table, h, count)
        mine = left if h == 0 else jnp.logical_not(left)
        ka[h] = jnp.where(mine, k_ref[...], aug_k[...])
        va[h] = jnp.where(mine, v_ref[...], aug_k[...])
        at = 0 if h == 0 else 64
        qa[h] = jnp.where(mine, query, put_pieces(aug_q[...], -lse_ref[:, at : at + 1], lane))
        delta = jnp.sum(jnp.where(mine, inner, 0.0), axis=1, keepdims=True)
        spare = put_pieces(jnp.zeros((length, 128), jnp.bfloat16), -delta, lane)
        ga[h] = jnp.where(mine, grad_ref[...], spare)
    for kb in range(count):
        keys = slice(kb * BLK, kb * BLK + BLK)
        low, high = window_of(kb, count)
        rows = slice(low * BLK, high * BLK)
        offset = middle - kb * BLK
        cut = slice(offset + low * BLK, offset + high * BLK)
        dks, dvs = [], []
        for h in range(2):
            s = dot_nt(ka[h, keys, :], qa[h, rows, :]) + strip[h, :, cut]
            p = jnp.exp(s)
            ds = p * dot_nt(va[h, keys, :], ga[h, rows, :])
            put_blocks(rel, h, offset // BLK + low, ds, rel_blocks)
            p = p.astype(jnp.bfloat16)
            ds = ds.astype(jnp.bfloat16)
            dvs.append(dot_nn(p, ga[h, rows, :]))
            dks.append(dot_nn(ds, qa[h, rows, :]))
            put_blocks(dq_acc, h, low, dot_tn(ka[h, keys, :], ds), dq_blocks)
        rel_blocks.update(range(offset // BLK + low, offset // BLK + high))
        dq_blocks.update(range(low, high))
        grads_ref[1, keys, :] = jnp.where(left, dks[0], dks[1]).astype(jnp.bfloat16)
        grads_ref[2, keys, :] = jnp.where(left, dvs[0], dvs[1]).astype(jnp.bfloat16)
    row = lax.broadcasted_iota(jnp.int32, (128, 1), 0)
    dq = jnp.where(row < 64, dq_acc[0], dq_acc[1]).T
    grads_ref[0] = (dq * 0.125).astype(jnp.bfloat16)
    for h in range(2):
        out = []
        for place in range(5):
            start = middle + (2 - place) * BLK
            if place in (0, 4):
                near = middle // BLK
                summed = jnp.zeros((1, BLK), jnp.float32)
                for block in sorted(rel_blocks):
                    if (block >= near + 2) if place == 0 else (block <= near - 2):
                        part = rel[h, :, block * BLK : block * BLK + BLK]
                        summed = summed + jnp.sum(part, axis=0, keepdims=True)
                out.append(jnp.concatenate([summed, jnp.zeros_like(summed)], axis=1))
            else:
                out.append(diagonal_sums(rel[h, :, start : start + BLK]))
        rel_ref[h] = jnp.concatenate(out + [jnp.zeros((3, 2 * BLK), jnp.float32)], axis=0)


def attention_forward(line, qkv, aug_q, aug_k, table):
    _, length, width = qkv.shape
    col = pl.BlockSpec((length, 128), lambda p: (0, p))
    buf = pltpu.VMEM((2, length, 128), jnp.bfloat16)
    return launch(
        line, forward_kernel, (qkv, qkv, qkv, aug_q, aug_k, table),
        [
            pl.BlockSpec((None, length, 128), lambda p: (0, 0, p)),
            pl.BlockSpec((None, length, 128), lambda p: (1, 0, p)),
            pl.BlockSpec((None, length, 128), lambda p: (2, 0, p)),
            fixed(aug_q), fixed(aug_k),
            pl.BlockSpec((None, 2, table.shape[2]), lambda p: (p, 0, 0)),
        ],
        (bf16(length, width), f32(length, width)), (col, col), (width // 128,),
        "attention_forward",
        scratch=[pltpu.VMEM((2, BLK, 2 * length - BLK), jnp.float32), buf, buf],
    )


def attention_backward(line, qkv, mixed, grad_mixed, lse, aug_q, aug_k, table):
    _, length, width = qkv.shape
    col = pl.BlockSpec((length, 128), lambda p: (0, p))
    buf = pltpu.VMEM((2, length, 128), jnp.bfloat16)
    strip = pltpu.VMEM((2, BLK, 2 * length - BLK), jnp.float32)
    return launch(
        line, backward_kernel,
        (qkv, qkv, qkv, mixed, grad_mixed, lse, aug_q, aug_k, table),
        [
            pl.BlockSpec((None, length, 128), lambda p: (0, 0, p)),
            pl.BlockSpec((None, length, 128), lambda p: (1, 0, p)),
            pl.BlockSpec((None, length, 128), lambda p: (2, 0, p)),
            col, col, col, fixed(aug_q), fixed(aug_k),
            pl.BlockSpec((None, 2, table.shape[2]), lambda p: (p, 0, 0)),
        ],
        (bf16(3, length, width), f32(width // 64, 8, 2 * BLK)),
        (
            pl.BlockSpec((3, length, 128), lambda p: (0, 0, p)),
            pl.BlockSpec((2, 8, 2 * BLK), lambda p: (p, 0, 0)),
        ),
        (width // 128,), "attention_backward",
        scratch=[strip, strip, buf, buf, buf, buf, pltpu.VMEM((2, 128, length), jnp.float32)],
    )


def bucket_choice(offsets, count):
    return (bucket_of(offsets)[:, None] == jnp.arange(count, dtype=jnp.int32)[None, :]).astype(jnp.float32)

def prepare(segments, rel_table):
    heads = rel_table.shape[1]
    offsets = jnp.arange(4 * BLK, dtype=jnp.int32) - 2 * BLK
    tables = []
    for sign in (1, -1):
        choose = bucket_choice(sign * offsets, rel_table.shape[0])
        table = lax.dot_general(rel_table, choose, (((0,), (1,)), ((), ())), precision=lax.Precision.HIGHEST)
        tables.append(table.reshape(heads // 2, 2, 4 * BLK))
    lane = (jnp.arange(128, dtype=jnp.int32) % 64)[None, :]
    row = segments.reshape(-1)[:, None]
    same = lane == row
    aug_q = jnp.where(jnp.logical_or(same, lane >= 8), 0.0, NEG).astype(jnp.bfloat16)
    aug_k = jnp.where(jnp.logical_or(same, jnp.logical_and(lane >= 8, lane < 11)), 1.0, 0.0).astype(jnp.bfloat16)
    return aug_q, aug_k, tables[0], tables[1]

def rel_gradient(rel, count):
    lane = jnp.arange(2 * BLK, dtype=jnp.int32)
    parts = []
    for place in range(5):
        if place == 0:
            offset = jnp.full((2 * BLK,), -600, jnp.int32)
        elif place == 4:
            offset = jnp.full((2 * BLK,), 600, jnp.int32)
        else:
            offset = BLK * (place - 2) - jnp.where(lane < BLK, lane, lane - 2 * BLK)
        parts.append(bucket_choice(offset, count))
    choose = jnp.concatenate(parts + [jnp.zeros((3 * 2 * BLK, count), jnp.float32)], axis=0)
    flat = rel.reshape(rel.shape[0], -1)
    return lax.dot_general(choose, flat, (((0,), (1,)), ((), ())), precision=lax.Precision.HIGHEST)


def iota(shape, axis):
    return lax.broadcasted_iota(jnp.int32, shape, axis)


def as_bf16(flag):
    return jnp.where(flag, 1.0, 0.0).astype(jnp.bfloat16)


def slots_kernel(owners, capacity, shift, place_ref, kind_ref, index_ref, coords_ref,
                 meta_ref, keys_ref, text_ref):
    tokens = place_ref.shape[1]
    place = place_ref[...]
    text = kind_ref[...] == 1
    owner = jnp.right_shift(place, shift)
    position = jnp.bitwise_and(place, (1 << shift) - 1)
    rows = owners + 16
    row = iota((rows, tokens), 0)
    member = jnp.logical_or(row == owner, jnp.logical_and(row == owners, text))
    upto = as_bf16(iota((tokens, tokens), 0) <= iota((tokens, tokens), 1))
    counts = dot_nn(as_bf16(member), upto)
    rank = jnp.sum(jnp.where(row == owner, counts, 0.0), axis=0, keepdims=True)
    rank = rank.astype(jnp.int32) - 1
    text_rank = jnp.where(text, counts[owners : owners + 1].astype(jnp.int32) - 1, 0)
    slot = owner * capacity + rank
    index = index_ref[...]
    coords = coords_ref[...]
    low = jnp.bitwise_and(coords, 3)
    high = jnp.right_shift(coords, 2)
    meta = jnp.concatenate(
        [
            kind_ref[...] + 1,
            jnp.right_shift(position, 2), jnp.bitwise_and(position, 3),
            high, low,
            jnp.right_shift(index, 4), jnp.bitwise_and(index, 15),
            jnp.right_shift(text_rank, 2), jnp.bitwise_and(text_rank, 3),
            jnp.zeros_like(index),
        ],
        axis=0,
    ).astype(jnp.float32).astype(jnp.bfloat16)
    slots = meta_ref.shape[1]
    for start in range(0, slots, 512):
        pick = as_bf16(iota((512, tokens), 0) + start == slot)
        meta_ref[:, start : start + 512] = dot_nt(meta, pick).astype(jnp.bfloat16)
        down = dot_nt(pick, meta)
        index = down[:, 11:12] * 16.0 + down[:, 12:13]
        rank = down[:, 13:14] * 4.0 + down[:, 14:15] + float(tokens - text_ref.shape[1])
        key = jnp.where(down[:, 0:1] > 1.5, rank, jnp.where(down[:, 0:1] > 0.5, index, -1.0))
        keys_ref[start : start + 512, :] = jnp.broadcast_to(key.astype(jnp.int32), (512, 8))
    texts = text_ref.shape[1]
    chosen = as_bf16(jnp.logical_and(iota((texts, tokens), 0) == text_rank, text))
    found = dot_nt(meta, chosen)
    text_ref[...] = jnp.broadcast_to(
        (found[11:12] * 16.0 + found[12:13]).astype(jnp.int32), text_ref.shape
    )


def find_slots(line, owners, capacity, shift, placing, src_kind, src_index, coords, texts):
    slots = owners * capacity
    operands = (placing.reshape(1, -1), src_kind.reshape(1, -1), src_index.reshape(1, -1), coords)
    shapes = (bf16(16, slots), i32(slots, 8), i32(8, texts))
    return launch(
        line, partial(slots_kernel, owners, capacity, shift), operands,
        [fixed(value) for value in operands], shapes, [fixed(value) for value in shapes], (1,),
        "find_slots",
    )


def unpack_kernel(key_ref, rows_ref, index_ref, out_ref):
    texts, tokens = index_ref.shape[1], rows_ref.shape[1]
    count, width = rows_ref.shape[0], out_ref.shape[1]
    total = None
    small = None
    for d in range(count):
        pick = as_bf16(iota((texts, tokens), 0) == key_ref[d : d + 1, :])
        part = dot_nn(pick, rows_ref[d])
        total = part if total is None else total + part
        part = join_small(rows_ref[d, tokens - 16 :, :])
        small = part if small is None else small + part
    out_ref[:texts, :] = total.astype(jnp.bfloat16)
    index = index_ref[...]
    row = iota((16, texts), 0)
    high = jnp.broadcast_to(jnp.right_shift(index[0:1], 4), (16, texts))
    low = jnp.broadcast_to(jnp.bitwise_and(index[0:1], 15), (16, texts))
    index = jnp.where(row == 0, high, jnp.where(row == 1, low, 0)).astype(jnp.float32)
    index = jnp.concatenate([index, jnp.zeros((16, width - texts), jnp.float32)], axis=1)
    out_ref[texts : texts + 16, :] = index.astype(jnp.bfloat16)
    out_ref[texts + 16 :, :] = split_small(small)


def unpack_text(line, keys, rows, index):
    width = rows.shape[2]
    shape = bf16(index.shape[1] + 32, width)
    return launch(
        line, unpack_kernel, (keys, rows, index), [fixed(keys), fixed(rows), fixed(index)],
        (shape,), (fixed(shape),), (1,), "unpack_text",
    )[0]


def pack_kernel(key_ref, patch_ref, text_ref, *refs):
    out_ref = refs[len(refs) // 2]
    size, patches, texts = out_ref.shape[0], patch_ref.shape[0], text_ref.shape[0]
    key = key_ref[:, 0:1]
    out = dot_nn(as_bf16(iota((size, patches), 1) == key), patch_ref[...])
    out = out + dot_nn(as_bf16(iota((size, texts), 1) + patches == key), text_ref[...])
    out_ref[...] = out.astype(jnp.bfloat16)

    @pl.when(pl.program_id(0) == 0)
    def _():
        for n in range(len(refs) // 2):
            refs[len(refs) // 2 + 1 + n][...] = refs[n][...]


def pack(line, keys, patches, text_rows, later):
    slots = keys.shape[0]
    width = patches.shape[1]
    return launch(
        line, pack_kernel, (keys, patches, text_rows) + later,
        [pl.BlockSpec((512, 8), lambda i: (i, 0)), fixed(patches), fixed(text_rows)]
        + [fixed(value) for value in later],
        (bf16(slots, width),) + later,
        (pl.BlockSpec((512, width), lambda i: (i, 0)),) + tuple(fixed(value) for value in later),
        (slots // 512,), "pack",
    )


def place_kernel(meta_ref, column_ref, row_ref, place_ref):
    slots, tokens = meta_ref.shape[1], row_ref.shape[1]
    meta = meta_ref[...]
    wide = meta.astype(jnp.float32)
    place = (wide[1:2] * 4.0 + wide[2:3]).astype(jnp.int32)
    place = jnp.where(wide[0:1] > 0.5, place, -1)
    place_ref[...] = jnp.broadcast_to(place, place_ref.shape)
    for start in range(0, tokens, 256):
        pick = as_bf16(iota((256, slots), 0) + start == place)
        down = dot_nt(pick, meta)
        values = [down[:, 0:1]] + [down[:, 3 + c : 4 + c] * 4.0 + down[:, 7 + c : 8 + c] for c in range(4)]
        lane = iota((256, 8), 1)
        block = jnp.zeros((256, 8), jnp.float32)
        for c in range(5):
            block = jnp.where(lane == c, values[c], block)
        column_ref[start : start + 256, :] = block.astype(jnp.int32)
        across = dot_nt(meta, pick)
        row_ref[:, start : start + 256] = jnp.concatenate(
            [across[0:1], across[3:7] * 4.0 + across[7:11], jnp.zeros((3, 256), jnp.float32)], axis=0
        ).astype(jnp.int32)


def place_meta(line, meta, tokens):
    shapes = (i32(tokens, 8), i32(8, tokens), i32(8, meta.shape[1]))
    return launch(
        line, place_kernel, (meta,), [fixed(meta)], shapes, [fixed(value) for value in shapes],
        (1,), "place_meta",
    )


def lookup_kernel(rows, fresh, side, mine_ref, other_ref, table_ref, *refs):
    width = table_ref.shape[2]
    outs = refs[-2:]
    entries = table_ref.shape[0] * rows
    for n, coords in enumerate((mine_ref, other_ref)):
        total = jnp.zeros(outs[n].shape, jnp.float32) if fresh else refs[n][...]
        for k in range(2):
            key = jnp.where(side[0] == 0, coords[:, k + 1 : k + 2], coords[:, k + 3 : k + 4])
            pick = as_bf16(iota((total.shape[0], entries), 1) == key)
            table = table_ref[:, k * rows : k * rows + rows, :].reshape(entries, width)
            total = total + dot_nn(pick, table)
        outs[n][...] = total


def layout_lookup(line, side, mine, other, columns, rows, sums=()):
    tokens = mine.shape[0]
    width = columns.shape[2]
    column = pl.BlockSpec((256, 8), lambda i, s: (i, 0))
    out = pl.BlockSpec((256, width), lambda i, s: (i, 0))
    return launch(
        line, partial(lookup_kernel, rows, not sums), (mine, other, columns, *sums),
        [column, column, fixed(columns)] + [out] * len(sums),
        (f32(tokens, width), f32(tokens, width)), (out, out), (tokens // 256,), "layout_lookup",
        scalars=(side,),
    )


def embed_kernel(place_ref, column_ref, arrived_ref, own_ref, got_ref, half_ref, project_ref,
                 gain_ref, weight_ref, visual_ref, packed_ref, normed_ref, out_ref):
    rows, slots = packed_ref.shape[0], arrived_ref.shape[0]
    pick = as_bf16(iota((rows, slots), 0) + pl.program_id(0) * rows == place_ref[0:1, :])
    raw = dot_nn(pick, arrived_ref[...])
    narrow = raw.astype(jnp.bfloat16)
    kind = column_ref[:, 0:1]
    visual_ref[...] = jnp.where(kind == 1, raw, 0.0).astype(jnp.bfloat16).T
    projected = dot_nn(narrow, project_ref[...])
    first = half_ref[0:1, 0:1] == 0
    own, got = own_ref[...], got_ref[...]
    layout = jnp.concatenate([jnp.where(first, own, got), jnp.where(first, got, own)], axis=1)
    embedded = jnp.where(kind == 2, raw, projected) + layout
    packed_ref[...] = embedded.astype(jnp.bfloat16)
    packed = packed_ref[...].astype(jnp.float32)
    scale = lax.rsqrt(jnp.mean(packed * packed, axis=-1, keepdims=True) + EPSILON)
    normed = (packed * scale * gain_ref[0:1, :].astype(jnp.float32)).astype(jnp.bfloat16)
    normed_ref[...] = normed.T
    for part in range(3):
        out_ref[part] = dot_nn(normed, weight_ref[part]).astype(jnp.bfloat16)


def embed(line, places, column, arrived, own, got, half, matrices, gains, tokens):
    width = arrived.shape[1]
    rows = 256
    wide = pl.BlockSpec((rows, width), lambda i: (i, 0))
    part = pl.BlockSpec((rows, own.shape[1]), lambda i: (i, 0))
    across = pl.BlockSpec((width, rows), lambda i: (0, i))
    return launch(
        line, embed_kernel, (places, column, arrived, own, got, half, matrices, gains, matrices),
        [
            fixed(places), pl.BlockSpec((rows, 8), lambda i: (i, 0)), fixed(arrived), part, part,
            fixed(half), pl.BlockSpec((None, width, width), lambda i: (3, 0, 0)), fixed(gains),
            pl.BlockSpec((3, width, width), lambda i: (0, 0, 0)),
        ],
        (bf16(width, tokens), bf16(tokens, width), bf16(width, tokens), bf16(3, tokens, width)),
        (across, wide, across, pl.BlockSpec((3, rows, width), lambda i: (0, i, 0))),
        (tokens // rows,), "embed",
    )


def input_grad_kernel(which, packed_ref, upper_ref, grads_ref, weight_ref, gain_ref,
                      out_ref, own_ref, other_ref, sum_ref):
    total = dot_nt(grads_ref[0], weight_ref[0])
    total = total + dot_nt(grads_ref[1], weight_ref[1])
    total = total + dot_nt(grads_ref[2], weight_ref[2])
    packed = packed_ref[...].astype(jnp.float32)
    scale = lax.rsqrt(jnp.mean(packed * packed, axis=-1, keepdims=True) + EPSILON)
    unit = packed * scale
    back = total * gain_ref[0:1, :].astype(jnp.float32)
    back = scale * (back - unit * jnp.mean(back * unit, axis=-1, keepdims=True))
    back = back + upper_ref[...]
    out_ref[...] = back.astype(jnp.bfloat16)
    put_halves(which, back, own_ref, other_ref)

    @pl.when(pl.program_id(0) == 0)
    def _():
        sum_ref[...] = jnp.zeros_like(sum_ref)

    sum_ref[0:1, :] += jnp.sum(total * unit, axis=0, keepdims=True)


def input_grad(line, which, packed, upper, grads, matrices, gains):
    tokens, width = packed.shape
    rows = 256
    half = width // 2
    wide = pl.BlockSpec((rows, width), lambda i, w: (i, 0))
    part = pl.BlockSpec((rows, half), lambda i, w: (i, 0))
    return launch(
        line, input_grad_kernel, (packed, upper, grads, matrices, gains),
        [
            wide, wide, pl.BlockSpec((3, rows, width), lambda i, w: (0, i, 0)),
            pl.BlockSpec((3, width, width), lambda i, w: (0, 0, 0)), fixed(gains),
        ],
        (bf16(tokens, width), bf16(tokens, half), bf16(tokens, half), f32(8, width)),
        (wide, part, part, pl.BlockSpec((8, width), lambda i, w: (0, 0))),
        (tokens // rows,), "input_grad", scalars=(which,),
    )


def split_small(small):
    parts = [part.astype(jnp.float32) for part in pieces(small)]
    pad = jnp.zeros((16 - 3 * small.shape[0], small.shape[1]), jnp.float32)
    return jnp.concatenate(parts + [pad], axis=0).astype(jnp.bfloat16)


def join_small(rows):
    rows = rows[:9].astype(jnp.float32)
    return rows[0:3] + rows[3:6] + rows[6:9]


def return_kernel(place_ref, rows_ref, small_ref, out_ref):
    slots = place_ref.shape[0]
    devices, capacity = out_ref.shape[0], out_ref.shape[1] - 16
    pick = as_bf16(iota((slots, rows_ref.shape[0]), 1) == place_ref[...])
    rows = dot_nn(pick, rows_ref[...]).astype(jnp.bfloat16)
    small = split_small(small_ref[0:3, :])
    for d in range(devices):
        out_ref[d, :capacity, :] = rows[d * capacity : d * capacity + capacity]
        out_ref[d, capacity:, :] = small


def return_rows(line, places, rows, small, capacity):
    count = places.shape[0] // capacity
    width = rows.shape[1]
    step = max(1, min(count, 512 // capacity))
    return launch(
        line, return_kernel, (places, rows, small),
        [pl.BlockSpec((step * capacity, 1), lambda i: (i, 0)), fixed(rows), fixed(small)],
        (bf16(count, capacity + 16, width),),
        (pl.BlockSpec((step, capacity + 16, width), lambda i: (i, 0, 0)),), (count // step,),
        "return_rows",
    )[0]


def layout_grad_kernel(side, mine_ref, other_ref, first_ref, second_ref, keep_ref, give_ref):
    pair = pl.program_id(0)
    shards, rows, width = keep_ref.shape
    entries = shards * rows
    table = 2 * jnp.where(pair < 2, 1 - side[0], side[0]) + jnp.bitwise_and(pair, 1)
    total = jnp.zeros((entries, width), jnp.float32)
    for coords, grads in ((mine_ref, first_ref), (other_ref, second_ref)):
        tokens = grads.shape[0]
        key = coords[pl.ds(table + 1, 1), :]
        pick = as_bf16(iota((entries, tokens), 0) + pl.program_id(1) * entries == key)
        total = total + dot_nn(pick, grads[...])
    total = total.reshape(shards, rows, width).astype(jnp.bfloat16)

    @pl.when(pair < 2)
    def _():
        give_ref[...] = total

    @pl.when(pair >= 2)
    def _():
        keep_ref[...] = total


def layout_grad(line, side, mine, other, first, second, shards, rows):
    width = first.shape[1]
    step = max(1, min(shards, 512 // rows))
    last = shards // step - 1
    block = (step, None, rows, width)
    shape = bf16(shards, 2, rows, width)
    return launch(
        line, layout_grad_kernel, (mine, other, first, second),
        [fixed(mine), fixed(other), fixed(first), fixed(second)], (shape, shape),
        (
            pl.BlockSpec(
                block, lambda t, i, s: (jnp.where(t < 2, 0, i), jnp.maximum(t - 2, 0), 0, 0)
            ),
            pl.BlockSpec(
                block, lambda t, i, s: (jnp.where(t < 2, i, last), jnp.minimum(t, 1), 0, 0)
            ),
        ),
        (4, shards // step), "layout_grad", scalars=(side,),
    )


def patch_kernel(key_ref, rows_ref, weight_ref, grad_ref):
    patches, tokens = grad_ref.shape[0], rows_ref.shape[1]
    total = None
    for d in range(rows_ref.shape[0]):
        pick = as_bf16(iota((patches, tokens), 0) == key_ref[d : d + 1, :])
        part = dot_nn(pick, rows_ref[d])
        total = part if total is None else total + part
    grad_ref[...] = dot_nt(total.astype(jnp.bfloat16), weight_ref[...])


def patch_grads(line, keys, rows, matrices, patches):
    width = rows.shape[2]
    shape = f32(patches, width)
    return launch(
        line, patch_kernel, (keys, rows, matrices),
        [fixed(keys), fixed(rows), pl.BlockSpec((None, width, width), lambda i: (3, 0, 0))],
        (shape,), (fixed(shape),), (1,), "patch_grads",
    )[0]


def text_kernel(*refs):
    out_ref = refs[4]
    size = out_ref.shape[0]
    parts = []
    for rows_ref in refs[:4]:
        texts = rows_ref.shape[0] - 32
        index = rows_ref[texts : texts + 16, :texts].astype(jnp.float32)
        key = (index[0:1] * 16.0 + index[1:2]).astype(jnp.int32)
        place = iota((size, texts), 0) + pl.program_id(0) * size
        parts.append(dot_nn(as_bf16(place == key), rows_ref[:texts, :]))
    out_ref[...] = (parts[0] + parts[1]) + (parts[2] + parts[3])


def text_grads(line, rows, entries):
    width = rows[0].shape[1]
    size = 512
    return launch(
        line, text_kernel, rows, [fixed(value) for value in rows],
        (f32(entries, width),), (pl.BlockSpec((size, width), lambda i: (i, 0)),),
        (pl.cdiv(entries, size),), "text_grads",
    )[0]


def feed_forward_kernel(core, packed_ref, mixed_ref, grad_ref, own_ref, other_ref, in_ref, down_ref,
                        gain_ref, result_ref, active_ref, hidden_ref, normed_ref, turned_ref, upper_ref,
                        branch_ref, back_ref, sum_ref):
    own, other = own_ref[...], other_ref[...]
    first = core[0] == 0
    mix = jnp.concatenate([jnp.where(first, own, other), jnp.where(first, other, own)], axis=1)
    attended = packed_ref[...].astype(jnp.float32) + dot_nn(mixed_ref[...], mix)
    turned_ref[...] = mixed_ref[...].T
    scale = lax.rsqrt(jnp.mean(attended * attended, axis=-1, keepdims=True) + EPSILON)
    unit = attended * scale
    gain = gain_ref[0:1, :].astype(jnp.float32)
    normed = (unit * gain).astype(jnp.bfloat16)
    normed_ref[...] = normed.T
    out_grad = grad_ref[...]
    result = attended
    back = jnp.zeros_like(attended)
    width = attended.shape[1]
    for part in range(in_ref.shape[0]):
        cut = slice(part * width, part * width + width)
        hidden = dot_nn(normed, in_ref[part])
        square = hidden * hidden
        tanh = jnp.tanh(hidden * (RATE + RATE * 0.044715 * square))
        half = 0.5 + 0.5 * tanh
        active = (hidden * half).astype(jnp.bfloat16)
        active_ref[cut, :] = active.T
        slope = half + hidden * half * (1.0 - tanh) * (RATE + 3.0 * 0.044715 * RATE * square)
        result = result + dot_nn(active, down_ref[cut, :])
        grad_hidden = (dot_nt(out_grad, down_ref[cut, :]) * slope).astype(jnp.bfloat16)
        hidden_ref[:, cut] = grad_hidden
        back = back + dot_nt(grad_hidden, in_ref[part])
    result_ref[...] = result.astype(jnp.bfloat16)

    @pl.when(pl.program_id(0) == 0)
    def _():
        sum_ref[...] = jnp.zeros_like(sum_ref)

    sum_ref[0:1, :] += jnp.sum(back * unit, axis=0, keepdims=True)
    back = back * gain
    back = scale * (back - unit * jnp.mean(back * unit, axis=-1, keepdims=True))
    back = back + out_grad.astype(jnp.float32)
    upper_ref[...] = back
    branch = back.astype(jnp.bfloat16)
    branch_ref[...] = branch
    back_ref[...] = dot_nt(branch, mix).astype(jnp.bfloat16)


def feed_forward(line, core, packed, mixed, out_grad, mix_own, mix_other, full_in, full_down, gains):
    tokens, width = packed.shape
    hidden = full_down.shape[0]
    rows = 256
    wide = pl.BlockSpec((rows, width), lambda i, c: (i, 0))
    tall = pl.BlockSpec((rows, hidden), lambda i, c: (i, 0))
    across = pl.BlockSpec((width, rows), lambda i, c: (0, i))
    narrow, turned = bf16(tokens, width), bf16(width, tokens)
    operands = (packed, mixed, out_grad, mix_own, mix_other, full_in, full_down, gains)
    return launch(
        line, feed_forward_kernel, operands,
        [wide, wide, wide] + [fixed(value) for value in operands[3:]],
        (
            narrow, bf16(hidden, tokens), bf16(tokens, hidden), turned, turned,
            f32(tokens, width), narrow, narrow, f32(8, width),
        ),
        (
            wide, pl.BlockSpec((hidden, rows), lambda i, c: (0, i)), tall, across, across,
            wide, wide, wide, pl.BlockSpec((8, width), lambda i, c: (0, 0)),
        ),
        (tokens // rows,), "feed_forward", scalars=(core,),
    )


def put_halves(which, total, keep_ref, give_ref):
    half = total.shape[1] // 2
    first, second = total[:, :half], total[:, half:]
    mine = which[0] == 0
    keep_ref[...] = jnp.where(mine, first, second).astype(jnp.bfloat16)
    give_ref[...] = jnp.where(mine, second, first).astype(jnp.bfloat16)


def contract_halves_kernel(which, left_ref, right_ref, keep_ref, give_ref):
    put_halves(which, dot_nn(left_ref[...], right_ref[...]), keep_ref, give_ref)


def contract_halves(line, which, left, right):
    count, tokens = left.shape
    width = right.shape[1]
    size, half = min(count, width), width // 2
    out = pl.BlockSpec((size, half), lambda i, w: (i, 0))
    shape = bf16(count, half)
    return launch(
        line, contract_halves_kernel, (left, right),
        [pl.BlockSpec((size, tokens), lambda i, w: (i, 0)), fixed(right)],
        (shape, shape), (out, out), (count // size,), "contract_halves", scalars=(which,),
    )


def contract_quarters_kernel(which, left_ref, right_ref, keep_ref, give_ref):
    del which
    total = dot_nn(left_ref[...], right_ref[...])
    shards, _, rows, half = keep_ref.shape

    def put(out_ref):
        for d in range(shards):
            for h in range(2):
                part = total[d * rows : d * rows + rows, h * half : h * half + half]
                out_ref[d, h] = part.astype(jnp.bfloat16)

    @pl.when(pl.program_id(0) < 2)
    def _():
        put(give_ref)

    @pl.when(pl.program_id(0) >= 2)
    def _():
        put(keep_ref)


def contract_quarters(line, which, left, right, shards):
    count, tokens = left.shape
    quarter = right.shape[1] // 4
    block = (shards, 2, count // shards, quarter // 2)
    shape = bf16(2, *block)

    def column(i, w):
        return (0, jnp.where(i < 2, 2 * i + 1 - w[0], 2 * (i - 2) + w[0]))

    return launch(
        line, contract_quarters_kernel, (left, right),
        [fixed(left), pl.BlockSpec((tokens, quarter), column)], (shape, shape),
        (
            pl.BlockSpec((None,) + block, lambda i, w: (jnp.maximum(i - 2, 0), 0, 0, 0, 0)),
            pl.BlockSpec((None,) + block, lambda i, w: (jnp.minimum(i, 1), 0, 0, 0, 0)),
        ),
        (4,), "contract_quarters", scalars=(which,),
    )


def square_kernel(which, normed_ref, grads_ref, visual_ref, packed_ref, keep_ref, give_ref):
    shards, rows, half = keep_ref.shape

    def put(total):
        mine = which[0] == 0
        for d in range(shards):
            part = total[d * rows : d * rows + rows]
            first, second = part[:, :half], part[:, half:]
            keep_ref[d] = jnp.where(mine, first, second).astype(jnp.bfloat16)
            give_ref[d] = jnp.where(mine, second, first).astype(jnp.bfloat16)

    @pl.when(pl.program_id(0) < 3)
    def _():
        put(dot_nn(normed_ref[...], grads_ref[...]))

    @pl.when(pl.program_id(0) == 3)
    def _():
        put(dot_nn(visual_ref[...], packed_ref[...]))


def square_grads(line, which, normed, grads, visual, grad_packed, shards):
    width, tokens = normed.shape
    rows, half = width // shards, width // 2
    out = pl.BlockSpec((shards, None, None, rows, half), lambda m, w: (0, m // 2, m % 2, 0, 0))
    shape = bf16(shards, 2, 2, rows, half)
    return launch(
        line, square_kernel, (normed, grads, visual, grad_packed),
        [
            fixed(normed),
            pl.BlockSpec((None, tokens, width), lambda m, w: (jnp.minimum(m, 2), 0, 0)),
            fixed(visual), fixed(grad_packed),
        ],
        (shape, shape), (out, out), (4,), "square_grads", scalars=(which,),
    )


def fold_kernel(bit, value_ref, got_ref, keep_ref, give_ref):
    del bit
    total = value_ref[...].astype(jnp.float32) + got_ref[...].astype(jnp.float32)

    @pl.when(pl.program_id(0) == 0)
    def _():
        give_ref[...] = total.astype(give_ref.dtype)

    @pl.when(pl.program_id(0) == 1)
    def _():
        keep_ref[...] = total.astype(keep_ref.dtype)


def fold(line, bit, value, got):
    a, _, b, rows, width = value.shape
    step = a
    while step > 1 and step * b * rows * width * value.dtype.itemsize > 1_600_000:
        step //= 2
    count = a // step
    source = pl.BlockSpec(
        (step, None, b, rows, width), lambda n, i, s: (i, jnp.where(n == 0, 1 - s[0], s[0]), 0, 0, 0)
    )
    block = (step, b, rows, width)
    shape = jax.ShapeDtypeStruct((a, b, rows, width), value.dtype)
    return launch(
        line, fold_kernel, (value, got), [source, source], (shape, shape),
        (
            pl.BlockSpec(block, lambda n, i, s: (jnp.where(n == 0, 0, i), 0, 0, 0)),
            pl.BlockSpec(block, lambda n, i, s: (jnp.where(n == 0, i, count - 1), 0, 0, 0)),
        ),
        (2, count), "fold", scalars=(bit,),
    )


def add_kernel(value_ref, got_ref, out_ref):
    total = value_ref[...].astype(jnp.float32) + got_ref[...].astype(jnp.float32)
    out_ref[...] = total.astype(out_ref.dtype)


def add(line, value, got):
    shape = jax.ShapeDtypeStruct(value.shape, value.dtype)
    return launch(
        line, add_kernel, (value, got), [fixed(value), fixed(got)], (shape,), (fixed(shape),),
        (1,), "add",
    )[0]


def rows_fold_kernel(side, down_ref, down_got_ref, mix_ref, mix_got_ref, keep_ref, give_ref):
    del side
    down = down_ref[...].astype(jnp.float32) + down_got_ref[...].astype(jnp.float32)
    mix = mix_ref[...].astype(jnp.float32) + mix_got_ref[...].astype(jnp.float32)
    total = jnp.concatenate([down, mix], axis=1).astype(jnp.bfloat16)

    @pl.when(pl.program_id(0) == 0)
    def _():
        give_ref[...] = total

    @pl.when(pl.program_id(0) == 1)
    def _():
        keep_ref[...] = total


def rows_fold(line, side, down, down_got, mix, mix_got):
    parts, _, rows, width = down.shape
    extra = mix.shape[2]
    step = max(1, parts // 2)

    def source(count):
        return pl.BlockSpec(
            (step, None, count, width), lambda n, i, s: (i, jnp.where(n == 0, 1 - s[0], s[0]), 0, 0)
        )

    shape = bf16(parts, rows + extra, width)
    block = (step, rows + extra, width)
    last = parts // step - 1
    return launch(
        line, rows_fold_kernel, (down, down_got, mix, mix_got),
        [source(rows), source(rows), source(extra), source(extra)], (shape, shape),
        (
            pl.BlockSpec(block, lambda n, i, s: (jnp.where(n == 0, 0, i), 0, 0)),
            pl.BlockSpec(block, lambda n, i, s: (jnp.where(n == 0, i, last), 0, 0)),
        ),
        (2, parts // step), "rows_fold", scalars=(side,),
    )


def stack_kernel(bit, value_ref, got_ref, out_ref):
    del bit

    @pl.when(pl.program_id(0) == 0)
    def _():
        out_ref[...] = value_ref[...]

    @pl.when(pl.program_id(0) == 1)
    def _():
        out_ref[...] = got_ref[...]


def stack(line, bit, value, got, waits=()):
    a, rows, width = value.shape
    return launch(
        line, stack_kernel, (value, got), [fixed(value), fixed(got)],
        (jax.ShapeDtypeStruct((a, 2, rows, width), value.dtype),),
        (
            pl.BlockSpec(
                (a, None, rows, width), lambda n, s: (0, jnp.where(n == 0, s[0], 1 - s[0]), 0, 0)
            ),
        ),
        (2,), "stack", scalars=(bit,), waits=waits,
    )[0]


def split_stack_kernel(parts, bit, value_ref, got_ref, *outs):
    del bit

    def put(source_ref):
        start = 0
        for rows, out_ref in zip(parts, outs):
            out_ref[...] = source_ref[:, start : start + rows, :]
            start += rows

    @pl.when(pl.program_id(0) == 0)
    def _():
        put(value_ref)

    @pl.when(pl.program_id(0) == 1)
    def _():
        put(got_ref)


def split_stack(line, bit, value, got, parts):
    a, _, width = value.shape
    return launch(
        line, partial(split_stack_kernel, parts), (value, got), [fixed(value), fixed(got)],
        [bf16(a, 2, rows, width) for rows in parts],
        [
            pl.BlockSpec(
                (a, None, rows, width), lambda n, s: (0, jnp.where(n == 0, s[0], 1 - s[0]), 0, 0)
            )
            for rows in parts
        ],
        (2,), "split_stack", scalars=(bit,),
    )


def both_sides(line, side, value, got):
    return stack(line, side, value, got)


def arrange_kernel(me, *refs):
    del me
    for n in range(4):

        @pl.when(pl.program_id(0) == n)
        def _():
            refs[4][...] = refs[n][...]


def arrange(line, me, values):
    shape = values[0].shape
    return launch(
        line, arrange_kernel, tuple(values), [fixed(value) for value in values],
        (bf16(4, *shape),),
        (pl.BlockSpec((None,) + shape, lambda n, s: (jnp.bitwise_xor(n, s[0]), 0, 0)),),
        (4,), "arrange", scalars=(me,),
    )[0]


def assemble_forward_kernel(me, *refs):
    down_ref, mix_ref, in_ref = refs[4:]
    half = refs[0].shape[1]
    for n in range(4):
        device = jnp.bitwise_xor(me[0], n)
        side = jnp.right_shift(device, 1)
        column = pl.ds(pl.multiple_of(jnp.bitwise_and(device, 1) * half, 128), half)
        start = 0
        for out_ref in (down_ref, mix_ref):
            rows = out_ref.shape[1]
            out_ref[side, :, column] = refs[n][start : start + rows, :].astype(jnp.float32)
            start += rows
        rows = in_ref.shape[0]
        for h in range(2):
            part = refs[n][start + h * rows : start + h * rows + rows, :].astype(jnp.float32)
            in_ref[:, pl.ds(pl.multiple_of((2 * device + h) * half, 128), half)] = part


def assemble_forward(line, me, values, down_rows, mix_rows, shard_rows):
    half = values[0].shape[1]
    shapes = (f32(2, down_rows, 2 * half), f32(2, mix_rows, 2 * half), f32(shard_rows, 8 * half))
    return launch(
        line, assemble_forward_kernel, tuple(values), [fixed(value) for value in values],
        shapes, [fixed(value) for value in shapes], (1,), "assemble_forward", scalars=(me,),
    )


def assemble_backward_kernel(me, *refs):
    layout_ref, qkv_ref, project_ref = refs[4:]
    half = refs[0].shape[1]
    layout_rows, rows = layout_ref.shape[1], project_ref.shape[0]
    for n in range(4):
        device = jnp.bitwise_xor(me[0], n)
        side = jnp.right_shift(device, 1)
        column = pl.ds(pl.multiple_of(jnp.bitwise_and(device, 1) * half, 128), half)
        for k in range(2):
            start = k * layout_rows
            layout_ref[2 * side + k, :, column] = refs[n][start : start + layout_rows, :].astype(
                jnp.float32
            )
        start = 2 * layout_rows
        qkv_ref[2 * side, :, column] = refs[n][start : start + rows, :].astype(jnp.float32)
        matrix = refs[n][start + rows : start + 2 * rows, :].astype(jnp.float32)

        @pl.when(side == 0)
        def _():
            qkv_ref[1, :, column] = matrix

        @pl.when(side == 1)
        def _():
            project_ref[:, column] = matrix


def assemble_backward(line, me, values, layout_rows, rows):
    half = values[0].shape[1]
    shapes = (f32(4, layout_rows, 2 * half), f32(3, rows, 2 * half), f32(rows, 2 * half))
    return launch(
        line, assemble_backward_kernel, tuple(values), [fixed(value) for value in values],
        shapes, [fixed(value) for value in shapes], (1,), "assemble_backward", scalars=(me,),
    )


def swap(value, axis, bit):
    count = lax.axis_size(axis)
    return lax.ppermute(value, axis, [(i, i ^ bit) for i in range(count)])


def bit_of(axis, bit):
    return jnp.bitwise_and(lax.axis_index(axis), bit) != 0


def bit_index(axis, bit):
    return bit_of(axis, bit).astype(jnp.int32).reshape(1)


class Gather:
    def __init__(self, line, value):
        self.line = line
        self.value = value[None]
        self.bit = lax.axis_size("dp") // 2
        self.got = swap(self.value, "dp", self.bit)

    def step(self, waits=()):
        rows, width = self.value.shape[1:]
        value = stack(self.line, bit_index("dp", self.bit), self.value, self.got, waits)
        self.value = value.reshape(-1, rows, width)
        self.bit //= 2
        self.got = swap(self.value, "dp", self.bit)

    def finish(self, parts):
        while self.bit > 1:
            self.step()
        values = split_stack(self.line, bit_index("dp", 1), self.value, self.got, parts)
        return [value.reshape((-1,) + value.shape[2:]) for value in values]


def padded(value):
    return jnp.pad(value, ((0, -value.shape[0] % 16), (0, 0)))


class Sum:
    def __init__(self, line, bits, value, got):
        self.line, self.bits, self.value, self.got = line, list(bits), value, got
        self.done = False

    def step(self):
        if self.done:
            return
        rows, width = self.value.shape[-2:]
        if not self.bits:
            self.value = add(self.line, self.value.reshape(rows, width), self.got.reshape(rows, width))
            self.done = True
            return
        bit = self.bits.pop()
        shape = (-1, 2, 1, rows, width)
        value, give = fold(
            self.line, bit_index("dp", bit), self.value.reshape(shape), self.got.reshape(shape)
        )
        self.value, self.got = value, swap(give, "dp", bit)

    def finish(self):
        while not self.done:
            self.step()
        return self.value


def shards(
    patches,
    src_kind,
    src_index,
    layout_coords,
    placing,
    segments,
    text_table,
    layout_tables,
    patch_proj,
    rel_table,
    norm_gains,
    w_qkv,
    w_attn_out,
    w_ff_in,
    w_ff_out,
    out_grad,
):
    data_count = lax.axis_size("dp")
    tokens = placing.shape[0]
    capacity = 2 * tokens // data_count
    width = text_table.shape[1]
    half_width = width // 2
    texts = tokens - patches.shape[0]
    shift = tokens.bit_length() - 1
    shard_rows = w_attn_out.shape[0]
    layout_rows = layout_tables.shape[1]
    stream = lax.axis_index("stream")
    core = jnp.bitwise_and(stream, 1)
    side = jnp.right_shift(stream, 1)
    gain_count = norm_gains.shape[1]

    own_core, own_side = core.reshape(1), side.reshape(1)
    dp_bits = [1 << n for n in reversed(range(data_count.bit_length() - 1))]
    line = Line()

    def own_half(value):
        return lax.dynamic_slice_in_dim(value, core * half_width, half_width, axis=-1)

    in_quarter = lax.dynamic_index_in_dim(
        w_ff_in.reshape(shard_rows, 4, -1), stream, 1, keepdims=False
    )
    down_quarter = lax.dynamic_index_in_dim(
        w_ff_out.reshape(4, -1, width), stream, 0, keepdims=False
    )
    layout_part = own_half(
        lax.dynamic_slice_in_dim(layout_tables, side * 2, 2, axis=0)
    ).reshape(-1, half_width)
    mix_part = own_half(
        lax.dynamic_slice_in_dim(w_attn_out, side * (shard_rows // 2), shard_rows // 2, axis=0)
    )
    gain_part = jnp.pad(norm_gains, ((0, 0), (0, half_width - gain_count)))
    table_rows, mix_rows = layout_part.shape[0], mix_part.shape[0]
    square = jnp.concatenate([w_qkv, patch_proj[None]], axis=0)
    square = lax.dynamic_index_in_dim(square, stream, 0, keepdims=False)
    square = lax.all_gather(square, "dp", axis=0, tiled=True)
    square_got = swap(square, "stream", 2)
    mix_part, gain_part = padded(mix_part), padded(gain_part)
    columns = Gather(line, jnp.concatenate([layout_part, mix_part, gain_part], axis=0))
    full_in = lax.all_gather(in_quarter, ("stream", "dp"), axis=0, tiled=True)
    full_in = full_in.reshape(4, width, -1)

    meta, slot_keys, text_index = find_slots(
        line, data_count, capacity, shift, placing, src_kind, src_index, layout_coords, texts
    )
    arrived_meta = lax.all_to_all(
        meta.reshape(16, data_count, capacity), "dp", split_axis=1, concat_axis=1, tiled=True
    ).reshape(16, -1)
    column, across, place = place_meta(line, arrived_meta, tokens)
    column_other = swap(column, "stream", 1)
    across_other = column_other.T
    columns.step()
    columns.step(waits=(column_other,))
    tables, mix, gains = columns.finish((table_rows, mix_part.shape[0], gain_part.shape[0]))
    tables_got = swap(tables, "stream", 2)
    mix_got = swap(mix, "stream", 2)
    gains = gains[:, :2, :gain_count].transpose(1, 0, 2).reshape(2, width)
    text_rows = jnp.take(text_table, text_index[0], axis=0)
    send_rows, down_quarter = pack(line, slot_keys, patches, text_rows, (down_quarter,))
    arrived = lax.all_to_all(
        send_rows.reshape(data_count, capacity, width), "dp", split_axis=0, concat_axis=0, tiled=True
    ).reshape(-1, width)
    full_down = lax.all_gather(down_quarter, ("dp", "stream"), axis=0, tiled=True)
    sums = layout_lookup(line, own_side, column, column_other, tables, layout_rows)
    matrices = arrange(
        line, stream.reshape(1),
        (square, swap(square, "stream", 1), square_got, swap(square_got, "stream", 1)),
    )
    own_sum, other_sum = layout_lookup(
        line, 1 - own_side, column, column_other, tables_got, layout_rows, sums
    )
    got_sum = swap(other_sum, "stream", 1)
    half_index = jnp.broadcast_to(core, (8, 128)).astype(jnp.int32)
    visual, packed, normed_one, projections = embed(
        line, place, column, arrived, own_sum, got_sum, half_index, matrices, gains[:1], tokens
    )
    mix_own = both_sides(line, own_side, mix, mix_got)
    mix_own = mix_own[:, :, :mix_rows].reshape(width, half_width)
    mix_other = swap(mix_own, "stream", 1)
    aug_q, aug_k, table, mirrored = prepare(segments, rel_table)
    mixed, lse = attention_forward(line, projections, aug_q, aug_k, table)
    (
        result, active, grad_hidden, normed_two, turned, upper, grad_branch, grad_mixed,
        gain_two_sum,
    ) = feed_forward(
        line, own_core, packed, mixed, out_grad, mix_own, mix_other, full_in, full_down, gains[1:]
    )

    in_keep, in_give = contract_quarters(
        line, own_core, normed_two, grad_hidden, data_count
    )
    in_got = swap(in_give, "stream", 1)
    down_keep, down_give = contract_halves(line, own_core, active, out_grad)
    down_got = swap(down_give, "stream", 1)
    mix_keep, mix_give = contract_halves(line, own_core, turned, grad_branch)
    mix_got = swap(mix_give, "stream", 1)
    in_shape = (data_count, 2, 2 * shard_rows, half_width)
    in_keep, in_give = fold(
        line, bit_index("dp", 1), in_keep.reshape(in_shape)[:, :, None],
        in_got.reshape(in_shape)[:, :, None],
    )
    in_got = swap(in_give, "dp", 1)
    down_shape = (data_count, 2, down_keep.shape[0] // data_count // 2, half_width)
    mix_shape = (data_count, 2, mix_rows, half_width)
    rows_keep, rows_give = rows_fold(
        line, own_side, down_keep.reshape(down_shape), down_got.reshape(down_shape),
        mix_keep.reshape(mix_shape), mix_got.reshape(mix_shape),
    )
    rows_got = swap(rows_give, "stream", 2)

    qkv_grads, grad_rel = attention_backward(
        line, projections, mixed, grad_mixed, lse, aug_q, aug_k, mirrored
    )
    rows_shape = (data_count // 2, 2, 1) + rows_keep.shape[1:]
    rows_keep, rows_give = fold(
        line, bit_index("dp", 1), rows_keep.reshape(rows_shape), rows_got.reshape(rows_shape)
    )
    rows_got = swap(rows_give, "dp", 1)
    in_shape = (1, 2, data_count // 2, 2 * shard_rows, half_width)
    in_keep, in_give = fold(line, own_side, in_keep.reshape(in_shape), in_got.reshape(in_shape))
    in_got = swap(in_give, "stream", 2)
    grad_packed, own_columns, other_columns, gain_one_sum = input_grad(
        line, own_core, packed, upper, qkv_grads, matrices, gains[:1]
    )
    other_columns = swap(other_columns, "stream", 1)
    rows_shape = (data_count // 4, 2) + rows_keep.shape[-2:]
    in_shape = (data_count // 4, 2) + in_keep.shape[-2:]
    value, give = rows_fold(
        line, bit_index("dp", 2), rows_keep.reshape(rows_shape), rows_got.reshape(rows_shape),
        in_keep.reshape(in_shape), in_got.reshape(in_shape),
    )
    forward_sum = Sum(line, dp_bits[:-2], value, swap(give, "dp", 2))
    rel = rel_gradient(grad_rel, rel_table.shape[0])
    rel_row = jnp.pad(rel.reshape(1, -1), ((0, 0), (0, width - rel.size)))
    small = jnp.concatenate([gain_one_sum[:1], gain_two_sum[:1], rel_row], axis=0)
    returned = return_rows(
        line, place[:1].reshape(-1, 1), grad_packed, jnp.pad(small, ((0, 5), (0, 0))), capacity
    )
    came_back = lax.all_to_all(returned, "dp", split_axis=0, concat_axis=0, tiled=True)

    table_keep, table_give = layout_grad(
        line, own_side, across, across_other, own_columns, other_columns, data_count, layout_rows
    )
    table_got = swap(table_give, "stream", 2)
    square_keep, square_give = square_grads(
        line, own_core, normed_one, qkv_grads, visual, grad_packed, data_count
    )
    square_got = swap(square_give, "stream", 1)
    square_shape = (data_count, 2, 1, 2 * shard_rows, half_width)
    square_keep, square_give = fold(
        line, own_side, square_keep.reshape(square_shape), square_got.reshape(square_shape)
    )
    square_got = swap(square_give, "stream", 2)
    table_shape = (data_count // 2, 2, 1, table_rows, half_width)
    table_keep, table_give = fold(
        line, bit_index("dp", 1), table_keep.reshape(table_shape), table_got.reshape(table_shape)
    )
    table_got = swap(table_give, "dp", 1)

    def stream_group(value):
        across_sides = swap(value, "stream", 2)
        return (value, swap(value, "stream", 1), across_sides, swap(across_sides, "stream", 1))

    wide_meta = meta.astype(jnp.float32)
    slot_kind = wide_meta[:1]
    slot_index = (wide_meta[11:12] * 16.0 + wide_meta[12:13]).astype(jnp.int32)
    slot_text = (wide_meta[13:14] * 4.0 + wide_meta[14:15]).astype(jnp.int32)

    def slot_keys_of(kind, value):
        keys = jnp.where(slot_kind == kind, value, -1).reshape(data_count, capacity)
        return jnp.pad(keys, ((0, 0), (0, 16)), constant_values=-1)

    text_grad_rows = unpack_text(line, slot_keys_of(2.0, slot_text), came_back, text_index)
    rows_side = swap(text_grad_rows, "stream", 2)
    rows_core = swap(text_grad_rows, "stream", 1)
    square_shape = (data_count // 2, 2, 1, 2 * shard_rows, half_width)
    square_keep, square_give = fold(
        line, bit_index("dp", 1), square_keep.reshape(square_shape),
        square_got.reshape(square_shape),
    )
    square_got = swap(square_give, "dp", 1)
    forward_sum.step()
    rows_both = swap(rows_side, "stream", 1)
    table_shape = (data_count // 4, 2, table_rows, half_width)
    square_shape = (data_count // 4, 2, 2 * shard_rows, half_width)
    value, give = rows_fold(
        line, bit_index("dp", 2), table_keep.reshape(table_shape), table_got.reshape(table_shape),
        square_keep.reshape(square_shape), square_got.reshape(square_shape),
    )
    backward_sum = Sum(line, dp_bits[:-2], value, swap(give, "dp", 2))
    text_grad_rows = (text_grad_rows, rows_side, rows_core, rows_both)
    grad_text = text_grads(line, text_grad_rows, text_table.shape[0])
    backward_sum.step()
    forward_sum.finish()
    forward_group = stream_group(forward_sum.value)
    grad_patches = patch_grads(
        line, slot_keys_of(1.0, slot_index), came_back, matrices, patches.shape[0]
    )
    backward_sum.finish()
    small = [join_small(rows[texts + 16 :]) for rows in text_grad_rows]
    small = (small[0] + small[1]) + (small[2] + small[3])

    shard_down, shard_mix, shard_in = assemble_forward(
        line, stream.reshape(1), forward_group, down_shape[2], mix_rows,
        shard_rows,
    )
    shard_layout, shard_qkv, shard_project = assemble_backward(
        line, stream.reshape(1), stream_group(backward_sum.value), layout_rows, shard_rows
    )
    grad_gains = lax.dynamic_slice_in_dim(
        small[:2], lax.axis_index("dp") * gain_count, gain_count, axis=1
    )
    return (
        result,
        grad_patches,
        grad_text,
        shard_layout,
        shard_project,
        small[2, : rel.size].reshape(rel.shape),
        grad_gains,
        shard_qkv,
        shard_mix.reshape(shard_rows, width),
        shard_in,
        shard_down.reshape(-1, width),
    )


def solution(mesh):
    return jax.shard_map(
        shards,
        mesh=mesh,
        in_specs=(
            P(("dp", "stream"), None),
            P(("dp", "stream")),
            P(("dp", "stream")),
            P(None, ("dp", "stream")),
            P(("dp", "stream")),
            P(("dp", "stream"), None),
            P("dp", None),
            P(None, "dp", None),
            P("dp", None),
            P(),
            P(None, "dp"),
            P(None, "dp", None),
            P("dp", None),
            P("dp", None),
            P("dp", None),
            P(("dp", "stream"), None),
        ),
        out_specs=(
            P(("dp", "stream"), None),
            P(("dp", "stream"), None),
            P("dp", None),
            P(None, "dp", None),
            P("dp", None),
            P(),
            P(None, "dp"),
            P(None, "dp", None),
            P("dp", None),
            P("dp", None),
            P("dp", None),
        ),
        check_vma=False,
    )
```
